128 devices in a mesh: rows: 64 (over y, z_lo, x, core), heads: 2 (over z_hi).
Axes of the slice: x: 4, y: 4, z: 4 (z_hi: 2, z_lo: 2; z = z_hi * 2 + z_lo), core: 2. Of those that a mesh axis runs over, the one named last changes fastest.
Arguments:
- tokens: bfloat16 [32768, 768], P('rows'), may hold values from -6 to 6
- cotangent: bfloat16 [32768, 768], P('rows'), may hold values from -6 to 6
- lengths: int32 [64], P('rows'), may hold values from 128 to 512, as said below
- repeats: int32 [64], P('rows'), may hold values from 1 to 4
- query_weight: bfloat16 [2, 768, 768], P(None, None, 'heads'), may hold values from -0.21875 to 0.21875
- query_bias: bfloat16 [2, 768], P(None, 'heads'), may hold values from -1 to 1
- key_weight: bfloat16 [2, 768, 768], P(None, None, 'heads'), may hold values from -0.21875 to 0.21875
- value_weight: bfloat16 [2, 768, 768], P(None, None, 'heads'), may hold values from -0.21875 to 0.21875
- value_bias: bfloat16 [2, 768], P(None, 'heads'), may hold values from -1 to 1
- output_weight: bfloat16 [2, 768, 768], P(None, 'heads'), may hold values from -1.75 to 1.75
- output_bias: bfloat16 [2, 768], replicated, may hold values from -1 to 1
- attn_gain: bfloat16 [2, 768], replicated, may hold values from 0.5 to 1.5
- attn_shift: bfloat16 [2, 768], replicated, may hold values from -1 to 1
- up_weight: bfloat16 [2, 768, 3072], P(None, None, 'heads'), may hold values from -0.21875 to 0.21875
- up_bias: bfloat16 [2, 3072], P(None, 'heads'), may hold values from -1 to 1
- down_weight: bfloat16 [2, 3072, 768], P(None, 'heads'), may hold values from -0.109375 to 0.109375
- down_bias: bfloat16 [2, 768], replicated, may hold values from -1 to 1
- ffn_gain: bfloat16 [2, 768], replicated, may hold values from 0.5 to 1.5
- ffn_shift: bfloat16 [2, 768], replicated, may hold values from -1 to 1
Outputs:
- block_output: bfloat16 [32768, 768], P('rows')
- token_grad: float32 [32768, 768], P('rows')
- grad_query_weight: float32 [2, 768, 768], P(None, None, 'heads')
- grad_query_bias: float32 [2, 768], P(None, 'heads')
- grad_key_weight: float32 [2, 768, 768], P(None, None, 'heads')
- grad_value_weight: float32 [2, 768, 768], P(None, None, 'heads')
- grad_value_bias: float32 [2, 768], P(None, 'heads')
- grad_output_weight: float32 [2, 768, 768], P(None, 'heads')
- grad_output_bias: float32 [2, 768], replicated
- grad_attn_gain: float32 [2, 768], replicated
- grad_attn_shift: float32 [2, 768], replicated
- grad_up_weight: float32 [2, 768, 3072], P(None, None, 'heads')
- grad_up_bias: float32 [2, 3072], P(None, 'heads')
- grad_down_weight: float32 [2, 3072, 768], P(None, 'heads')
- grad_down_bias: float32 [2, 768], replicated
- grad_ffn_gain: float32 [2, 768], replicated
- grad_ffn_shift: float32 [2, 768], replicated
The draws below stay inside these ranges and needn't reach their ends.
Inputs may be any that keep to these rules, and one draw needn't show every extreme that they name: `lengths`: live tokens stand at the start of a row; some row has exactly 512.
All inputs are finite; a program needn't handle non-finite values.
Results may differ from the reference program's by a relative error of at most 0.028.
The reference program's roundings to bfloat16 on the way count: a program that leaves them out, or rounds other values in their place, can miss the bound.
Values sent between devices are 32-bit elements; how exact they have to be, the bound alone decides.
No kernel may reach another device: no remote copies, remote signals or barrier semaphores. Data moves between devices by JAX's collectives and lax.ppermute only.
A program may use at most 192 MiB of HBM per device.

```python
import math
import jax
import jax.numpy as jnp
from jax import lax

D = 768
HEAD_COUNT = 12
HEAD_DIM = 64
FF = 3072
LAYERS = 2
MAXLEN = 512
ROWS = 64
TOKENS = 32768


def draw_lengths(key, part):
    key = jax.random.fold_in(key, 11)
    keys = jax.random.split(key, 4)
    shorter = jax.random.randint(keys[0], (ROWS,), MAXLEN // 4, 3 * MAXLEN // 4 + 1)
    longer = jax.random.randint(keys[1], (ROWS,), 3 * MAXLEN // 4, MAXLEN + 1)
    picked = jax.random.randint(keys[2], (ROWS,), 0, 8) == 0
    chosen = jax.random.randint(keys[3], (), 0, ROWS)
    lengths = jnp.where(picked, longer, shorter)
    lengths = jnp.where(jnp.arange(ROWS) == chosen, MAXLEN, lengths)
    return lengths.astype(jnp.int32)


def set_ends(array, key, low, largest):
    place = [jax.random.randint(jax.random.fold_in(key, axis), (), 0, length) for axis, length in enumerate(array.shape)]
    main_axis = array.shape.index(max(array.shape))
    neighbour = place[:main_axis] + [(place[main_axis] + 1) % array.shape[main_axis]] + place[main_axis + 1:]
    return array.at[tuple(place)].set(low).at[tuple(neighbour)].set(largest)


def shard_levels(key, shape, shards, low, largest):
    level, own = 1.0, jax.random.fold_in(key, 6)
    for axis_at, blocks in shards:
        steps = jnp.exp(jax.random.uniform(jax.random.fold_in(own, axis_at), (blocks,), jnp.float32, low / len(shards), largest / len(shards)))
        level = level * jnp.repeat(steps, shape[axis_at] // blocks).reshape([-1 if axis == axis_at else 1 for axis in range(len(shape))])
    return level


def scatter_about(rng, dims, scale, reach, cuts=(), dtype=jnp.bfloat16):
    entries = jax.random.normal(rng, dims, jnp.float32) * scale
    if len(cuts) > 0:
        entries = shard_levels(rng, dims, cuts, -0.22, 0.18) * entries
    return jnp.clip(entries, min=-reach, max=reach).astype(dtype)


def setup_inputs(seed: int = 0) -> dict:
    key_of = jax.random.split(jax.random.key(seed), 20)
    tokens = scatter_about(key_of[0], (TOKENS, D), 1.0, 6.0, ((0, 64),))
    cotangent = scatter_about(key_of[1], (TOKENS, D), 1.0, 6.0, ((0, 64),))
    lengths = draw_lengths(jax.random.fold_in(key_of[19], 71), 0)
    repeats = set_ends(jax.random.randint(key_of[3], (ROWS,), 1, 5), jax.random.fold_in(key_of[3], 1), 1, 4).astype(jnp.int32)
    query_weight = scatter_about(key_of[4], (LAYERS, D, D), D ** -0.5, 0.21875, ((2, 2),))
    query_bias = scatter_about(key_of[5], (LAYERS, D), 0.2, 1.0, ((1, 2),))
    key_weight = scatter_about(key_of[6], (LAYERS, D, D), D ** -0.5, 0.21875, ((2, 2),))
    value_weight = scatter_about(key_of[7], (LAYERS, D, D), D ** -0.5, 0.21875, ((2, 2),))
    value_bias = scatter_about(key_of[8], (LAYERS, D), 0.2, 1.0, ((1, 2),))
    output_weight = scatter_about(key_of[9], (LAYERS, D, D), (max(2, D // 64)) ** -0.5, 1.75, ((1, 2),))
    output_bias = scatter_about(key_of[10], (LAYERS, D), 0.2, 1.0)
    attn_gain = jnp.clip(1.0 + 0.1 * jax.random.normal(key_of[11], (LAYERS, D), jnp.float32), 0.5, 1.5).astype(jnp.bfloat16)
    attn_shift = scatter_about(key_of[12], (LAYERS, D), 0.2, 1.0)
    up_weight = scatter_about(key_of[13], (LAYERS, D, FF), D ** -0.5, 0.21875, ((2, 2),))
    up_bias = scatter_about(key_of[14], (LAYERS, FF), 0.2, 1.0, ((1, 2),))
    down_weight = scatter_about(key_of[15], (LAYERS, FF, D), FF ** -0.5, 0.109375, ((1, 2),))
    down_bias = scatter_about(key_of[16], (LAYERS, D), 0.2, 1.0)
    ffn_gain = jnp.clip(1.0 + 0.1 * jax.random.normal(key_of[17], (LAYERS, D), jnp.float32), 0.5, 1.5).astype(jnp.bfloat16)
    ffn_shift = scatter_about(key_of[18], (LAYERS, D), 0.2, 1.0)
    return {"tokens": tokens, "cotangent": cotangent, "lengths": lengths, "repeats": repeats, "query_weight": query_weight, "query_bias": query_bias, "key_weight": key_weight, "value_weight": value_weight, "value_bias": value_bias, "output_weight": output_weight, "output_bias": output_bias, "attn_gain": attn_gain, "attn_shift": attn_shift, "up_weight": up_weight, "up_bias": up_bias, "down_weight": down_weight, "down_bias": down_bias, "ffn_gain": ffn_gain, "ffn_shift": ffn_shift}


@jax.custom_vjp
def low(v):
    return lax.optimization_barrier(v.astype(jnp.bfloat16)).astype(jnp.float32)

@jax.custom_vjp
def low_back(v):
    return v

def low_keep(v):
    return (low(v), None)

def low_pass(kept, grad):
    return (grad,)

def back_keep(v):
    return (v, None)

def back_low(kept, grad):
    return (low(grad),)
low.defvjp(low_keep, low_pass)
low_back.defvjp(back_keep, back_low)
norm_eps = 1e-12
exact = lax.Precision.HIGHEST

def product(left, right):
    return jnp.dot(left, right, precision=exact, preferred_element_type=jnp.float32)

def normalize(summed, gain, shift):
    center = summed - lax.optimization_barrier(jnp.mean(summed, axis=-1, keepdims=True))
    inverse = lax.rsqrt(lax.optimization_barrier(jnp.mean(center * center, axis=-1, keepdims=True)) + norm_eps)
    return center * inverse * gain + shift

def attend_row(operands):
    query_row, key_row, value_row, length = operands
    query_heads = query_row.reshape(MAXLEN, HEAD_COUNT, HEAD_DIM)
    key_heads = key_row.reshape(MAXLEN, HEAD_COUNT, HEAD_DIM)
    value_heads = value_row.reshape(MAXLEN, HEAD_COUNT, HEAD_DIM)
    scores = jnp.einsum('qhe,khe->hqk', query_heads, key_heads, precision=exact) * HEAD_DIM ** (-0.5)
    scores = low_back(scores)
    valid = jnp.arange(MAXLEN) < length
    scores = jnp.where(valid[None, None, :], scores, -1e+30)
    probs = low(jax.nn.softmax(scores, axis=-1))
    mixture = jnp.einsum('hqk,khe->qhe', probs, value_heads, precision=exact)
    return low(low_back(mixture.reshape(MAXLEN, D)))

def layer(current, lengths, weights):
    query_weight, query_bias, key_weight, value_weight, value_bias, output_weight, output_bias, attn_gain, attn_shift, up_weight, up_bias, down_weight, down_bias, ffn_gain, ffn_shift = weights
    rows_here = lengths.shape[0]
    rounded = low(current)
    queries = low(low_back(product(rounded, query_weight) + query_bias))
    key_rows = low(low_back(product(rounded, key_weight)))
    value_rows = low(low_back(product(rounded, value_weight) + value_bias))
    mixture = lax.map(jax.checkpoint(attend_row), (queries.reshape(rows_here, MAXLEN, D), key_rows.reshape(rows_here, MAXLEN, D), value_rows.reshape(rows_here, MAXLEN, D), lengths))
    attended = low_back(product(mixture.reshape(rows_here * MAXLEN, D), output_weight) + output_bias)
    hidden = normalize(current + attended, attn_gain, attn_shift)
    pre_active = low_back(product(low(hidden), up_weight) + up_bias)
    active = low(jax.nn.gelu(pre_active, approximate=False))
    ffn_out = low_back(product(active, down_weight) + down_bias)
    return normalize(hidden + ffn_out, ffn_gain, ffn_shift)

def reference(tokens, cotangent, lengths, repeats, query_weight, query_bias, key_weight, value_weight, value_bias, output_weight, output_bias, attn_gain, attn_shift, up_weight, up_bias, down_weight, down_bias, ffn_gain, ffn_shift):
    params = tuple((item.astype(jnp.float32) for item in (query_weight, query_bias, key_weight, value_weight, value_bias, output_weight, output_bias, attn_gain, attn_shift, up_weight, up_bias, down_weight, down_bias, ffn_gain, ffn_shift)))
    group = math.gcd(ROWS, max(1, 4096 // MAXLEN))
    blocks = ROWS // group
    inputs = tokens.astype(jnp.float32).reshape(blocks, group * MAXLEN, D)
    positions = jnp.arange(MAXLEN)
    weighting = jnp.where(positions[None, :] < lengths[:, None], repeats[:, None], 0).astype(jnp.float32)
    seeds = (cotangent.astype(jnp.float32).reshape(ROWS, MAXLEN, D) * weighting[:, :, None]).reshape(blocks, group * MAXLEN, D)
    grouped_lengths = lengths.reshape(blocks, group)

    def visit(totals, operands):
        block_input, block_lengths, block_seed = operands

        def forward(current, weights):
            for layer_index in range(LAYERS):
                current = layer(current, block_lengths, tuple((item[layer_index] for item in weights)))
            return current
        result, pullback = jax.vjp(forward, block_input, params)
        grad_input, grad_params = pullback(block_seed)
        totals = jax.tree.map(jnp.add, totals, grad_params)
        return (totals, (result, grad_input))
    zeros = tuple((jnp.zeros_like(item) for item in params))
    totals, (results, gradients) = lax.scan(visit, zeros, (inputs, grouped_lengths, seeds))
    grad_query_weight, grad_query_bias, grad_key_weight, grad_value_weight, grad_value_bias, grad_output_weight, grad_output_bias, grad_attn_gain, grad_attn_shift, grad_up_weight, grad_up_bias, grad_down_weight, grad_down_bias, grad_ffn_gain, grad_ffn_shift = totals
    return (results.reshape(TOKENS, D).astype(jnp.bfloat16), gradients.reshape(TOKENS, D), grad_query_weight, grad_query_bias, grad_key_weight, grad_value_weight, grad_value_bias, grad_output_weight, grad_output_bias, grad_attn_gain, grad_attn_shift, grad_up_weight, grad_up_bias, grad_down_weight, grad_down_bias, grad_ffn_gain, grad_ffn_shift)
```

```python
import jax
import jax.numpy as jnp
from jax import lax
from jax.experimental import pallas as pl
from jax.experimental.pallas import tpu as pltpu
from jax.sharding import Mesh, PartitionSpec as P

HEAD_DIM = 64
EPS = 1e-12
F32 = jnp.float32
BF16 = jnp.bfloat16
SWAP = ((0, 1), (1, 0))
EDGE0 = ((0, 1), (1, 0), (2, 3), (3, 2))
EDGE1 = ((1, 2), (2, 1), (3, 0), (0, 3))
LINKS = (("x", EDGE0), ("x", EDGE1), ("y", EDGE0), ("y", EDGE1))
PLANE = ("y", "x")


def normalize(summed, gain, shift):
    center = summed - jnp.mean(summed, axis=-1, keepdims=True)
    inverse = lax.rsqrt(jnp.mean(center * center, axis=-1, keepdims=True) + EPS)
    scaled = center * inverse
    return (scaled * gain + shift, scaled, inverse)


def normalize_back(gradient, gain, scaled, inverse):
    gained = gradient * gain
    return inverse * (
        gained
        - jnp.mean(gained, axis=-1, keepdims=True)
        - scaled * jnp.mean(gained * scaled, axis=-1, keepdims=True)
    )


def normal_cdf(values):
    return 0.5 * (1.0 + lax.erf(values * (0.5**0.5)))


def gelu(values):
    return values * normal_cdf(values)


def gelu_slope(values):
    density = jnp.exp(-0.5 * values * values) * 0.3989422804014327
    return normal_cdf(values) + values * density


def dot(left, right):
    return jnp.dot(left, right, preferred_element_type=F32)


def dot_t(left, right):
    return jnp.einsum("sd,fd->sf", left, right, preferred_element_type=F32)


def t_dot(left, right):
    return jnp.einsum("sf,sd->fd", left, right, preferred_element_type=F32)


def split_heads(block):
    return block.reshape(block.shape[0], block.shape[1] // HEAD_DIM, HEAD_DIM)


def masked_scores(queries, keys, length):
    scores = jnp.einsum("qhe,khe->hqk", queries, keys, preferred_element_type=F32) * HEAD_DIM**-0.5
    valid = jnp.arange(keys.shape[0]) < length
    return jnp.where(valid[None, None, :], scores, -1e30)


def attend(queries, keys, values, length):
    scores = masked_scores(split_heads(queries), split_heads(keys), length)
    highest = jnp.max(scores, axis=-1, keepdims=True)
    raised = jnp.exp(scores - highest)
    totals = jnp.sum(raised, axis=-1, keepdims=True)
    probs = (raised / totals).astype(BF16)
    mixture = jnp.einsum("hqk,khe->qhe", probs, split_heads(values), preferred_element_type=F32)
    logsum = highest + jnp.log(totals)
    return mixture.reshape(queries.shape).astype(BF16), logsum


def attend_back(queries, keys, values, grads, length, logsum):
    query_heads, key_heads = split_heads(queries), split_heads(keys)
    grad_heads = split_heads(grads)
    scores = masked_scores(query_heads, key_heads, length)
    probs = jnp.exp(scores - logsum)
    grad_probs = jnp.einsum("qhe,khe->hqk", grad_heads, split_heads(values), preferred_element_type=F32)
    inner = jnp.sum(probs * grad_probs, axis=-1, keepdims=True)
    grad_scores = (probs * (grad_probs - inner)).astype(BF16)
    scale = HEAD_DIM**-0.5
    grad_query = jnp.einsum("hqk,khe->qhe", grad_scores, key_heads, preferred_element_type=F32) * scale
    grad_key = jnp.einsum("hqk,qhe->khe", grad_scores, query_heads, preferred_element_type=F32) * scale
    grad_value = jnp.einsum("hqk,qhe->khe", probs.astype(BF16), grad_heads, preferred_element_type=F32)
    shape = queries.shape
    return tuple(item.reshape(shape).astype(BF16) for item in (grad_query, grad_key, grad_value))


def column_sum(values):
    return jnp.sum(values.astype(F32), axis=0)


def swap(values, axis):
    return lax.ppermute(values, axis, SWAP)


def pair_sum(values):
    return values + swap(values, "h")


def piece(values, index, size):
    return lax.dynamic_slice_in_dim(values, index * size, size, 0)


def in_order(side, mine, other):
    return jnp.concatenate([jnp.where(side == 0, mine, other), jnp.where(side == 0, other, mine)])


def after(values, *earlier):
    return lax.optimization_barrier((values, *earlier))[0]


def sort_kernel(piece_ref, down_ref, up_ref):
    chips, _, _, rows, width = piece_ref.shape
    for i in range(chips):
        down_ref[0, i * rows : (i + 1) * rows, :] = piece_ref[i, 0, 0].astype(BF16)
        up = piece_ref[i, 1, 0].astype(BF16)
        half = rows // 2
        up_ref[0, i * half : (i + 1) * half, :width] = up[:half]
        up_ref[0, i * half : (i + 1) * half, width:] = up[half:]


def sort_weights(gathered):
    chips, _, layers, rows, width = gathered.shape
    step = 4
    units = chips * rows
    return pl.pallas_call(
        sort_kernel,
        grid=(layers, chips // step),
        in_specs=[pl.BlockSpec((step, 2, 1, rows, width), lambda l, i: (i, 0, l, 0, 0))],
        out_specs=[
            pl.BlockSpec((1, step * rows, width), lambda l, i: (l, i, 0)),
            pl.BlockSpec((1, step * rows // 2, units), lambda l, i: (l, i, 0)),
        ],
        out_shape=[
            jax.ShapeDtypeStruct((layers, units, width), BF16),
            jax.ShapeDtypeStruct((layers, width, units), BF16),
        ],
        compiler_params=pltpu.CompilerParams(vmem_limit_bytes=40 * 2**20),
        cost_estimate=pl.CostEstimate(flops=0, bytes_accessed=6 * layers * 2 * units * width, transcendentals=0),
        name="sort_weights",
    )(gathered)


def rows_of(ref):
    chips, _, rows, columns = ref.shape
    return ref[...].reshape(chips * rows, columns)


def place_feed_kernel(down_in, up_in, down_ref, up_ref):
    down_ref[0] = rows_of(down_in)
    up_ref[0] = rows_of(up_in).T


def place_attention_kernel(query_in, key_in, value_in, output_in, query_ref, key_ref, value_ref, output_ref):
    query_ref[0] = rows_of(query_in).T
    key_ref[0] = rows_of(key_in).T
    value_ref[0] = rows_of(value_in).T
    output_ref[0] = rows_of(output_in)


def place_gradients(gathered, width):
    chips, _, rows, _ = gathered.shape
    step = 4
    units, block = chips * rows, step * rows
    half = width // 2

    def feed_in(core):
        return pl.BlockSpec((step, 1, rows, width), lambda l, i: (i, core, 0, 1 - l))

    def attention_in(core, which):
        return pl.BlockSpec((step, 1, rows, half), lambda l, i: (2 * i + which, core, 0, 5 - l))

    limit = pltpu.CompilerParams(vmem_limit_bytes=40 * 2**20)
    down, up = pl.pallas_call(
        place_feed_kernel,
        grid=(2, chips // step),
        in_specs=[feed_in(0), feed_in(1)],
        out_specs=[
            pl.BlockSpec((1, block, width), lambda l, i: (l, i, 0)),
            pl.BlockSpec((1, width, block), lambda l, i: (l, 0, i)),
        ],
        out_shape=[
            jax.ShapeDtypeStruct((2, units, width), F32),
            jax.ShapeDtypeStruct((2, width, units), F32),
        ],
        compiler_params=limit,
        name="place_feed",
    )(gathered, gathered)
    tall = pl.BlockSpec((1, half, block), lambda l, i: (l, i, 0))
    tall_shape = jax.ShapeDtypeStruct((2, width, block), F32)
    query, key, value, output = pl.pallas_call(
        place_attention_kernel,
        grid=(2, 2),
        in_specs=[attention_in(0, 0), attention_in(0, 1), attention_in(1, 0), attention_in(1, 1)],
        out_specs=[tall, tall, tall, pl.BlockSpec((1, block, half), lambda l, i: (l, 0, i))],
        out_shape=[tall_shape, tall_shape, tall_shape, jax.ShapeDtypeStruct((2, block, width), F32)],
        compiler_params=limit,
        name="place_attention",
    )(gathered, gathered, gathered, gathered)
    return query, key, value, output, up, down


def local(
    tokens,
    cotangent,
    lengths,
    repeats,
    query_weight,
    query_bias,
    key_weight,
    value_weight,
    value_bias,
    output_weight,
    output_bias,
    attn_gain,
    attn_shift,
    up_weight,
    up_bias,
    down_weight,
    down_bias,
    ffn_gain,
    ffn_shift,
):
    length = lengths[0]
    side = lax.axis_index("h")
    core = lax.axis_index("c")
    chip = lax.axis_index("y") * 4 + lax.axis_index("x")
    first_core = core == 0
    slots, width = tokens.shape
    half_slots = slots // 2
    units = up_weight.shape[2]
    columns = query_weight.shape[2]

    rows_down, rows_up = units // 16, width // 16
    pieces = []
    for layer in (0, 1):
        up_piece = piece(up_weight[layer], chip, rows_up)
        up_piece = jnp.concatenate([up_piece[:, :width], up_piece[:, width:]])
        pieces.append(jnp.where(first_core, piece(down_weight[layer], chip, rows_down), up_piece).astype(F32))
    gathered = lax.all_gather(swap(jnp.concatenate(pieces), "h"), PLANE + ("c",))
    peer_down, peer_up = sort_weights(gathered.reshape(16, 2, 2, rows_down, width))
    peer_up_bias = swap(up_bias.astype(F32), "h")

    def own_slots(values):
        return piece(values, side, half_slots)

    def attention_in(layer, rounded):
        queries = (dot(rounded, query_weight[layer]) + query_bias[layer]).astype(BF16)
        keys = dot(rounded, key_weight[layer]).astype(BF16)
        values = (dot(rounded, value_weight[layer]) + value_bias[layer]).astype(BF16)
        mixture, logsum = attend(queries, keys, values, length)
        return queries, keys, values, mixture, logsum

    def attention_back(layer, saved, rounded, grad_one_own):
        queries, keys, values, mixture, logsum = saved
        grad_one = 2.0 * in_order(side, *(lambda sent: (sent, swap(sent, "h")))(0.5 * grad_one_own))
        attended_low = grad_one.astype(BF16)
        grad_mixture = dot_t(attended_low, output_weight[layer]).astype(BF16)
        query_low, key_low, value_low = attend_back(queries, keys, values, grad_mixture, length, logsum)
        lows = (query_low, key_low, value_low)

        def into_input(pick):
            return (
                dot_t(pick(query_low), query_weight[layer])
                + dot_t(pick(key_low), key_weight[layer])
                + dot_t(pick(value_low), value_weight[layer])
            )

        small = [jnp.concatenate([column_sum(query_low), column_sum(value_low)]), column_sum(attended_low)]
        return grad_one, lows, attended_low, into_input, small

    def attention_weights_back(saved, rounded, lows, attended_low):
        mixture = saved[3]
        query_low, key_low, value_low = lows
        sent = jnp.concatenate(
            [
                t_dot(jnp.where(first_core, value_low, query_low), rounded),
                t_dot(jnp.where(first_core, mixture, key_low), jnp.where(first_core, attended_low, rounded)),
            ]
        )
        received = swap(sent, "c")
        kept = jnp.concatenate(
            [
                t_dot(jnp.where(first_core, query_low, value_low), rounded),
                t_dot(jnp.where(first_core, key_low, mixture), jnp.where(first_core, rounded, attended_low)),
            ]
        )
        total = kept + received
        return jnp.concatenate([total[:, : width // 2], total[:, width // 2 :]])

    def feed_back(layer, gradient, saved):
        scaled_two, inverse_two, pres, actives, hidden_low, scaled_one, inverse_one = saved
        grad_two = normalize_back(gradient, ffn_gain[layer], scaled_two, inverse_two)
        ffn_low = grad_two.astype(BF16)
        downs, ups = (down_weight[layer], peer_down[layer]), (up_weight[layer], peer_up[layer])
        pre_lows = [
            (dot_t(ffn_low, down) * gelu_slope(pre)).astype(BF16) for down, pre in zip(downs, pres, strict=True)
        ]
        grad_hidden = grad_two + dot_t(pre_lows[0], ups[0]) + dot_t(pre_lows[1], ups[1])
        grad_one = normalize_back(grad_hidden, attn_gain[layer], scaled_one, inverse_one)
        shared = [
            jnp.sum(grad_hidden * scaled_one, axis=0),
            jnp.sum(grad_hidden, axis=0),
            column_sum(ffn_low),
            jnp.sum(gradient * scaled_two, axis=0),
            jnp.sum(gradient, axis=0),
        ]
        biases = [column_sum(item).reshape(-1, width) for item in pre_lows]
        return grad_one, ffn_low, pre_lows, shared, biases

    def feed_weights_back(saved, ffn_low, pre_lows):
        actives, hidden_low = saved[3], saved[4]
        right = jnp.where(first_core, hidden_low, ffn_low)
        sent = jnp.concatenate(
            [t_dot(jnp.where(first_core, pre, act), right) for pre, act in zip(pre_lows, actives)], axis=1
        )
        received = swap(sent, "c")
        right = jnp.where(first_core, ffn_low, hidden_low)
        kept = jnp.concatenate(
            [t_dot(jnp.where(first_core, act, pre), right) for pre, act in zip(pre_lows, actives)], axis=1
        )
        return kept + received

    x1 = tokens.astype(F32)
    att1 = attention_in(0, tokens)
    attended = pair_sum(dot(att1[3], output_weight[0])) + output_bias[0]
    hidden, scaled, inverse = normalize(x1 + attended, attn_gain[0], attn_shift[0])
    hidden_low = hidden.astype(BF16)
    pre = dot(hidden_low, up_weight[0]) + up_bias[0]
    active = gelu(pre).astype(BF16)
    ffn_out = pair_sum(dot(active, down_weight[0])) + down_bias[0]
    x2, scaled_two, inverse_two = normalize(hidden + ffn_out, ffn_gain[0], ffn_shift[0])
    hidden_own = own_slots(hidden_low)
    pre_peer = dot(hidden_own, peer_up[0]) + peer_up_bias[0]
    saved1 = (
        own_slots(scaled_two),
        own_slots(inverse_two),
        (own_slots(pre), pre_peer),
        (own_slots(active), gelu(pre_peer).astype(BF16)),
        hidden_own,
        own_slots(scaled),
        own_slots(inverse),
    )

    x2_low = x2.astype(BF16)
    att2 = attention_in(1, x2_low)
    mixture = att2[3]
    received = swap(dot(piece(mixture, 1 - side, half_slots), output_weight[1]), "h")
    attended = dot(own_slots(mixture), output_weight[1]) + received + output_bias[1]
    hidden, scaled, inverse = normalize(own_slots(x2) + attended, attn_gain[1], attn_shift[1])
    hidden_low = hidden.astype(BF16)
    pre = dot(hidden_low, up_weight[1]) + up_bias[1]
    pre_peer = dot(hidden_low, peer_up[1]) + peer_up_bias[1]
    active, active_peer = gelu(pre).astype(BF16), gelu(pre_peer).astype(BF16)
    ffn_out = dot(active, down_weight[1]) + dot(active_peer, peer_down[1]) + down_bias[1]
    _, scaled_last, inverse_last = normalize(hidden + ffn_out, ffn_gain[1], ffn_shift[1])
    saved2 = (scaled_last, inverse_last, (pre, pre_peer), (active, active_peer), hidden_low, scaled, inverse)

    places = side * half_slots + jnp.arange(half_slots)
    weighting = jnp.where(places < length, repeats[0], 0).astype(F32)[:, None]
    gradient2 = own_slots(cotangent).astype(F32) * weighting
    grad_one_own, ffn_low, pre_lows, shared2, biases2 = feed_back(1, gradient2, saved2)
    grad_one2, lows2, attended_low2, into_input, small_att2 = attention_back(1, att2, x2_low, grad_one_own)
    sent = swap(into_input(lambda item: piece(item, 1 - side, half_slots)), "h")
    feed2 = feed_weights_back(saved2, ffn_low, pre_lows)
    gradient1 = grad_one_own + into_input(own_slots) + sent
    gradient1, feed2 = lax.optimization_barrier((gradient1, feed2))
    feed2 = lax.psum_scatter(feed2, PLANE, tiled=True)

    grad_one_own1, ffn_low, pre_lows, shared1, biases1 = feed_back(0, gradient1, saved1)
    grad_one1, lows1, attended_low1, into_input, small_att1 = attention_back(0, att1, tokens, grad_one_own1)
    feed1 = feed_weights_back(saved1, ffn_low, pre_lows)
    attn2 = attention_weights_back(att2, x2_low, lows2, attended_low2)
    attn1 = attention_weights_back(att1, tokens, lows1, attended_low1)
    rest = lax.psum_scatter(jnp.concatenate([feed1, attn2, attn1], axis=1), PLANE, tiled=True)

    feed2, rest = lax.optimization_barrier((feed2, rest))
    own = jnp.concatenate([feed2[:, :width], rest[:, :width], rest[:, 2 * width :]], axis=1)
    peer = jnp.concatenate([feed2[:, width:], rest[:, width : 2 * width]], axis=1)
    across = lax.ppermute(peer, ("zl", "h"), ((0, 3), (3, 0), (1, 2), (2, 1)))
    peer = swap(peer, "h") + across
    own = own + swap(own, "zl")
    own = jnp.concatenate([own[:, : 2 * width] + peer, own[:, 2 * width :]], axis=1)
    gathered = lax.all_gather(own, PLANE + ("c",)).reshape(16, 2, *own.shape)
    grad_query, grad_key, grad_value, grad_output, grad_up, grad_down = place_gradients(gathered, width)

    token_grad = grad_one1 + pair_sum(into_input(lambda item: item))
    scaled_last = after(scaled_last, token_grad)
    scaled_all = in_order(side, scaled_last, swap(scaled_last, "h"))
    block_output = (scaled_all * ffn_gain[1] + ffn_shift[1]).astype(BF16)
    shared = jnp.stack(shared1 + shared2)
    mine = jnp.concatenate([shared, biases1[0], biases2[0]])
    mine = mine + swap(jnp.concatenate([shared, biases1[1], biases2[1]]), "h")
    small = jnp.concatenate([mine, jnp.stack(small_att1 + small_att2)])
    small = after(small, block_output)
    small = small + swap(small, "c")
    for axis, pairs in LINKS:
        small = small + lax.ppermute(small, axis, pairs)
    small = small + swap(small, "zl")
    bias_rows = units // width
    shared = small[:10].reshape(2, 5, width)
    grad_up_bias = small[10 : 10 + 2 * bias_rows].reshape(2, units)
    attention = small[10 + 2 * bias_rows :].reshape(2, 2, width)

    return (
        block_output,
        token_grad,
        grad_query,
        attention[:, 0, :columns],
        grad_key,
        grad_value,
        attention[:, 0, columns:],
        grad_output,
        attention[:, 1],
        shared[:, 0],
        shared[:, 1],
        grad_up,
        grad_up_bias,
        grad_down,
        shared[:, 2],
        shared[:, 3],
        shared[:, 4],
    )


def solution(mesh):
    fine = Mesh(mesh.devices.reshape(4, 2, 4, 2, 2), ("y", "zl", "x", "c", "h"))
    rows = ("y", "zl", "x", "c")
    in_specs = (
        P(rows, None),
        P(rows, None),
        P(rows),
        P(rows),
        P(None, None, "h"),
        P(None, "h"),
        P(None, None, "h"),
        P(None, None, "h"),
        P(None, "h"),
        P(None, "h", None),
        P(),
        P(),
        P(),
        P(None, None, "h"),
        P(None, "h"),
        P(None, "h", None),
        P(),
        P(),
        P(),
    )
    out_specs = (
        P(rows, None),
        P(rows, None),
        P(None, None, "h"),
        P(None, "h"),
        P(None, None, "h"),
        P(None, None, "h"),
        P(None, "h"),
        P(None, "h", None),
        P(),
        P(),
        P(),
        P(None, None, "h"),
        P(None, "h"),
        P(None, "h", None),
        P(),
        P(),
        P(),
    )
    return jax.shard_map(local, mesh=fine, in_specs=in_specs, out_specs=out_specs, check_vma=False)
```

```python
import jax
import jax.numpy as jnp
from jax import lax
from jax.experimental import pallas as pl
from jax.experimental.pallas import tpu as pltpu
from jax.sharding import Mesh, PartitionSpec as P

HEAD_DIM = 64
EPS = 1e-12
F32 = jnp.float32
BF16 = jnp.bfloat16
SWAP = ((0, 1), (1, 0))
EDGE0 = ((0, 1), (1, 0), (2, 3), (3, 2))
EDGE1 = ((1, 2), (2, 1), (3, 0), (0, 3))
LINKS = (("x", EDGE0), ("x", EDGE1), ("y", EDGE0), ("y", EDGE1))
PLANE = ("y", "x")


def normalize(summed, gain, shift):
    center = summed - jnp.mean(summed, axis=-1, keepdims=True)
    inverse = lax.rsqrt(jnp.mean(center * center, axis=-1, keepdims=True) + EPS)
    scaled = center * inverse
    return (scaled * gain + shift, scaled, inverse)


def normalize_back(gradient, gain, scaled, inverse):
    gained = gradient * gain
    return inverse * (
        gained
        - jnp.mean(gained, axis=-1, keepdims=True)
        - scaled * jnp.mean(gained * scaled, axis=-1, keepdims=True)
    )


def normal_cdf(values):
    return 0.5 * (1.0 + lax.erf(values * (0.5**0.5)))


def gelu(values):
    return values * normal_cdf(values)


def gelu_slope(values):
    density = jnp.exp(-0.5 * values * values) * 0.3989422804014327
    return normal_cdf(values) + values * density


def dot(left, right):
    return jnp.dot(left, right, preferred_element_type=F32)


def dot_t(left, right):
    return jnp.einsum("sd,fd->sf", left, right, preferred_element_type=F32)


def t_dot(left, right):
    return jnp.einsum("sf,sd->fd", left, right, preferred_element_type=F32)


def column_sum(values):
    return jnp.sum(values.astype(F32), axis=0)


def swap(values, axis):
    return lax.ppermute(values, axis, SWAP)


def pair_sum(values):
    return values + swap(values, "h")


def piece(values, index, size):
    return lax.dynamic_slice_in_dim(values, index * size, size, 0)


def in_order(side, mine, other):
    return jnp.concatenate([jnp.where(side == 0, mine, other), jnp.where(side == 0, other, mine)])


def together(*values):
    return lax.optimization_barrier(values)


def t_dot_in_kernel(left, right):
    return lax.dot_general(left, right, (((0,), (0,)), ((), ())), preferred_element_type=F32)


LIMIT = pltpu.CompilerParams(vmem_limit_bytes=48 * 2**20)
SCALAR = pl.BlockSpec(memory_space=pltpu.SMEM)


def across_lanes(left, right):
    return lax.dot_general(left, right, (((1,), (1,)), ((), ())), preferred_element_type=F32)


def attend_kernel(
    length_ref,
    slot_ref,
    query_weight,
    query_bias,
    key_weight,
    value_weight,
    value_bias,
    output_weight,
    query_ref,
    key_ref,
    value_ref,
    mixture_ref,
    logsum_ref,
    share_ref,
):
    slots = slot_ref[...]
    query_ref[...] = (dot(slots, query_weight[0]) + query_bias[...]).astype(BF16)
    key_ref[...] = dot(slots, key_weight[0]).astype(BF16)
    value_ref[...] = (dot(slots, value_weight[0]) + value_bias[...]).astype(BF16)
    count = slots.shape[0]
    valid = lax.broadcasted_iota(jnp.int32, (count, count), 0) < length_ref[0]
    for head in range(2):
        cut = slice(head * HEAD_DIM, (head + 1) * HEAD_DIM)
        scores = across_lanes(key_ref[:, cut], query_ref[:, cut]) * HEAD_DIM**-0.5
        scores = jnp.where(valid, scores, -1e30)
        highest = jnp.max(scores, axis=0, keepdims=True)
        raised = jnp.exp(scores - highest)
        totals = jnp.sum(raised, axis=0, keepdims=True)
        probs = (raised * (1.0 / totals)).astype(BF16)
        mixture_ref[:, cut] = t_dot_in_kernel(probs, value_ref[:, cut]).astype(BF16)
        logsum_ref[0, head : head + 1, :] = highest + jnp.log(totals)
    share = dot(mixture_ref[...], output_weight[0])

    @pl.when(pl.program_id(0) == 0)
    def _():
        share_ref[...] = share

    @pl.when(pl.program_id(0) != 0)
    def _():
        share_ref[...] += share


def attend(layer, length, slots, query_weight, query_bias, key_weight, value_weight, value_bias, output_weight):
    count, width = slots.shape
    heads = query_weight.shape[2]
    pair = 2 * HEAD_DIM
    steps = heads // pair
    whole = pl.BlockSpec((count, width), lambda i: (0, 0))
    weight = pl.BlockSpec((1, width, pair), lambda i: (layer, 0, i))
    bias = pl.BlockSpec((1, pair), lambda i: (0, i))
    part = pl.BlockSpec((count, pair), lambda i: (0, i))
    part_shape = jax.ShapeDtypeStruct((count, heads), BF16)
    return pl.pallas_call(
        attend_kernel,
        grid=(steps,),
        in_specs=[SCALAR, whole, weight, bias, weight, weight, bias]
        + [pl.BlockSpec((1, pair, width), lambda i: (layer, i, 0))],
        out_specs=[part] * 4 + [pl.BlockSpec((1, 2, count), lambda i: (i, 0, 0)), whole],
        out_shape=[part_shape] * 4
        + [jax.ShapeDtypeStruct((steps, 2, count), F32), jax.ShapeDtypeStruct((count, width), F32)],
        compiler_params=LIMIT,
        cost_estimate=pl.CostEstimate(
            flops=8 * count * width * heads + 4 * count * count * heads,
            bytes_accessed=8 * width * heads + 8 * count * width,
            transcendentals=count * count * heads // HEAD_DIM,
        ),
        name="attend",
    )(length.reshape(1), slots, query_weight, query_bias, key_weight, value_weight, value_bias, output_weight)


def attend_back_kernel(
    length_ref,
    query_ref,
    key_ref,
    value_ref,
    logsum_ref,
    grad_ref,
    query_weight,
    key_weight,
    value_weight,
    output_weight,
    query_low,
    key_low,
    value_low,
    share_ref,
    query_sum,
    value_sum,
):
    grads = across_lanes(grad_ref[...], output_weight[0]).astype(BF16)
    count = grads.shape[0]
    valid = lax.broadcasted_iota(jnp.int32, (count, count), 0) < length_ref[0]
    scale = HEAD_DIM**-0.5
    for head in range(2):
        cut = slice(head * HEAD_DIM, (head + 1) * HEAD_DIM)
        queries, keys, grad = query_ref[:, cut], key_ref[:, cut], grads[:, cut]
        scores = jnp.where(valid, across_lanes(keys, queries) * scale, -1e30)
        probs = jnp.exp(scores - logsum_ref[0, head : head + 1, :])
        grad_probs = across_lanes(value_ref[:, cut], grad)
        inner = jnp.sum(probs * grad_probs, axis=0, keepdims=True)
        grad_scores = (probs * (grad_probs - inner)).astype(BF16)
        query_low[:, cut] = (t_dot_in_kernel(grad_scores, keys) * scale).astype(BF16)
        key_low[:, cut] = (dot(grad_scores, queries) * scale).astype(BF16)
        value_low[:, cut] = dot(probs.astype(BF16), grad).astype(BF16)
    query_sum[...] = jnp.sum(query_low[...].astype(F32), axis=0, keepdims=True)
    value_sum[...] = jnp.sum(value_low[...].astype(F32), axis=0, keepdims=True)
    share = across_lanes(query_low[...], query_weight[0])
    share += across_lanes(key_low[...], key_weight[0])
    share += across_lanes(value_low[...], value_weight[0])

    @pl.when(pl.program_id(0) == 0)
    def _():
        share_ref[...] = share

    @pl.when(pl.program_id(0) != 0)
    def _():
        share_ref[...] += share


def attend_back(layer, length, saved, attended_low, query_weight, key_weight, value_weight, output_weight):
    queries, keys, values, _, logsum = saved
    count, width = attended_low.shape
    heads = queries.shape[1]
    pair = 2 * HEAD_DIM
    steps = heads // pair
    whole = pl.BlockSpec((count, width), lambda i: (0, 0))
    weight = pl.BlockSpec((1, width, pair), lambda i: (layer, 0, i))
    part = pl.BlockSpec((count, pair), lambda i: (0, i))
    part_shape = jax.ShapeDtypeStruct((count, heads), BF16)
    sums = pl.BlockSpec((1, pair), lambda i: (0, i))
    sums_shape = jax.ShapeDtypeStruct((1, heads), F32)
    return pl.pallas_call(
        attend_back_kernel,
        grid=(steps,),
        in_specs=[SCALAR, part, part, part, pl.BlockSpec((1, 2, count), lambda i: (i, 0, 0)), whole]
        + [weight] * 3
        + [pl.BlockSpec((1, pair, width), lambda i: (layer, i, 0))],
        out_specs=[part] * 3 + [whole, sums, sums],
        out_shape=[part_shape] * 3 + [jax.ShapeDtypeStruct((count, width), F32), sums_shape, sums_shape],
        compiler_params=LIMIT,
        cost_estimate=pl.CostEstimate(
            flops=8 * count * width * heads + 10 * count * count * heads,
            bytes_accessed=8 * width * heads + 8 * count * width,
            transcendentals=count * count * heads // HEAD_DIM,
        ),
        name="attend_back",
    )(length.reshape(1), queries, keys, values, logsum, attended_low, query_weight, key_weight, value_weight, output_weight)


def pieces_kernel(place_ref, down_in, up_in, piece_ref):
    width = piece_ref.shape[2]

    @pl.when(place_ref[1] == 0)
    def _():
        piece_ref[0] = down_in[0].astype(F32)

    @pl.when(place_ref[1] != 0)
    def _():
        half = up_in.shape[1]
        piece_ref[0, :half, :] = up_in[0, :, :width].astype(F32)
        piece_ref[0, half:, :] = up_in[0, :, width:].astype(F32)


def weight_pieces(chip, core, down_weight, up_weight):
    layers, units, width = down_weight.shape
    rows = units // 16
    return pl.pallas_call(
        pieces_kernel,
        grid_spec=pltpu.PrefetchScalarGridSpec(
            num_scalar_prefetch=1,
            grid=(layers,),
            in_specs=[
                pl.BlockSpec((1, rows, width), lambda l, place: (l, place[0], 0)),
                pl.BlockSpec((1, rows // 2, units), lambda l, place: (l, place[0], 0)),
            ],
            out_specs=pl.BlockSpec((1, rows, width), lambda l, place: (l, 0, 0)),
        ),
        out_shape=jax.ShapeDtypeStruct((layers, rows, width), F32),
        compiler_params=LIMIT,
        name="weight_pieces",
    )(jnp.stack([chip, core]), down_weight, up_weight)


def feed_sums_kernel(received, part_ref, act_own, act_peer, pre_own, pre_peer, ffn_low, hidden_low, *refs):
    out_ref = refs[-1]
    width = ffn_low.shape[1]

    def write(own, peer, right):
        for k, left in enumerate((own, peer)):
            total = t_dot_in_kernel(left[...], right[...])
            cut = slice(k * width, (k + 1) * width)
            out_ref[:, cut] = total + refs[0][:, cut] if received else total

    @pl.when(part_ref[0] == 0)
    def _():
        write(act_own, act_peer, ffn_low)

    @pl.when(part_ref[0] != 0)
    def _():
        write(pre_own, pre_peer, hidden_low)


def feed_sums(part, actives, pre_lows, ffn_low, hidden_low, columns, received=None):
    slots, units = actives[0].shape
    width = ffn_low.shape[1]
    block = units // 4
    left = pl.BlockSpec((slots, block), lambda i: (0, i))
    right = pl.BlockSpec((slots, width), lambda i: (0, 0))
    rows = pl.BlockSpec((block, 2 * width), lambda i: (i, 0))
    more = [] if received is None else [received]
    return pl.pallas_call(
        lambda *refs: feed_sums_kernel(bool(more), *refs),
        grid=(4,),
        in_specs=[SCALAR] + [left] * 4 + [right] * 2 + [rows] * len(more),
        out_specs=rows,
        out_shape=jax.ShapeDtypeStruct((units, columns), F32),
        compiler_params=LIMIT,
        cost_estimate=pl.CostEstimate(
            flops=4 * slots * units * width, bytes_accessed=(8 + 8 * len(more)) * units * width, transcendentals=0
        ),
        name="feed_sums",
    )(part.reshape(1), *actives, *pre_lows, ffn_low, hidden_low, *more)


def attention_sums_kernel(received, part_ref, query_ref, key_ref, value_ref, mixture_ref, slot_ref, grad_ref, *refs):
    out_ref = refs[-1]
    second = lax.rem(pl.program_id(0), 2)

    def write(which, left, right):
        @pl.when(2 * part_ref[0] + second == which)
        def _():
            total = t_dot_in_kernel(left[...], right[...])
            out_ref[...] = total + refs[0][...] if received else total

    write(0, query_ref, slot_ref)
    write(1, key_ref, slot_ref)
    write(2, value_ref, slot_ref)
    write(3, mixture_ref, grad_ref)


def attention_sums(part, lows, mixture, rounded, attended_low, received=None, into=None, place=0):
    slots, heads = mixture.shape
    half = rounded.shape[1] // 2
    left = pl.BlockSpec((slots, heads), lambda i: (0, 0))
    right = pl.BlockSpec((slots, half), lambda i: (0, i // 2))
    rows = pl.BlockSpec((heads, half), lambda i: (i, 0))
    more = [] if received is None else [received, into]
    shape = (4 * heads, half) if into is None else into.shape
    return pl.pallas_call(
        lambda *refs: attention_sums_kernel(bool(more), *refs),
        grid=(4,),
        in_specs=[SCALAR] + [left] * 4 + [right] * 2 + ([rows, pl.BlockSpec(memory_space=pl.ANY)] if more else []),
        out_specs=pl.BlockSpec((heads, half), lambda i: (i, place)),
        out_shape=jax.ShapeDtypeStruct(shape, F32),
        input_output_aliases={8: 0} if more else {},
        compiler_params=LIMIT,
        cost_estimate=pl.CostEstimate(flops=8 * slots * heads * half, bytes_accessed=16 * heads * half, transcendentals=0),
        name="attention_sums",
    )(part.reshape(1), *lows, mixture, rounded, attended_low, *more)


def sort_kernel(piece_ref, down_ref, up_ref):
    chips, _, rows, width = piece_ref.shape
    for i in range(chips):
        down_ref[i * rows : (i + 1) * rows, :] = piece_ref[i, 0].astype(BF16)
        up = piece_ref[i, 1].astype(BF16)
        half = rows // 2
        up_ref[i * half : (i + 1) * half, :width] = up[:half]
        up_ref[i * half : (i + 1) * half, width:] = up[half:]


def sort_weights(gathered):
    chips, _, rows, width = gathered.shape
    step = 4
    units = chips * rows
    return pl.pallas_call(
        sort_kernel,
        grid=(chips // step,),
        in_specs=[pl.BlockSpec((step, 2, rows, width), lambda i: (i, 0, 0, 0))],
        out_specs=[
            pl.BlockSpec((step * rows, width), lambda i: (i, 0)),
            pl.BlockSpec((step * rows // 2, units), lambda i: (i, 0)),
        ],
        out_shape=[
            jax.ShapeDtypeStruct((units, width), BF16),
            jax.ShapeDtypeStruct((width, units), BF16),
        ],
        compiler_params=LIMIT,
        cost_estimate=pl.CostEstimate(flops=0, bytes_accessed=12 * units * width, transcendentals=0),
        name="sort_weights",
    )(gathered)


def rows_of(ref):
    chips, _, rows, columns = ref.shape
    return ref[...].reshape(chips * rows, columns)


def place_feed_kernel(down_in, up_in, down_ref, up_ref):
    down_ref[0] = rows_of(down_in)
    up_ref[0] = rows_of(up_in).T


def place_attention_kernel(query_in, key_in, value_in, output_in, query_ref, key_ref, value_ref, output_ref):
    query_ref[0] = rows_of(query_in).T
    key_ref[0] = rows_of(key_in).T
    value_ref[0] = rows_of(value_in).T
    output_ref[0] = rows_of(output_in)


def place_gradients(gathered, width):
    chips, _, rows, _ = gathered.shape
    step = 4
    units, block = chips * rows, step * rows
    half = width // 2

    def feed_in(core):
        return pl.BlockSpec((step, 1, rows, width), lambda l, i: (i, core, 0, 1 - l))

    def attention_in(core, which):
        return pl.BlockSpec((step, 1, rows, half), lambda l, i: (2 * i + which, core, 0, 5 - l))

    limit = pltpu.CompilerParams(vmem_limit_bytes=40 * 2**20)
    down, up = pl.pallas_call(
        place_feed_kernel,
        grid=(2, chips // step),
        in_specs=[feed_in(0), feed_in(1)],
        out_specs=[
            pl.BlockSpec((1, block, width), lambda l, i: (l, i, 0)),
            pl.BlockSpec((1, width, block), lambda l, i: (l, 0, i)),
        ],
        out_shape=[
            jax.ShapeDtypeStruct((2, units, width), F32),
            jax.ShapeDtypeStruct((2, width, units), F32),
        ],
        compiler_params=limit,
        name="place_feed",
    )(gathered, gathered)
    tall = pl.BlockSpec((1, half, block), lambda l, i: (l, i, 0))
    tall_shape = jax.ShapeDtypeStruct((2, width, block), F32)
    query, key, value, output = pl.pallas_call(
        place_attention_kernel,
        grid=(2, 2),
        in_specs=[attention_in(0, 0), attention_in(0, 1), attention_in(1, 0), attention_in(1, 1)],
        out_specs=[tall, tall, tall, pl.BlockSpec((1, block, half), lambda l, i: (l, 0, i))],
        out_shape=[tall_shape, tall_shape, tall_shape, jax.ShapeDtypeStruct((2, block, width), F32)],
        compiler_params=limit,
        name="place_attention",
    )(gathered, gathered, gathered, gathered)
    return query, key, value, output, up, down


def local(
    tokens,
    cotangent,
    lengths,
    repeats,
    query_weight,
    query_bias,
    key_weight,
    value_weight,
    value_bias,
    output_weight,
    output_bias,
    attn_gain,
    attn_shift,
    up_weight,
    up_bias,
    down_weight,
    down_bias,
    ffn_gain,
    ffn_shift,
):
    length = lengths[0]
    side = lax.axis_index("h")
    core = lax.axis_index("c")
    chip = lax.axis_index("y") * 4 + lax.axis_index("x")
    first_core = core == 0
    slots, width = tokens.shape
    half_slots = slots // 2
    units = up_weight.shape[2]
    columns = query_weight.shape[2]

    rows_down = units // 16
    pieces = weight_pieces(chip, core, down_weight, up_weight)
    gathered1, pieces2 = lax.all_gather(swap(pieces[0], "h"), PLANE + ("c",)), pieces[1]
    peer_up_bias = swap(up_bias.astype(F32), "h")

    def own_slots(values):
        return piece(values, side, half_slots)

    def attention_forward(layer, rounded):
        *attention, share = attend(
            layer,
            length,
            rounded,
            query_weight,
            query_bias[layer].astype(F32)[None],
            key_weight,
            value_weight,
            value_bias[layer].astype(F32)[None],
            output_weight,
        )
        return attention, own_slots(share), piece(share, 1 - side, half_slots)

    def attention_back(layer, saved, grad_one_sent, received):
        grad_one = 2.0 * in_order(side, grad_one_sent, received)
        attended_low = grad_one.astype(BF16)
        *lows, share, query_sum, value_sum = attend_back(
            layer, length, saved, attended_low, query_weight, key_weight, value_weight, output_weight
        )
        small = [jnp.concatenate([query_sum[0], value_sum[0]]), column_sum(attended_low)]
        return grad_one, lows, attended_low, share, small

    def feed_back(layer, gradient, saved):
        scaled_two, inverse_two, pres, actives, hidden_low, scaled_one, inverse_one = saved
        grad_two = normalize_back(gradient, ffn_gain[layer], scaled_two, inverse_two)
        ffn_low = grad_two.astype(BF16)
        downs, ups = (down_weight[layer], peer_down[layer]), (up_weight[layer], peer_up[layer])
        pre_lows = [
            (dot_t(ffn_low, down) * gelu_slope(pre)).astype(BF16) for down, pre in zip(downs, pres, strict=True)
        ]
        grad_hidden = grad_two + dot_t(pre_lows[0], ups[0]) + dot_t(pre_lows[1], ups[1])
        grad_one = normalize_back(grad_hidden, attn_gain[layer], scaled_one, inverse_one)
        shared = [
            jnp.sum(grad_hidden * scaled_one, axis=0),
            jnp.sum(grad_hidden, axis=0),
            column_sum(ffn_low),
            jnp.sum(gradient * scaled_two, axis=0),
            jnp.sum(gradient, axis=0),
        ]
        biases = [column_sum(item).reshape(-1, width) for item in pre_lows]
        return grad_one, ffn_low, pre_lows, shared, biases

    def layer_forward(layer, x_own, share, sent, peers):
        attended = share + swap(sent, "h") + output_bias[layer]
        hidden, scaled, inverse = normalize(x_own + attended, attn_gain[layer], attn_shift[layer])
        hidden_low = hidden.astype(BF16)
        pre = dot(hidden_low, up_weight[layer]) + up_bias[layer]
        active = gelu(pre).astype(BF16)
        ffn_out = dot(active, down_weight[layer])
        peer_down, peer_up = peers
        pre_peer = dot(hidden_low, peer_up) + peer_up_bias[layer]
        active_peer = gelu(pre_peer).astype(BF16)
        ffn_out = ffn_out + dot(active_peer, peer_down) + down_bias[layer]
        out, scaled_two, inverse_two = normalize(hidden + ffn_out, ffn_gain[layer], ffn_shift[layer])
        saved = (scaled_two, inverse_two, (pre, pre_peer), (active, active_peer), hidden_low, scaled, inverse)
        return out, saved

    att1, share, sent = attention_forward(0, tokens)
    pieces2, sent = together(pieces2, sent)
    pieces2 = swap(pieces2, "h")
    peers1 = sort_weights(gathered1.reshape(16, 2, rows_down, width))
    x2_own, saved1 = layer_forward(0, own_slots(tokens).astype(F32), share, sent, peers1)
    sent = 0.5 * x2_own
    pieces2, sent = together(pieces2, sent)
    gathered2 = lax.all_gather(pieces2, PLANE + ("c",))
    x2_low = (2.0 * in_order(side, sent, swap(sent, "h"))).astype(BF16)
    att2, share, sent = attention_forward(1, x2_low)
    peers2 = sort_weights(gathered2.reshape(16, 2, rows_down, width))
    _, saved2 = layer_forward(1, x2_own, share, sent, peers2)
    scaled_last = saved2[0]
    mixture = att2[3]
    peer_down, peer_up = (peers1[0], peers2[0]), (peers1[1], peers2[1])

    places = side * half_slots + jnp.arange(half_slots)
    weighting = jnp.where(places < length, repeats[0], 0).astype(F32)[:, None]
    gradient2 = own_slots(cotangent).astype(F32) * weighting
    grad_one_own, ffn_low, pre_lows, shared2, biases2 = feed_back(1, gradient2, saved2)
    sent = 0.5 * grad_one_own
    received = swap(sent, "h")
    feed2_received = swap(feed_sums(1 - core, saved2[3], pre_lows, ffn_low, saved2[4], 2 * width), "c")
    feed2 = feed_sums(core, saved2[3], pre_lows, ffn_low, saved2[4], 2 * width, feed2_received)
    feed2, received = together(feed2, received)
    feed2 = lax.psum_scatter(feed2, PLANE, tiled=True)
    _, lows2, attended_low2, share, small_att2 = attention_back(1, att2, sent, received)
    received = swap(piece(share, 1 - side, half_slots), "h")
    attn2_received = swap(attention_sums(1 - core, lows2, mixture, x2_low, attended_low2), "c")
    gradient1 = grad_one_own + own_slots(share) + received

    grad_one_own1, ffn_low, pre_lows, shared1, biases1 = feed_back(0, gradient1, saved1)
    sent = 0.5 * grad_one_own1
    received = swap(sent, "h")
    feed1_received = swap(feed_sums(1 - core, saved1[3], pre_lows, ffn_low, saved1[4], 2 * width), "c")
    rest = feed_sums(core, saved1[3], pre_lows, ffn_low, saved1[4], 3 * width, feed1_received)
    rest, received = together(rest, received)
    grad_one1, lows1, attended_low1, share, small_att1 = attention_back(0, att1, sent, received)
    attn1_received = swap(attention_sums(1 - core, lows1, att1[3], tokens, attended_low1), "c")
    rest = attention_sums(core, lows2, mixture, x2_low, attended_low2, attn2_received, rest, 4)
    rest = attention_sums(core, lows1, att1[3], tokens, attended_low1, attn1_received, rest, 5)
    rest, feed2 = together(rest, feed2)
    rest = lax.psum_scatter(rest, PLANE, tiled=True)

    def across(own, peer):
        diagonal = lax.ppermute(peer, ("zl", "h"), ((0, 3), (3, 0), (1, 2), (2, 1)))
        peer = swap(peer, "h") + diagonal
        own = own + swap(own, "zl")
        return jnp.concatenate([own[:, :width] + peer, own[:, width:]], axis=1)

    feed2 = across(feed2[:, :width], feed2[:, width:])
    feed2, rest = together(feed2, rest)
    rest = across(jnp.concatenate([rest[:, :width], rest[:, 2 * width :]], axis=1), rest[:, width : 2 * width])
    own = jnp.concatenate([feed2, rest], axis=1)
    gathered = lax.all_gather(own, PLANE + ("c",)).reshape(16, 2, *own.shape)
    grad_query, grad_key, grad_value, grad_output, grad_up, grad_down = place_gradients(gathered, width)

    token_grad = grad_one1 + pair_sum(share)
    scaled_last, token_grad = together(scaled_last, token_grad)
    scaled_all = in_order(side, scaled_last, swap(scaled_last, "h"))
    block_output = (scaled_all * ffn_gain[1] + ffn_shift[1]).astype(BF16)
    shared = jnp.stack(shared1 + shared2)
    mine = jnp.concatenate([shared, biases1[0], biases2[0]])
    mine = mine + swap(jnp.concatenate([shared, biases1[1], biases2[1]]), "h")
    small = jnp.concatenate([mine, jnp.stack(small_att1 + small_att2)])
    small, block_output = together(small, block_output)
    small = small + swap(small, "c")
    for axis, pairs in LINKS:
        small = small + lax.ppermute(small, axis, pairs)
    small = small + swap(small, "zl")
    bias_rows = units // width
    shared = small[:10].reshape(2, 5, width)
    grad_up_bias = small[10 : 10 + 2 * bias_rows].reshape(2, units)
    attention = small[10 + 2 * bias_rows :].reshape(2, 2, width)

    return (
        block_output,
        token_grad,
        grad_query,
        attention[:, 0, :columns],
        grad_key,
        grad_value,
        attention[:, 0, columns:],
        grad_output,
        attention[:, 1],
        shared[:, 0],
        shared[:, 1],
        grad_up,
        grad_up_bias,
        grad_down,
        shared[:, 2],
        shared[:, 3],
        shared[:, 4],
    )


def solution(mesh):
    fine = Mesh(mesh.devices.reshape(4, 2, 4, 2, 2), ("y", "zl", "x", "c", "h"))
    rows = ("y", "zl", "x", "c")
    in_specs = (
        P(rows, None),
        P(rows, None),
        P(rows),
        P(rows),
        P(None, None, "h"),
        P(None, "h"),
        P(None, None, "h"),
        P(None, None, "h"),
        P(None, "h"),
        P(None, "h", None),
        P(),
        P(),
        P(),
        P(None, None, "h"),
        P(None, "h"),
        P(None, "h", None),
        P(),
        P(),
        P(),
    )
    out_specs = (
        P(rows, None),
        P(rows, None),
        P(None, None, "h"),
        P(None, "h"),
        P(None, None, "h"),
        P(None, None, "h"),
        P(None, "h"),
        P(None, "h", None),
        P(),
        P(),
        P(),
        P(None, None, "h"),
        P(None, "h"),
        P(None, "h", None),
        P(),
        P(),
        P(),
    )
    return jax.shard_map(local, mesh=fine, in_specs=in_specs, out_specs=out_specs, check_vma=False)
```

```python
import jax
import jax.numpy as jnp
from jax import lax
from jax.experimental import pallas as pl
from jax.experimental.pallas import tpu as pltpu
from jax.sharding import Mesh, PartitionSpec as P

HEAD_DIM = 64
EPS = 1e-12
F32 = jnp.float32
BF16 = jnp.bfloat16
SWAP = ((0, 1), (1, 0))
EDGE0 = ((0, 1), (1, 0), (2, 3), (3, 2))
EDGE1 = ((1, 2), (2, 1), (3, 0), (0, 3))
LINKS = (("x", EDGE0), ("x", EDGE1), ("y", EDGE0), ("y", EDGE1))
PLANE = ("y", "x")


def normalize(summed, gain, shift):
    center = summed - jnp.mean(summed, axis=-1, keepdims=True)
    inverse = lax.rsqrt(jnp.mean(center * center, axis=-1, keepdims=True) + EPS)
    scaled = center * inverse
    return (scaled * gain + shift, scaled, inverse)


def normalize_back(gradient, gain, scaled, inverse):
    gained = gradient * gain
    return inverse * (
        gained
        - jnp.mean(gained, axis=-1, keepdims=True)
        - scaled * jnp.mean(gained * scaled, axis=-1, keepdims=True)
    )


def normal_cdf(values):
    return 0.5 * (1.0 + lax.erf(values * (0.5**0.5)))


def gelu(values):
    return values * normal_cdf(values)


def gelu_slope(values):
    density = jnp.exp(-0.5 * values * values) * 0.3989422804014327
    return normal_cdf(values) + values * density


def dot(left, right):
    return jnp.dot(left, right, preferred_element_type=F32)


def dot_t(left, right):
    return jnp.einsum("sd,fd->sf", left, right, preferred_element_type=F32)


def t_dot(left, right):
    return jnp.einsum("sf,sd->fd", left, right, preferred_element_type=F32)


def column_sum(values):
    return jnp.sum(values.astype(F32), axis=0)


def swap(values, axis):
    return lax.ppermute(values, axis, SWAP)


def pair_sum(values):
    return values + swap(values, "h")


def piece(values, index, size):
    return lax.dynamic_slice_in_dim(values, index * size, size, 0)


def ring_parts(values, axis, dim):
    place = lax.axis_index(axis)
    kept = lax.dynamic_index_in_dim(values, place, dim, keepdims=False)
    received = []
    for distance in (1, 3, 2):
        sent = lax.dynamic_index_in_dim(values, lax.rem(place + distance, 4), dim, keepdims=False)
        pairs = [(start, (start + distance) % 4) for start in range(4)]
        received.append(lax.ppermute(sent, axis, pairs))
    return [kept, *received]


def plane_sum(values):
    rows, columns = values.shape
    values = values.reshape(4, 4, 2, rows // 32, columns)
    x_first = ring_parts(values[:, :, 0], "x", 1)
    y_first = ring_parts(values[:, :, 1], "y", 0)
    parts = together(*x_first, *y_first)
    x_first = ring_parts(sum(parts[1:4], parts[0]), "y", 0)
    y_first = ring_parts(sum(parts[5:], parts[4]), "x", 0)
    parts = together(*x_first, *y_first)
    return jnp.concatenate([sum(parts[1:4], parts[0]), sum(parts[5:], parts[4])])


def in_order(side, mine, other):
    return jnp.concatenate([jnp.where(side == 0, mine, other), jnp.where(side == 0, other, mine)])


def together(*values):
    return lax.optimization_barrier(values)


def t_dot_in_kernel(left, right):
    return lax.dot_general(left, right, (((0,), (0,)), ((), ())), preferred_element_type=F32)


LIMIT = pltpu.CompilerParams(vmem_limit_bytes=48 * 2**20)
SCALAR = pl.BlockSpec(memory_space=pltpu.SMEM)


def across_lanes(left, right):
    return lax.dot_general(left, right, (((1,), (1,)), ((), ())), preferred_element_type=F32)


def attend_kernel(
    length_ref,
    slot_ref,
    query_weight,
    query_bias,
    key_weight,
    value_weight,
    value_bias,
    output_weight,
    query_ref,
    key_ref,
    value_ref,
    mixture_ref,
    logsum_ref,
    share_ref,
):
    slots = slot_ref[...]
    query_ref[...] = (dot(slots, query_weight[0]) + query_bias[...]).astype(BF16)
    key_ref[...] = dot(slots, key_weight[0]).astype(BF16)
    value_ref[...] = (dot(slots, value_weight[0]) + value_bias[...]).astype(BF16)
    count = slots.shape[0]
    valid = lax.broadcasted_iota(jnp.int32, (count, count), 0) < length_ref[0]
    for head in range(2):
        cut = slice(head * HEAD_DIM, (head + 1) * HEAD_DIM)
        scores = across_lanes(key_ref[:, cut], query_ref[:, cut]) * HEAD_DIM**-0.5
        scores = jnp.where(valid, scores, -1e30)
        highest = jnp.max(scores, axis=0, keepdims=True)
        raised = jnp.exp(scores - highest)
        totals = jnp.sum(raised, axis=0, keepdims=True)
        probs = (raised * (1.0 / totals)).astype(BF16)
        mixture_ref[:, cut] = t_dot_in_kernel(probs, value_ref[:, cut]).astype(BF16)
        logsum_ref[0, head : head + 1, :] = highest + jnp.log(totals)
    share = dot(mixture_ref[...], output_weight[0])

    @pl.when(pl.program_id(0) == 0)
    def _():
        share_ref[...] = share

    @pl.when(pl.program_id(0) != 0)
    def _():
        share_ref[...] += share


def attend(layer, length, slots, query_weight, query_bias, key_weight, value_weight, value_bias, output_weight):
    count, width = slots.shape
    heads = query_weight.shape[2]
    pair = 2 * HEAD_DIM
    steps = heads // pair
    whole = pl.BlockSpec((count, width), lambda i: (0, 0))
    weight = pl.BlockSpec((1, width, pair), lambda i: (layer, 0, i))
    bias = pl.BlockSpec((1, pair), lambda i: (0, i))
    part = pl.BlockSpec((count, pair), lambda i: (0, i))
    part_shape = jax.ShapeDtypeStruct((count, heads), BF16)
    return pl.pallas_call(
        attend_kernel,
        grid=(steps,),
        in_specs=[SCALAR, whole, weight, bias, weight, weight, bias]
        + [pl.BlockSpec((1, pair, width), lambda i: (layer, i, 0))],
        out_specs=[part] * 4 + [pl.BlockSpec((1, 2, count), lambda i: (i, 0, 0)), whole],
        out_shape=[part_shape] * 4
        + [jax.ShapeDtypeStruct((steps, 2, count), F32), jax.ShapeDtypeStruct((count, width), F32)],
        compiler_params=LIMIT,
        cost_estimate=pl.CostEstimate(
            flops=8 * count * width * heads + 4 * count * count * heads,
            bytes_accessed=8 * width * heads + 8 * count * width,
            transcendentals=count * count * heads // HEAD_DIM,
        ),
        name="attend",
    )(length.reshape(1), slots, query_weight, query_bias, key_weight, value_weight, value_bias, output_weight)


def attend_back_kernel(
    length_ref,
    query_ref,
    key_ref,
    value_ref,
    logsum_ref,
    grad_ref,
    query_weight,
    key_weight,
    value_weight,
    output_weight,
    query_low,
    key_low,
    value_low,
    share_ref,
    query_sum,
    value_sum,
):
    grads = across_lanes(grad_ref[...], output_weight[0]).astype(BF16)
    count = grads.shape[0]
    valid = lax.broadcasted_iota(jnp.int32, (count, count), 0) < length_ref[0]
    scale = HEAD_DIM**-0.5
    for head in range(2):
        cut = slice(head * HEAD_DIM, (head + 1) * HEAD_DIM)
        queries, keys, grad = query_ref[:, cut], key_ref[:, cut], grads[:, cut]
        scores = jnp.where(valid, across_lanes(keys, queries) * scale, -1e30)
        probs = jnp.exp(scores - logsum_ref[0, head : head + 1, :])
        grad_probs = across_lanes(value_ref[:, cut], grad)
        inner = jnp.sum(probs * grad_probs, axis=0, keepdims=True)
        grad_scores = (probs * (grad_probs - inner)).astype(BF16)
        query_low[:, cut] = (t_dot_in_kernel(grad_scores, keys) * scale).astype(BF16)
        key_low[:, cut] = (dot(grad_scores, queries) * scale).astype(BF16)
        value_low[:, cut] = dot(probs.astype(BF16), grad).astype(BF16)
    query_sum[...] = jnp.sum(query_low[...].astype(F32), axis=0, keepdims=True)
    value_sum[...] = jnp.sum(value_low[...].astype(F32), axis=0, keepdims=True)
    share = across_lanes(query_low[...], query_weight[0])
    share += across_lanes(key_low[...], key_weight[0])
    share += across_lanes(value_low[...], value_weight[0])

    @pl.when(pl.program_id(0) == 0)
    def _():
        share_ref[...] = share

    @pl.when(pl.program_id(0) != 0)
    def _():
        share_ref[...] += share


def attend_back(layer, length, saved, attended_low, query_weight, key_weight, value_weight, output_weight):
    queries, keys, values, _, logsum = saved
    count, width = attended_low.shape
    heads = queries.shape[1]
    pair = 2 * HEAD_DIM
    steps = heads // pair
    whole = pl.BlockSpec((count, width), lambda i: (0, 0))
    weight = pl.BlockSpec((1, width, pair), lambda i: (layer, 0, i))
    part = pl.BlockSpec((count, pair), lambda i: (0, i))
    part_shape = jax.ShapeDtypeStruct((count, heads), BF16)
    sums = pl.BlockSpec((1, pair), lambda i: (0, i))
    sums_shape = jax.ShapeDtypeStruct((1, heads), F32)
    return pl.pallas_call(
        attend_back_kernel,
        grid=(steps,),
        in_specs=[SCALAR, part, part, part, pl.BlockSpec((1, 2, count), lambda i: (i, 0, 0)), whole]
        + [weight] * 3
        + [pl.BlockSpec((1, pair, width), lambda i: (layer, i, 0))],
        out_specs=[part] * 3 + [whole, sums, sums],
        out_shape=[part_shape] * 3 + [jax.ShapeDtypeStruct((count, width), F32), sums_shape, sums_shape],
        compiler_params=LIMIT,
        cost_estimate=pl.CostEstimate(
            flops=8 * count * width * heads + 10 * count * count * heads,
            bytes_accessed=8 * width * heads + 8 * count * width,
            transcendentals=count * count * heads // HEAD_DIM,
        ),
        name="attend_back",
    )(length.reshape(1), queries, keys, values, logsum, attended_low, query_weight, key_weight, value_weight, output_weight)


def pieces_kernel(place_ref, down_in, up_in, piece_ref):
    width = piece_ref.shape[2]

    @pl.when(place_ref[1] == 0)
    def _():
        piece_ref[0] = down_in[0].astype(F32)

    @pl.when(place_ref[1] != 0)
    def _():
        half = up_in.shape[1]
        piece_ref[0, :half, :] = up_in[0, :, :width].astype(F32)
        piece_ref[0, half:, :] = up_in[0, :, width:].astype(F32)


def weight_pieces(chip, core, down_weight, up_weight):
    layers, units, width = down_weight.shape
    rows = units // 16
    return pl.pallas_call(
        pieces_kernel,
        grid_spec=pltpu.PrefetchScalarGridSpec(
            num_scalar_prefetch=1,
            grid=(layers,),
            in_specs=[
                pl.BlockSpec((1, rows, width), lambda l, place: (l, place[0], 0)),
                pl.BlockSpec((1, rows // 2, units), lambda l, place: (l, place[0], 0)),
            ],
            out_specs=pl.BlockSpec((1, rows, width), lambda l, place: (l, 0, 0)),
        ),
        out_shape=jax.ShapeDtypeStruct((layers, rows, width), F32),
        compiler_params=LIMIT,
        name="weight_pieces",
    )(jnp.stack([chip, core]), down_weight, up_weight)


def feed_sums_kernel(received, part_ref, act_own, act_peer, pre_own, pre_peer, ffn_low, hidden_low, *refs):
    out_ref = refs[-1]
    width = ffn_low.shape[1]

    def write(own, peer, right):
        for k, left in enumerate((own, peer)):
            total = t_dot_in_kernel(left[...], right[...])
            cut = slice(k * width, (k + 1) * width)
            out_ref[:, cut] = total + refs[0][:, cut] if received else total

    @pl.when(part_ref[0] == 0)
    def _():
        write(act_own, act_peer, ffn_low)

    @pl.when(part_ref[0] != 0)
    def _():
        write(pre_own, pre_peer, hidden_low)


def feed_sums(part, actives, pre_lows, ffn_low, hidden_low, columns, received=None):
    slots, units = actives[0].shape
    width = ffn_low.shape[1]
    block = units // 4
    left = pl.BlockSpec((slots, block), lambda i: (0, i))
    right = pl.BlockSpec((slots, width), lambda i: (0, 0))
    rows = pl.BlockSpec((block, 2 * width), lambda i: (i, 0))
    more = [] if received is None else [received]
    return pl.pallas_call(
        lambda *refs: feed_sums_kernel(bool(more), *refs),
        grid=(4,),
        in_specs=[SCALAR] + [left] * 4 + [right] * 2 + [rows] * len(more),
        out_specs=rows,
        out_shape=jax.ShapeDtypeStruct((units, columns), F32),
        compiler_params=LIMIT,
        cost_estimate=pl.CostEstimate(
            flops=4 * slots * units * width, bytes_accessed=(8 + 8 * len(more)) * units * width, transcendentals=0
        ),
        name="feed_sums",
    )(part.reshape(1), *actives, *pre_lows, ffn_low, hidden_low, *more)


def attention_sums_kernel(received, part_ref, query_ref, key_ref, value_ref, mixture_ref, slot_ref, grad_ref, *refs):
    out_ref = refs[-1]
    second = lax.rem(pl.program_id(0), 2)

    def write(which, left, right):
        @pl.when(2 * part_ref[0] + second == which)
        def _():
            total = t_dot_in_kernel(left[...], right[...])
            out_ref[...] = total + refs[0][...] if received else total

    write(0, query_ref, slot_ref)
    write(1, key_ref, slot_ref)
    write(2, value_ref, slot_ref)
    write(3, mixture_ref, grad_ref)


def attention_sums(part, lows, mixture, rounded, attended_low, received=None, columns=None, into=None):
    slots, heads = mixture.shape
    half = rounded.shape[1] // 2
    left = pl.BlockSpec((slots, heads), lambda i: (0, 0))
    right = pl.BlockSpec((slots, half), lambda i: (0, i // 2))
    rows = pl.BlockSpec((heads, half), lambda i: (i, 0))
    more = [item for item in (received, into) if item is not None]
    place = 0 if into is None else 1
    shape = (4 * heads, half if columns is None else columns)
    return pl.pallas_call(
        lambda *refs: attention_sums_kernel(received is not None, *refs),
        grid=(4,),
        in_specs=[SCALAR] + [left] * 4 + [right] * 2 + [rows, pl.BlockSpec(memory_space=pl.ANY)][: len(more)],
        out_specs=pl.BlockSpec((heads, half), lambda i: (i, place)),
        out_shape=jax.ShapeDtypeStruct(shape, F32),
        input_output_aliases={8: 0} if place else {},
        compiler_params=LIMIT,
        cost_estimate=pl.CostEstimate(flops=8 * slots * heads * half, bytes_accessed=16 * heads * half, transcendentals=0),
        name="attention_sums",
    )(part.reshape(1), *lows, mixture, rounded, attended_low, *more)


def sort_kernel(piece_ref, down_ref, up_ref):
    chips, _, rows, width = piece_ref.shape
    for i in range(chips):
        down_ref[i * rows : (i + 1) * rows, :] = piece_ref[i, 0].astype(BF16)
        up = piece_ref[i, 1].astype(BF16)
        half = rows // 2
        up_ref[i * half : (i + 1) * half, :width] = up[:half]
        up_ref[i * half : (i + 1) * half, width:] = up[half:]


def sort_weights(gathered):
    chips, _, rows, width = gathered.shape
    step = 4
    units = chips * rows
    return pl.pallas_call(
        sort_kernel,
        grid=(chips // step,),
        in_specs=[pl.BlockSpec((step, 2, rows, width), lambda i: (i, 0, 0, 0))],
        out_specs=[
            pl.BlockSpec((step * rows, width), lambda i: (i, 0)),
            pl.BlockSpec((step * rows // 2, units), lambda i: (i, 0)),
        ],
        out_shape=[
            jax.ShapeDtypeStruct((units, width), BF16),
            jax.ShapeDtypeStruct((width, units), BF16),
        ],
        compiler_params=LIMIT,
        cost_estimate=pl.CostEstimate(flops=0, bytes_accessed=12 * units * width, transcendentals=0),
        name="sort_weights",
    )(gathered)


def rows_of(ref):
    chips, _, rows, columns = ref.shape
    return ref[...].reshape(chips * rows, columns)


def place_feed_kernel(down_in, up_in, down_ref, up_ref):
    down_ref[0] = rows_of(down_in)
    up_ref[0] = rows_of(up_in).T


def place_attention_kernel(query_in, key_in, value_in, output_in, query_ref, key_ref, value_ref, output_ref):
    query_ref[0] = rows_of(query_in).T
    key_ref[0] = rows_of(key_in).T
    value_ref[0] = rows_of(value_in).T
    output_ref[0] = rows_of(output_in)


def place_gradients(gathered, width):
    chips, _, rows, _ = gathered.shape
    step = 4
    units, block = chips * rows, step * rows
    half = width // 2

    def feed_in(core):
        return pl.BlockSpec((step, 1, rows, width), lambda l, i: (i, core, 0, 1 - l))

    def attention_in(core, which):
        return pl.BlockSpec((step, 1, rows, half), lambda l, i: (2 * i + which, core, 0, 5 - l))

    limit = pltpu.CompilerParams(vmem_limit_bytes=40 * 2**20)
    down, up = pl.pallas_call(
        place_feed_kernel,
        grid=(2, chips // step),
        in_specs=[feed_in(0), feed_in(1)],
        out_specs=[
            pl.BlockSpec((1, block, width), lambda l, i: (l, i, 0)),
            pl.BlockSpec((1, width, block), lambda l, i: (l, 0, i)),
        ],
        out_shape=[
            jax.ShapeDtypeStruct((2, units, width), F32),
            jax.ShapeDtypeStruct((2, width, units), F32),
        ],
        compiler_params=limit,
        name="place_feed",
    )(gathered, gathered)
    tall = pl.BlockSpec((1, half, block), lambda l, i: (l, i, 0))
    tall_shape = jax.ShapeDtypeStruct((2, width, block), F32)
    query, key, value, output = pl.pallas_call(
        place_attention_kernel,
        grid=(2, 2),
        in_specs=[attention_in(0, 0), attention_in(0, 1), attention_in(1, 0), attention_in(1, 1)],
        out_specs=[tall, tall, tall, pl.BlockSpec((1, block, half), lambda l, i: (l, 0, i))],
        out_shape=[tall_shape, tall_shape, tall_shape, jax.ShapeDtypeStruct((2, block, width), F32)],
        compiler_params=limit,
        name="place_attention",
    )(gathered, gathered, gathered, gathered)
    return query, key, value, output, up, down


def local(
    tokens,
    cotangent,
    lengths,
    repeats,
    query_weight,
    query_bias,
    key_weight,
    value_weight,
    value_bias,
    output_weight,
    output_bias,
    attn_gain,
    attn_shift,
    up_weight,
    up_bias,
    down_weight,
    down_bias,
    ffn_gain,
    ffn_shift,
):
    length = lengths[0]
    side = lax.axis_index("h")
    core = lax.axis_index("c")
    chip = lax.axis_index("y") * 4 + lax.axis_index("x")
    first_core = core == 0
    slots, width = tokens.shape
    half_slots = slots // 2
    units = up_weight.shape[2]
    columns = query_weight.shape[2]

    rows_down = units // 16
    pieces = weight_pieces(chip, core, down_weight, up_weight)
    gathered1, pieces2 = lax.all_gather(swap(pieces[0], "h"), PLANE + ("c",)), pieces[1]
    peer_up_bias = swap(up_bias.astype(F32), "h")

    def own_slots(values):
        return piece(values, side, half_slots)

    def attention_forward(layer, rounded):
        *attention, share = attend(
            layer,
            length,
            rounded,
            query_weight,
            query_bias[layer].astype(F32)[None],
            key_weight,
            value_weight,
            value_bias[layer].astype(F32)[None],
            output_weight,
        )
        return attention, own_slots(share), piece(share, 1 - side, half_slots)

    def attention_back(layer, saved, grad_one_sent, received):
        grad_one = 2.0 * in_order(side, grad_one_sent, received)
        attended_low = grad_one.astype(BF16)
        *lows, share, query_sum, value_sum = attend_back(
            layer, length, saved, attended_low, query_weight, key_weight, value_weight, output_weight
        )
        small = [jnp.concatenate([query_sum[0], value_sum[0]]), column_sum(attended_low)]
        return grad_one, lows, attended_low, share, small

    def feed_back(layer, gradient, saved):
        scaled_two, inverse_two, pres, actives, hidden_low, scaled_one, inverse_one = saved
        grad_two = normalize_back(gradient, ffn_gain[layer], scaled_two, inverse_two)
        ffn_low = grad_two.astype(BF16)
        downs, ups = (down_weight[layer], peer_down[layer]), (up_weight[layer], peer_up[layer])
        pre_lows = [
            (dot_t(ffn_low, down) * gelu_slope(pre)).astype(BF16) for down, pre in zip(downs, pres, strict=True)
        ]
        grad_hidden = grad_two + dot_t(pre_lows[0], ups[0]) + dot_t(pre_lows[1], ups[1])
        grad_one = normalize_back(grad_hidden, attn_gain[layer], scaled_one, inverse_one)
        shared = [
            jnp.sum(grad_hidden * scaled_one, axis=0),
            jnp.sum(grad_hidden, axis=0),
            column_sum(ffn_low),
            jnp.sum(gradient * scaled_two, axis=0),
            jnp.sum(gradient, axis=0),
        ]
        biases = [column_sum(item).reshape(-1, width) for item in pre_lows]
        return grad_one, ffn_low, pre_lows, shared, biases

    def layer_forward(layer, x_own, share, received, peers):
        attended = share + received + output_bias[layer]
        hidden, scaled, inverse = normalize(x_own + attended, attn_gain[layer], attn_shift[layer])
        hidden_low = hidden.astype(BF16)
        pre = dot(hidden_low, up_weight[layer]) + up_bias[layer]
        active = gelu(pre).astype(BF16)
        ffn_out = dot(active, down_weight[layer])
        peer_down, peer_up = peers
        pre_peer = dot(hidden_low, peer_up) + peer_up_bias[layer]
        active_peer = gelu(pre_peer).astype(BF16)
        ffn_out = ffn_out + dot(active_peer, peer_down) + down_bias[layer]
        out, scaled_two, inverse_two = normalize(hidden + ffn_out, ffn_gain[layer], ffn_shift[layer])
        saved = (scaled_two, inverse_two, (pre, pre_peer), (active, active_peer), hidden_low, scaled, inverse)
        return out, saved

    att1, share, sent = attention_forward(0, tokens)
    pieces2, sent = together(pieces2, sent)
    pieces2 = swap(pieces2, "h")
    peers1 = sort_weights(gathered1.reshape(16, 2, rows_down, width))
    x2_own, saved1 = layer_forward(0, own_slots(tokens).astype(F32), share, swap(sent, "h"), peers1)
    sent = 0.5 * x2_own
    pieces2, sent = together(pieces2, sent)
    gathered2 = lax.all_gather(pieces2, PLANE + ("c",))
    x2_low = (2.0 * in_order(side, sent, swap(sent, "h"))).astype(BF16)
    att2, share, sent = attention_forward(1, x2_low)
    peers2 = sort_weights(gathered2.reshape(16, 2, rows_down, width))
    sent, peer_down, peer_up = together(swap(sent, "h"), *peers2)
    _, saved2 = layer_forward(1, x2_own, share, sent, (peer_down, peer_up))
    scaled_last = saved2[0]
    mixture = att2[3]
    peer_down, peer_up = (peers1[0], peers2[0]), (peers1[1], peers2[1])

    places = side * half_slots + jnp.arange(half_slots)
    weighting = jnp.where(places < length, repeats[0], 0).astype(F32)[:, None]
    gradient2 = own_slots(cotangent).astype(F32) * weighting
    grad_one_own, ffn_low, pre_lows, shared2, biases2 = feed_back(1, gradient2, saved2)
    sent = 0.5 * grad_one_own
    received = swap(sent, "h")
    feed2_received = swap(feed_sums(1 - core, saved2[3], pre_lows, ffn_low, saved2[4], 2 * width), "c")
    feed2 = feed_sums(core, saved2[3], pre_lows, ffn_low, saved2[4], 2 * width, feed2_received)
    feed2, received = together(feed2, received)
    feed2 = lax.psum_scatter(feed2, PLANE, tiled=True)
    _, lows2, attended_low2, share, small_att2 = attention_back(1, att2, sent, received)
    received = swap(piece(share, 1 - side, half_slots), "h")
    attn2_received = swap(attention_sums(1 - core, lows2, mixture, x2_low, attended_low2), "c")
    gradient1 = grad_one_own + own_slots(share) + received

    grad_one_own1, ffn_low, pre_lows, shared1, biases1 = feed_back(0, gradient1, saved1)
    sent = 0.5 * grad_one_own1
    received = swap(sent, "h")
    feed1_received = swap(feed_sums(1 - core, saved1[3], pre_lows, ffn_low, saved1[4], 2 * width), "c")
    rest = feed_sums(core, saved1[3], pre_lows, ffn_low, saved1[4], 2 * width, feed1_received)
    rest, received = together(rest, received)
    grad_one1, lows1, attended_low1, share, small_att1 = attention_back(0, att1, sent, received)
    attn = attention_sums(core, lows2, mixture, x2_low, attended_low2, attn2_received, width)
    rest, feed2, *lows1 = together(rest, feed2, *lows1)
    rest = lax.psum_scatter(rest, PLANE, tiled=True)
    attn1_received = swap(attention_sums(1 - core, lows1, att1[3], tokens, attended_low1), "c")
    attn = attention_sums(core, lows1, att1[3], tokens, attended_low1, attn1_received, width, attn)
    attn = plane_sum(attn)

    def across(values):
        own, peer = values[:, :width], values[:, width:]
        diagonal = lax.ppermute(peer, ("zl", "h"), ((0, 3), (3, 0), (1, 2), (2, 1)))
        return own + swap(own, "zl") + (swap(peer, "h") + diagonal)

    feed2 = across(feed2)
    attn = attn + swap(attn, "zl")
    feed2, attn, rest = together(feed2, attn, rest)
    own = jnp.concatenate([feed2, across(rest), attn], axis=1)
    gathered = lax.all_gather(own, PLANE + ("c",)).reshape(16, 2, *own.shape)
    grad_query, grad_key, grad_value, grad_output, grad_up, grad_down = place_gradients(gathered, width)

    token_grad = grad_one1 + pair_sum(share)
    scaled_last, token_grad = together(scaled_last, token_grad)
    scaled_all = in_order(side, scaled_last, swap(scaled_last, "h"))
    block_output = (scaled_all * ffn_gain[1] + ffn_shift[1]).astype(BF16)
    shared = jnp.stack(shared1 + shared2)
    mine = jnp.concatenate([shared, biases1[0], biases2[0]])
    mine = mine + swap(jnp.concatenate([shared, biases1[1], biases2[1]]), "h")
    small = jnp.concatenate([mine, jnp.stack(small_att1 + small_att2)])
    small, block_output = together(small, block_output)
    small = small + swap(small, "c")
    for axis, pairs in LINKS:
        small = small + lax.ppermute(small, axis, pairs)
    small = small + swap(small, "zl")
    bias_rows = units // width
    shared = small[:10].reshape(2, 5, width)
    grad_up_bias = small[10 : 10 + 2 * bias_rows].reshape(2, units)
    attention = small[10 + 2 * bias_rows :].reshape(2, 2, width)

    return (
        block_output,
        token_grad,
        grad_query,
        attention[:, 0, :columns],
        grad_key,
        grad_value,
        attention[:, 0, columns:],
        grad_output,
        attention[:, 1],
        shared[:, 0],
        shared[:, 1],
        grad_up,
        grad_up_bias,
        grad_down,
        shared[:, 2],
        shared[:, 3],
        shared[:, 4],
    )


def solution(mesh):
    fine = Mesh(mesh.devices.reshape(4, 2, 4, 2, 2), ("y", "zl", "x", "c", "h"))
    rows = ("y", "zl", "x", "c")
    in_specs = (
        P(rows, None),
        P(rows, None),
        P(rows),
        P(rows),
        P(None, None, "h"),
        P(None, "h"),
        P(None, None, "h"),
        P(None, None, "h"),
        P(None, "h"),
        P(None, "h", None),
        P(),
        P(),
        P(),
        P(None, None, "h"),
        P(None, "h"),
        P(None, "h", None),
        P(),
        P(),
        P(),
    )
    out_specs = (
        P(rows, None),
        P(rows, None),
        P(None, None, "h"),
        P(None, "h"),
        P(None, None, "h"),
        P(None, None, "h"),
        P(None, "h"),
        P(None, "h", None),
        P(),
        P(),
        P(),
        P(None, None, "h"),
        P(None, "h"),
        P(None, "h", None),
        P(),
        P(),
        P(),
    )
    return jax.shard_map(local, mesh=fine, in_specs=in_specs, out_specs=out_specs, check_vma=False)
```

```python
import jax
import jax.numpy as jnp
from jax import lax
from jax.experimental import pallas as pl
from jax.experimental.pallas import tpu as pltpu
from jax.sharding import Mesh, PartitionSpec as P

HEAD_DIM = 64
EPS = 1e-12
F32 = jnp.float32
BF16 = jnp.bfloat16
SWAP = ((0, 1), (1, 0))
EDGE0 = ((0, 1), (1, 0), (2, 3), (3, 2))
EDGE1 = ((1, 2), (2, 1), (3, 0), (0, 3))
LINKS = (("x", EDGE0), ("x", EDGE1), ("y", EDGE0), ("y", EDGE1))
PLANE = ("y", "x")


def normalize(summed, gain, shift):
    center = summed - jnp.mean(summed, axis=-1, keepdims=True)
    inverse = lax.rsqrt(jnp.mean(center * center, axis=-1, keepdims=True) + EPS)
    scaled = center * inverse
    return (scaled * gain + shift, scaled, inverse)


def normalize_back(gradient, gain, scaled, inverse):
    gained = gradient * gain
    return inverse * (
        gained
        - jnp.mean(gained, axis=-1, keepdims=True)
        - scaled * jnp.mean(gained * scaled, axis=-1, keepdims=True)
    )


def normal_cdf(values):
    return 0.5 * (1.0 + lax.erf(values * (0.5**0.5)))


def gelu(values):
    return values * normal_cdf(values)


def gelu_slope(values):
    density = jnp.exp(-0.5 * values * values) * 0.3989422804014327
    return normal_cdf(values) + values * density


def dot(left, right):
    return jnp.dot(left, right, preferred_element_type=F32)


def dot_t(left, right):
    return jnp.einsum("sd,fd->sf", left, right, preferred_element_type=F32)


def t_dot(left, right):
    return jnp.einsum("sf,sd->fd", left, right, preferred_element_type=F32)


def column_sum(values):
    return jnp.sum(values.astype(F32), axis=0)


def swap(values, axis):
    return lax.ppermute(values, axis, SWAP)


def pair_sum(values):
    return values + swap(values, "h")


def piece(values, index, size):
    return lax.dynamic_slice_in_dim(values, index * size, size, 0)


def ring_parts(values, axis, dim):
    place = lax.axis_index(axis)
    kept = lax.dynamic_index_in_dim(values, place, dim, keepdims=False)
    received = []
    for distance in (1, 3, 2):
        sent = lax.dynamic_index_in_dim(values, lax.rem(place + distance, 4), dim, keepdims=False)
        pairs = [(start, (start + distance) % 4) for start in range(4)]
        received.append(lax.ppermute(sent, axis, pairs))
    return [kept, *received]


def plane_sum(values):
    rows, columns = values.shape
    values = values.reshape(4, 4, 2, rows // 32, columns)
    x_first = ring_parts(values[:, :, 0], "x", 1)
    y_first = ring_parts(values[:, :, 1], "y", 0)
    parts = together(*x_first, *y_first)
    x_first = ring_parts(sum(parts[1:4], parts[0]), "y", 0)
    y_first = ring_parts(sum(parts[5:], parts[4]), "x", 0)
    parts = together(*x_first, *y_first)
    return jnp.concatenate([sum(parts[1:4], parts[0]), sum(parts[5:], parts[4])])


def in_order(side, mine, other):
    return jnp.concatenate([jnp.where(side == 0, mine, other), jnp.where(side == 0, other, mine)])


def together(*values):
    return lax.optimization_barrier(values)


def t_dot_in_kernel(left, right):
    return lax.dot_general(left, right, (((0,), (0,)), ((), ())), preferred_element_type=F32)


LIMIT = pltpu.CompilerParams(vmem_limit_bytes=48 * 2**20)
SCALAR = pl.BlockSpec(memory_space=pltpu.SMEM)


def across_lanes(left, right):
    return lax.dot_general(left, right, (((1,), (1,)), ((), ())), preferred_element_type=F32)


def attend_kernel(
    length_ref,
    slot_ref,
    query_weight,
    query_bias,
    key_weight,
    value_weight,
    value_bias,
    output_weight,
    query_ref,
    key_ref,
    value_ref,
    mixture_ref,
    logsum_ref,
    share_ref,
):
    slots = slot_ref[...]
    query_ref[...] = (dot(slots, query_weight[0]) + query_bias[...]).astype(BF16)
    key_ref[...] = dot(slots, key_weight[0]).astype(BF16)
    value_ref[...] = (dot(slots, value_weight[0]) + value_bias[...]).astype(BF16)
    count = slots.shape[0]
    valid = lax.broadcasted_iota(jnp.int32, (count, count), 0) < length_ref[0]
    for head in range(2):
        cut = slice(head * HEAD_DIM, (head + 1) * HEAD_DIM)
        scores = across_lanes(key_ref[:, cut], query_ref[:, cut]) * HEAD_DIM**-0.5
        scores = jnp.where(valid, scores, -1e30)
        highest = jnp.max(scores, axis=0, keepdims=True)
        raised = jnp.exp(scores - highest)
        totals = jnp.sum(raised, axis=0, keepdims=True)
        probs = (raised * (1.0 / totals)).astype(BF16)
        mixture_ref[:, cut] = t_dot_in_kernel(probs, value_ref[:, cut]).astype(BF16)
        logsum_ref[0, head : head + 1, :] = highest + jnp.log(totals)
    share = dot(mixture_ref[...], output_weight[0])

    @pl.when(pl.program_id(0) == 0)
    def _():
        share_ref[...] = share

    @pl.when(pl.program_id(0) != 0)
    def _():
        share_ref[...] += share


def attend(layer, length, slots, query_weight, query_bias, key_weight, value_weight, value_bias, output_weight):
    count, width = slots.shape
    heads = query_weight.shape[2]
    pair = 2 * HEAD_DIM
    steps = heads // pair
    whole = pl.BlockSpec((count, width), lambda i: (0, 0))
    weight = pl.BlockSpec((1, width, pair), lambda i: (layer, 0, i))
    bias = pl.BlockSpec((1, pair), lambda i: (0, i))
    part = pl.BlockSpec((count, pair), lambda i: (0, i))
    part_shape = jax.ShapeDtypeStruct((count, heads), BF16)
    return pl.pallas_call(
        attend_kernel,
        grid=(steps,),
        in_specs=[SCALAR, whole, weight, bias, weight, weight, bias]
        + [pl.BlockSpec((1, pair, width), lambda i: (layer, i, 0))],
        out_specs=[part] * 4 + [pl.BlockSpec((1, 2, count), lambda i: (i, 0, 0)), whole],
        out_shape=[part_shape] * 4
        + [jax.ShapeDtypeStruct((steps, 2, count), F32), jax.ShapeDtypeStruct((count, width), F32)],
        compiler_params=LIMIT,
        cost_estimate=pl.CostEstimate(
            flops=8 * count * width * heads + 4 * count * count * heads,
            bytes_accessed=8 * width * heads + 8 * count * width,
            transcendentals=count * count * heads // HEAD_DIM,
        ),
        name="attend",
    )(length.reshape(1), slots, query_weight, query_bias, key_weight, value_weight, value_bias, output_weight)


def attend_back_kernel(
    length_ref,
    query_ref,
    key_ref,
    value_ref,
    logsum_ref,
    grad_ref,
    query_weight,
    key_weight,
    value_weight,
    output_weight,
    query_low,
    key_low,
    value_low,
    share_ref,
    query_sum,
    value_sum,
):
    grads = across_lanes(grad_ref[...], output_weight[0]).astype(BF16)
    count = grads.shape[0]
    valid = lax.broadcasted_iota(jnp.int32, (count, count), 0) < length_ref[0]
    scale = HEAD_DIM**-0.5
    for head in range(2):
        cut = slice(head * HEAD_DIM, (head + 1) * HEAD_DIM)
        queries, keys, grad = query_ref[:, cut], key_ref[:, cut], grads[:, cut]
        scores = jnp.where(valid, across_lanes(keys, queries) * scale, -1e30)
        probs = jnp.exp(scores - logsum_ref[0, head : head + 1, :])
        grad_probs = across_lanes(value_ref[:, cut], grad)
        inner = jnp.sum(probs * grad_probs, axis=0, keepdims=True)
        grad_scores = (probs * (grad_probs - inner)).astype(BF16)
        query_low[:, cut] = (t_dot_in_kernel(grad_scores, keys) * scale).astype(BF16)
        key_low[:, cut] = (dot(grad_scores, queries) * scale).astype(BF16)
        value_low[:, cut] = dot(probs.astype(BF16), grad).astype(BF16)
    query_sum[...] = jnp.sum(query_low[...].astype(F32), axis=0, keepdims=True)
    value_sum[...] = jnp.sum(value_low[...].astype(F32), axis=0, keepdims=True)
    share = across_lanes(query_low[...], query_weight[0])
    share += across_lanes(key_low[...], key_weight[0])
    share += across_lanes(value_low[...], value_weight[0])

    @pl.when(pl.program_id(0) == 0)
    def _():
        share_ref[...] = share

    @pl.when(pl.program_id(0) != 0)
    def _():
        share_ref[...] += share


def attend_back(layer, length, saved, attended_low, query_weight, key_weight, value_weight, output_weight):
    queries, keys, values, _, logsum = saved
    count, width = attended_low.shape
    heads = queries.shape[1]
    pair = 2 * HEAD_DIM
    steps = heads // pair
    whole = pl.BlockSpec((count, width), lambda i: (0, 0))
    weight = pl.BlockSpec((1, width, pair), lambda i: (layer, 0, i))
    part = pl.BlockSpec((count, pair), lambda i: (0, i))
    part_shape = jax.ShapeDtypeStruct((count, heads), BF16)
    sums = pl.BlockSpec((1, pair), lambda i: (0, i))
    sums_shape = jax.ShapeDtypeStruct((1, heads), F32)
    return pl.pallas_call(
        attend_back_kernel,
        grid=(steps,),
        in_specs=[SCALAR, part, part, part, pl.BlockSpec((1, 2, count), lambda i: (i, 0, 0)), whole]
        + [weight] * 3
        + [pl.BlockSpec((1, pair, width), lambda i: (layer, i, 0))],
        out_specs=[part] * 3 + [whole, sums, sums],
        out_shape=[part_shape] * 3 + [jax.ShapeDtypeStruct((count, width), F32), sums_shape, sums_shape],
        compiler_params=LIMIT,
        cost_estimate=pl.CostEstimate(
            flops=8 * count * width * heads + 10 * count * count * heads,
            bytes_accessed=8 * width * heads + 8 * count * width,
            transcendentals=count * count * heads // HEAD_DIM,
        ),
        name="attend_back",
    )(length.reshape(1), queries, keys, values, logsum, attended_low, query_weight, key_weight, value_weight, output_weight)


def pieces_kernel(place_ref, down_in, up_in, piece_ref):
    width = piece_ref.shape[2]

    @pl.when(place_ref[1] == 0)
    def _():
        piece_ref[0] = down_in[0].astype(F32)

    @pl.when(place_ref[1] != 0)
    def _():
        half = up_in.shape[1]
        piece_ref[0, :half, :] = up_in[0, :, :width].astype(F32)
        piece_ref[0, half:, :] = up_in[0, :, width:].astype(F32)


def weight_pieces(chip, core, down_weight, up_weight):
    layers, units, width = down_weight.shape
    rows = units // 16
    return pl.pallas_call(
        pieces_kernel,
        grid_spec=pltpu.PrefetchScalarGridSpec(
            num_scalar_prefetch=1,
            grid=(layers,),
            in_specs=[
                pl.BlockSpec((1, rows, width), lambda l, place: (l, place[0], 0)),
                pl.BlockSpec((1, rows // 2, units), lambda l, place: (l, place[0], 0)),
            ],
            out_specs=pl.BlockSpec((1, rows, width), lambda l, place: (l, 0, 0)),
        ),
        out_shape=jax.ShapeDtypeStruct((layers, rows, width), F32),
        compiler_params=LIMIT,
        name="weight_pieces",
    )(jnp.stack([chip, core]), down_weight, up_weight)


def feed_sums_kernel(received, part_ref, active, pre_low, ffn_low, hidden_low, *refs):
    out_ref = refs[-1]

    def write(left, right):
        total = t_dot_in_kernel(left[...], right[...])
        out_ref[...] = total + refs[0][...] if received else total

    @pl.when(part_ref[0] == 0)
    def _():
        write(active, ffn_low)

    @pl.when(part_ref[0] != 0)
    def _():
        write(pre_low, hidden_low)


def feed_sums(part, active, pre_low, ffn_low, hidden_low, received=None, columns=None, into=None):
    slots, units = active.shape
    width = ffn_low.shape[1]
    block = units // 4
    left = pl.BlockSpec((slots, block), lambda i: (0, i))
    right = pl.BlockSpec((slots, width), lambda i: (0, 0))
    rows = pl.BlockSpec((block, width), lambda i: (i, 0))
    more = [item for item in (received, into) if item is not None]
    place = 0 if into is None else 1
    return pl.pallas_call(
        lambda *refs: feed_sums_kernel(received is not None, *refs),
        grid=(4,),
        in_specs=[SCALAR] + [left] * 2 + [right] * 2 + [rows, pl.BlockSpec(memory_space=pl.ANY)][: len(more)],
        out_specs=pl.BlockSpec((block, width), lambda i: (i, place)),
        out_shape=jax.ShapeDtypeStruct((units, width if columns is None else columns), F32),
        input_output_aliases={6: 0} if place else {},
        compiler_params=LIMIT,
        cost_estimate=pl.CostEstimate(
            flops=2 * slots * units * width, bytes_accessed=(8 if more else 4) * units * width, transcendentals=0
        ),
        name="feed_sums",
    )(part.reshape(1), active, pre_low, ffn_low, hidden_low, *more)


def attention_sums_kernel(received, part_ref, query_ref, key_ref, value_ref, mixture_ref, slot_ref, grad_ref, *refs):
    out_ref = refs[-1]
    second = lax.rem(pl.program_id(0), 2)

    def write(which, left, right):
        @pl.when(2 * part_ref[0] + second == which)
        def _():
            total = t_dot_in_kernel(left[...], right[...])
            out_ref[...] = total + refs[0][...] if received else total

    write(0, query_ref, slot_ref)
    write(1, key_ref, slot_ref)
    write(2, value_ref, slot_ref)
    write(3, mixture_ref, grad_ref)


def attention_sums(part, lows, mixture, rounded, attended_low, received=None, into=None, place=0):
    slots, heads = mixture.shape
    half = rounded.shape[1] // 2
    left = pl.BlockSpec((slots, heads), lambda i: (0, 0))
    right = pl.BlockSpec((slots, half), lambda i: (0, i // 2))
    rows = pl.BlockSpec((heads, half), lambda i: (i, 0))
    more = [item for item in (received, into) if item is not None]
    shape = (4 * heads, half) if into is None else into.shape
    return pl.pallas_call(
        lambda *refs: attention_sums_kernel(received is not None, *refs),
        grid=(4,),
        in_specs=[SCALAR] + [left] * 4 + [right] * 2 + [rows, pl.BlockSpec(memory_space=pl.ANY)][: len(more)],
        out_specs=pl.BlockSpec((heads, half), lambda i: (i, place)),
        out_shape=jax.ShapeDtypeStruct(shape, F32),
        input_output_aliases={} if into is None else {8: 0},
        compiler_params=LIMIT,
        cost_estimate=pl.CostEstimate(flops=8 * slots * heads * half, bytes_accessed=16 * heads * half, transcendentals=0),
        name="attention_sums",
    )(part.reshape(1), *lows, mixture, rounded, attended_low, *more)


def sort_kernel(piece_ref, down_ref, up_ref):
    chips, _, rows, width = piece_ref.shape
    for i in range(chips):
        down_ref[i * rows : (i + 1) * rows, :] = piece_ref[i, 0].astype(BF16)
        up = piece_ref[i, 1].astype(BF16)
        half = rows // 2
        up_ref[i * half : (i + 1) * half, :width] = up[:half]
        up_ref[i * half : (i + 1) * half, width:] = up[half:]


def sort_weights(gathered):
    chips, _, rows, width = gathered.shape
    step = 4
    units = chips * rows
    return pl.pallas_call(
        sort_kernel,
        grid=(chips // step,),
        in_specs=[pl.BlockSpec((step, 2, rows, width), lambda i: (i, 0, 0, 0))],
        out_specs=[
            pl.BlockSpec((step * rows, width), lambda i: (i, 0)),
            pl.BlockSpec((step * rows // 2, units), lambda i: (i, 0)),
        ],
        out_shape=[
            jax.ShapeDtypeStruct((units, width), BF16),
            jax.ShapeDtypeStruct((width, units), BF16),
        ],
        compiler_params=LIMIT,
        cost_estimate=pl.CostEstimate(flops=0, bytes_accessed=12 * units * width, transcendentals=0),
        name="sort_weights",
    )(gathered)


def rows_of(ref):
    chips, _, rows, columns = ref.shape
    return ref[...].reshape(chips * rows, columns)


def place_feed_kernel(down_in, up_in, down_ref, up_ref):
    down_ref[0] = rows_of(down_in)
    up_ref[0] = rows_of(up_in).T


def place_attention_kernel(query_in, key_in, value_in, output_in, query_ref, key_ref, value_ref, output_ref):
    query_ref[0] = rows_of(query_in).T
    key_ref[0] = rows_of(key_in).T
    value_ref[0] = rows_of(value_in).T
    output_ref[0] = rows_of(output_in)


def place_gradients(gathered, width):
    chips, _, rows, _ = gathered.shape
    step = 4
    units, block = chips * rows, step * rows
    half = width // 2

    def feed_in(core):
        return pl.BlockSpec((step, 1, rows, width), lambda l, i: (i, core, 0, 1 - l))

    def attention_in(core, which):
        return pl.BlockSpec((step, 1, rows, half), lambda l, i: (2 * i + which, core, 0, 5 - l))

    limit = pltpu.CompilerParams(vmem_limit_bytes=40 * 2**20)
    down, up = pl.pallas_call(
        place_feed_kernel,
        grid=(2, chips // step),
        in_specs=[feed_in(0), feed_in(1)],
        out_specs=[
            pl.BlockSpec((1, block, width), lambda l, i: (l, i, 0)),
            pl.BlockSpec((1, width, block), lambda l, i: (l, 0, i)),
        ],
        out_shape=[
            jax.ShapeDtypeStruct((2, units, width), F32),
            jax.ShapeDtypeStruct((2, width, units), F32),
        ],
        compiler_params=limit,
        name="place_feed",
    )(gathered, gathered)
    tall = pl.BlockSpec((1, half, block), lambda l, i: (l, i, 0))
    tall_shape = jax.ShapeDtypeStruct((2, width, block), F32)
    query, key, value, output = pl.pallas_call(
        place_attention_kernel,
        grid=(2, 2),
        in_specs=[attention_in(0, 0), attention_in(0, 1), attention_in(1, 0), attention_in(1, 1)],
        out_specs=[tall, tall, tall, pl.BlockSpec((1, block, half), lambda l, i: (l, 0, i))],
        out_shape=[tall_shape, tall_shape, tall_shape, jax.ShapeDtypeStruct((2, block, width), F32)],
        compiler_params=limit,
        name="place_attention",
    )(gathered, gathered, gathered, gathered)
    return query, key, value, output, up, down


def local(
    tokens,
    cotangent,
    lengths,
    repeats,
    query_weight,
    query_bias,
    key_weight,
    value_weight,
    value_bias,
    output_weight,
    output_bias,
    attn_gain,
    attn_shift,
    up_weight,
    up_bias,
    down_weight,
    down_bias,
    ffn_gain,
    ffn_shift,
):
    length = lengths[0]
    side = lax.axis_index("h")
    core = lax.axis_index("c")
    chip = lax.axis_index("y") * 4 + lax.axis_index("x")
    first_core = core == 0
    slots, width = tokens.shape
    half_slots = slots // 2
    units = up_weight.shape[2]
    columns = query_weight.shape[2]

    rows_down = units // 16
    pieces = weight_pieces(chip, core, down_weight, up_weight)
    gathered1, pieces2 = lax.all_gather(swap(pieces[0], "h"), PLANE + ("c",)), pieces[1]
    peer_up_bias = swap(up_bias.astype(F32), "h")

    def own_slots(values):
        return piece(values, side, half_slots)

    def feed_weights_back(saved, pre_lows, ffn_low, columns):
        actives, hidden_low = saved[3], saved[4]
        received = [
            swap(feed_sums(1 - core, active, pre_low, ffn_low, hidden_low), "c")
            for active, pre_low in zip(actives, pre_lows, strict=True)
        ]
        total = feed_sums(core, actives[0], pre_lows[0], ffn_low, hidden_low, received[0], columns)
        return feed_sums(core, actives[1], pre_lows[1], ffn_low, hidden_low, received[1], columns, total)

    def attention_forward(layer, rounded):
        *attention, share = attend(
            layer,
            length,
            rounded,
            query_weight,
            query_bias[layer].astype(F32)[None],
            key_weight,
            value_weight,
            value_bias[layer].astype(F32)[None],
            output_weight,
        )
        return attention, own_slots(share), piece(share, 1 - side, half_slots)

    def attention_back(layer, saved, grad_one_sent, received):
        grad_one = 2.0 * in_order(side, grad_one_sent, received)
        attended_low = grad_one.astype(BF16)
        *lows, share, query_sum, value_sum = attend_back(
            layer, length, saved, attended_low, query_weight, key_weight, value_weight, output_weight
        )
        small = [jnp.concatenate([query_sum[0], value_sum[0]]), column_sum(attended_low)]
        return grad_one, lows, attended_low, share, small

    def feed_back(layer, gradient, saved):
        scaled_two, inverse_two, pres, actives, hidden_low, scaled_one, inverse_one = saved
        grad_two = normalize_back(gradient, ffn_gain[layer], scaled_two, inverse_two)
        ffn_low = grad_two.astype(BF16)
        downs, ups = (down_weight[layer], peer_down[layer]), (up_weight[layer], peer_up[layer])
        pre_lows = [
            (dot_t(ffn_low, down) * gelu_slope(pre)).astype(BF16) for down, pre in zip(downs, pres, strict=True)
        ]
        grad_hidden = grad_two + dot_t(pre_lows[0], ups[0]) + dot_t(pre_lows[1], ups[1])
        grad_one = normalize_back(grad_hidden, attn_gain[layer], scaled_one, inverse_one)
        shared = [
            jnp.sum(grad_hidden * scaled_one, axis=0),
            jnp.sum(grad_hidden, axis=0),
            column_sum(ffn_low),
            jnp.sum(gradient * scaled_two, axis=0),
            jnp.sum(gradient, axis=0),
        ]
        biases = [column_sum(item).reshape(-1, width) for item in pre_lows]
        return grad_one, ffn_low, pre_lows, shared, biases

    def layer_forward(layer, x_own, share, received, peers):
        attended = share + received + output_bias[layer]
        hidden, scaled, inverse = normalize(x_own + attended, attn_gain[layer], attn_shift[layer])
        hidden_low = hidden.astype(BF16)
        pre = dot(hidden_low, up_weight[layer]) + up_bias[layer]
        active = gelu(pre).astype(BF16)
        ffn_out = dot(active, down_weight[layer])
        peer_down, peer_up = peers
        pre_peer = dot(hidden_low, peer_up) + peer_up_bias[layer]
        active_peer = gelu(pre_peer).astype(BF16)
        ffn_out = ffn_out + dot(active_peer, peer_down) + down_bias[layer]
        out, scaled_two, inverse_two = normalize(hidden + ffn_out, ffn_gain[layer], ffn_shift[layer])
        saved = (scaled_two, inverse_two, (pre, pre_peer), (active, active_peer), hidden_low, scaled, inverse)
        return out, saved

    att1, share, sent = attention_forward(0, tokens)
    pieces2, sent = together(pieces2, sent)
    pieces2 = swap(pieces2, "h")
    peers1 = sort_weights(gathered1.reshape(16, 2, rows_down, width))
    x2_own, saved1 = layer_forward(0, own_slots(tokens).astype(F32), share, swap(sent, "h"), peers1)
    sent = 0.5 * x2_own
    pieces2, sent = together(pieces2, sent)
    gathered2 = lax.all_gather(pieces2, PLANE + ("c",))
    x2_low = (2.0 * in_order(side, sent, swap(sent, "h"))).astype(BF16)
    att2, share, sent = attention_forward(1, x2_low)
    peers2 = sort_weights(gathered2.reshape(16, 2, rows_down, width))
    sent, peer_down, peer_up = together(swap(sent, "h"), *peers2)
    _, saved2 = layer_forward(1, x2_own, share, sent, (peer_down, peer_up))
    scaled_last = saved2[0]
    mixture = att2[3]
    peer_down, peer_up = (peers1[0], peers2[0]), (peers1[1], peers2[1])

    places = side * half_slots + jnp.arange(half_slots)
    weighting = jnp.where(places < length, repeats[0], 0).astype(F32)[:, None]
    gradient2 = own_slots(cotangent).astype(F32) * weighting
    grad_one_own, ffn_low, pre_lows, shared2, biases2 = feed_back(1, gradient2, saved2)
    sent = 0.5 * grad_one_own
    received = swap(sent, "h")
    feed2 = feed_weights_back(saved2, pre_lows, ffn_low, 2 * width)
    feed2, received = together(feed2, received)
    feed2 = lax.psum_scatter(feed2, PLANE, tiled=True)
    _, lows2, attended_low2, share, small_att2 = attention_back(1, att2, sent, received)
    received = swap(piece(share, 1 - side, half_slots), "h")
    attn2_received = swap(attention_sums(1 - core, lows2, mixture, x2_low, attended_low2), "c")
    gradient1 = grad_one_own + own_slots(share) + received

    grad_one_own1, ffn_low, pre_lows, shared1, biases1 = feed_back(0, gradient1, saved1)
    sent = 0.5 * grad_one_own1
    received = swap(sent, "h")
    rest = feed_weights_back(saved1, pre_lows, ffn_low, 2 * width + columns)
    rest = attention_sums(core, lows2, mixture, x2_low, attended_low2, attn2_received, rest, 2 * width // columns)
    rest, received, feed2 = together(rest, received, feed2)
    rest = lax.psum_scatter(rest, PLANE, tiled=True)
    grad_one1, lows1, attended_low1, share, small_att1 = attention_back(0, att1, sent, received)
    attn1_received = swap(attention_sums(1 - core, lows1, att1[3], tokens, attended_low1), "c")
    attn1 = plane_sum(attention_sums(core, lows1, att1[3], tokens, attended_low1, attn1_received))

    def across(own, peer):
        diagonal = lax.ppermute(peer, ("zl", "h"), ((0, 3), (3, 0), (1, 2), (2, 1)))
        own = own + swap(own, "zl")
        peer = swap(peer, "h") + diagonal
        return jnp.concatenate([own[:, :width] + peer, own[:, width:]], axis=1)

    feed2 = across(feed2[:, :width], feed2[:, width:])
    attn1 = attn1 + swap(attn1, "zl")
    feed2, attn1, rest = together(feed2, attn1, rest)
    rest = across(jnp.concatenate([rest[:, :width], rest[:, 2 * width :]], axis=1), rest[:, width : 2 * width])
    own = jnp.concatenate([feed2, rest, attn1], axis=1)
    gathered = lax.all_gather(own, PLANE + ("c",)).reshape(16, 2, *own.shape)
    grad_query, grad_key, grad_value, grad_output, grad_up, grad_down = place_gradients(gathered, width)

    token_grad = grad_one1 + pair_sum(share)
    scaled_last, token_grad = together(scaled_last, token_grad)
    scaled_all = in_order(side, scaled_last, swap(scaled_last, "h"))
    block_output = (scaled_all * ffn_gain[1] + ffn_shift[1]).astype(BF16)
    shared = jnp.stack(shared1 + shared2)
    mine = jnp.concatenate([shared, biases1[0], biases2[0]])
    mine = mine + swap(jnp.concatenate([shared, biases1[1], biases2[1]]), "h")
    small = jnp.concatenate([mine, jnp.stack(small_att1 + small_att2)])
    small, block_output = together(small, block_output)
    small = small + swap(small, "c")
    for axis, pairs in LINKS:
        small = small + lax.ppermute(small, axis, pairs)
    small = small + swap(small, "zl")
    bias_rows = units // width
    shared = small[:10].reshape(2, 5, width)
    grad_up_bias = small[10 : 10 + 2 * bias_rows].reshape(2, units)
    attention = small[10 + 2 * bias_rows :].reshape(2, 2, width)

    return (
        block_output,
        token_grad,
        grad_query,
        attention[:, 0, :columns],
        grad_key,
        grad_value,
        attention[:, 0, columns:],
        grad_output,
        attention[:, 1],
        shared[:, 0],
        shared[:, 1],
        grad_up,
        grad_up_bias,
        grad_down,
        shared[:, 2],
        shared[:, 3],
        shared[:, 4],
    )


def solution(mesh):
    fine = Mesh(mesh.devices.reshape(4, 2, 4, 2, 2), ("y", "zl", "x", "c", "h"))
    rows = ("y", "zl", "x", "c")
    in_specs = (
        P(rows, None),
        P(rows, None),
        P(rows),
        P(rows),
        P(None, None, "h"),
        P(None, "h"),
        P(None, None, "h"),
        P(None, None, "h"),
        P(None, "h"),
        P(None, "h", None),
        P(),
        P(),
        P(),
        P(None, None, "h"),
        P(None, "h"),
        P(None, "h", None),
        P(),
        P(),
        P(),
    )
    out_specs = (
        P(rows, None),
        P(rows, None),
        P(None, None, "h"),
        P(None, "h"),
        P(None, None, "h"),
        P(None, None, "h"),
        P(None, "h"),
        P(None, "h", None),
        P(),
        P(),
        P(),
        P(None, None, "h"),
        P(None, "h"),
        P(None, "h", None),
        P(),
        P(),
        P(),
    )
    return jax.shard_map(local, mesh=fine, in_specs=in_specs, out_specs=out_specs, check_vma=False)
```

```python
import jax
import jax.numpy as jnp
from jax import lax
from jax.experimental import pallas as pl
from jax.experimental.pallas import tpu as pltpu
from jax.sharding import Mesh, PartitionSpec as P

HEAD_DIM = 64
EPS = 1e-12
F32 = jnp.float32
BF16 = jnp.bfloat16
SWAP = ((0, 1), (1, 0))
EDGE0 = ((0, 1), (1, 0), (2, 3), (3, 2))
EDGE1 = ((1, 2), (2, 1), (3, 0), (0, 3))
LINKS = (("x", EDGE0), ("x", EDGE1), ("y", EDGE0), ("y", EDGE1))
PLANE = ("y", "x")


def normalize(summed, gain, shift):
    center = summed - jnp.mean(summed, axis=-1, keepdims=True)
    inverse = lax.rsqrt(jnp.mean(center * center, axis=-1, keepdims=True) + EPS)
    scaled = center * inverse
    return (scaled * gain + shift, scaled, inverse)


def normalize_back(gradient, gain, scaled, inverse):
    gained = gradient * gain
    return inverse * (
        gained
        - jnp.mean(gained, axis=-1, keepdims=True)
        - scaled * jnp.mean(gained * scaled, axis=-1, keepdims=True)
    )


def normal_cdf(values):
    return 0.5 * (1.0 + lax.erf(values * (0.5**0.5)))


def gelu(values):
    return values * normal_cdf(values)


def gelu_slope(values):
    density = jnp.exp(-0.5 * values * values) * 0.3989422804014327
    return normal_cdf(values) + values * density


def dot(left, right):
    return jnp.dot(left, right, preferred_element_type=F32)


def dot_t(left, right):
    return jnp.einsum("sd,fd->sf", left, right, preferred_element_type=F32)


def t_dot(left, right):
    return jnp.einsum("sf,sd->fd", left, right, preferred_element_type=F32)


def column_sum(values):
    return jnp.sum(values.astype(F32), axis=0)


def swap(values, axis):
    return lax.ppermute(values, axis, SWAP)


def pair_sum(values):
    return values + swap(values, "h")


def piece(values, index, size):
    return lax.dynamic_slice_in_dim(values, index * size, size, 0)


def ring_parts(values, axis, dim):
    place = lax.axis_index(axis)
    kept = lax.dynamic_index_in_dim(values, place, dim, keepdims=False)
    received = []
    for distance in (1, 3, 2):
        sent = lax.dynamic_index_in_dim(values, lax.rem(place + distance, 4), dim, keepdims=False)
        pairs = [(start, (start + distance) % 4) for start in range(4)]
        received.append(lax.ppermute(sent, axis, pairs))
    return [kept, *received]


def plane_sum(values):
    rows, columns = values.shape
    values = values.reshape(4, 4, 2, rows // 32, columns)
    x_first = ring_parts(values[:, :, 0], "x", 1)
    y_first = ring_parts(values[:, :, 1], "y", 0)
    parts = together(*x_first, *y_first)
    x_first = ring_parts(sum(parts[1:4], parts[0]), "y", 0)
    y_first = ring_parts(sum(parts[5:], parts[4]), "x", 0)
    parts = together(*x_first, *y_first)
    return jnp.concatenate([sum(parts[1:4], parts[0]), sum(parts[5:], parts[4])])


def in_order(side, mine, other):
    return jnp.concatenate([jnp.where(side == 0, mine, other), jnp.where(side == 0, other, mine)])


def together(*values):
    return lax.optimization_barrier(values)


def t_dot_in_kernel(left, right):
    return lax.dot_general(left, right, (((0,), (0,)), ((), ())), preferred_element_type=F32)


LIMIT = pltpu.CompilerParams(vmem_limit_bytes=48 * 2**20)
SCALAR = pl.BlockSpec(memory_space=pltpu.SMEM)


def across_lanes(left, right):
    return lax.dot_general(left, right, (((1,), (1,)), ((), ())), preferred_element_type=F32)


def attend_kernel(
    place_ref,
    slot_ref,
    query_weight,
    query_bias,
    key_weight,
    value_weight,
    value_bias,
    output_weight,
    query_ref,
    key_ref,
    value_ref,
    mixture_ref,
    logsum_ref,
    own_ref,
    sent_ref,
):
    slots = slot_ref[...]
    query_ref[...] = (dot(slots, query_weight[0]) + query_bias[...]).astype(BF16)
    key_ref[...] = dot(slots, key_weight[0]).astype(BF16)
    value_ref[...] = (dot(slots, value_weight[0]) + value_bias[...]).astype(BF16)
    count = slots.shape[0]
    valid = lax.broadcasted_iota(jnp.int32, (count, count), 0) < place_ref[0]
    for head in range(2):
        cut = slice(head * HEAD_DIM, (head + 1) * HEAD_DIM)
        scores = across_lanes(key_ref[:, cut], query_ref[:, cut] * HEAD_DIM**-0.5)
        scores = jnp.where(valid, scores, -1e30)
        highest = jnp.max(scores, axis=0, keepdims=True)
        raised = jnp.exp(scores - highest)
        totals = jnp.sum(raised, axis=0, keepdims=True)
        probs = (raised * (1.0 / totals)).astype(BF16)
        mixture_ref[:, cut] = t_dot_in_kernel(probs, value_ref[:, cut]).astype(BF16)
        logsum_ref[0, head : head + 1, :] = highest + jnp.log(totals)
    half = count // 2
    for side, share_ref in ((place_ref[1], own_ref), (1 - place_ref[1], sent_ref)):
        rows = mixture_ref[pl.ds(pl.multiple_of(side * half, half), half), :]
        share = dot(rows, output_weight[0])

        @pl.when(pl.program_id(0) == 0)
        def _():
            share_ref[...] = share

        @pl.when(pl.program_id(0) != 0)
        def _():
            share_ref[...] += share


def attend(layer, length, side, slots, query_weight, query_bias, key_weight, value_weight, value_bias, output_weight):
    count, width = slots.shape
    heads = query_weight.shape[2]
    pair = 2 * HEAD_DIM
    steps = heads // pair
    whole = pl.BlockSpec((count, width), lambda i: (0, 0))
    weight = pl.BlockSpec((1, width, pair), lambda i: (layer, 0, i))
    bias = pl.BlockSpec((1, pair), lambda i: (0, i))
    part = pl.BlockSpec((count, pair), lambda i: (0, i))
    part_shape = jax.ShapeDtypeStruct((count, heads), BF16)
    return pl.pallas_call(
        attend_kernel,
        grid=(steps,),
        in_specs=[SCALAR, whole, weight, bias, weight, weight, bias]
        + [pl.BlockSpec((1, pair, width), lambda i: (layer, i, 0))],
        out_specs=[part] * 4
        + [pl.BlockSpec((1, 2, count), lambda i: (i, 0, 0))]
        + [pl.BlockSpec((count // 2, width), lambda i: (0, 0))] * 2,
        out_shape=[part_shape] * 4
        + [jax.ShapeDtypeStruct((steps, 2, count), F32)]
        + [jax.ShapeDtypeStruct((count // 2, width), F32)] * 2,
        compiler_params=LIMIT,
        cost_estimate=pl.CostEstimate(
            flops=8 * count * width * heads + 4 * count * count * heads,
            bytes_accessed=8 * width * heads + 8 * count * width,
            transcendentals=count * count * heads // HEAD_DIM,
        ),
        name="attend",
    )(jnp.stack([length, side]), slots, query_weight, query_bias, key_weight, value_weight, value_bias, output_weight)


def attend_back_kernel(
    length_ref,
    query_ref,
    key_ref,
    value_ref,
    logsum_ref,
    grad_ref,
    query_weight,
    key_weight,
    value_weight,
    output_weight,
    query_low,
    key_low,
    value_low,
    share_ref,
    query_sum,
    value_sum,
):
    grads = across_lanes(grad_ref[...], output_weight[0]).astype(BF16)
    count = grads.shape[0]
    valid = lax.broadcasted_iota(jnp.int32, (count, count), 0) < length_ref[0]
    scale = HEAD_DIM**-0.5
    for head in range(2):
        cut = slice(head * HEAD_DIM, (head + 1) * HEAD_DIM)
        queries, keys, grad = query_ref[:, cut], key_ref[:, cut], grads[:, cut]
        scores = jnp.where(valid, across_lanes(keys, queries * scale), -1e30)
        probs = jnp.exp(scores - logsum_ref[0, head : head + 1, :])
        grad_probs = across_lanes(value_ref[:, cut], grad)
        inner = jnp.sum(probs * grad_probs, axis=0, keepdims=True)
        grad_scores = (probs * (grad_probs - inner)).astype(BF16)
        query_low[:, cut] = (t_dot_in_kernel(grad_scores, keys) * scale).astype(BF16)
        key_low[:, cut] = (dot(grad_scores, queries) * scale).astype(BF16)
        value_low[:, cut] = dot(probs.astype(BF16), grad).astype(BF16)
    query_sum[...] = jnp.sum(query_low[...].astype(F32), axis=0, keepdims=True)
    value_sum[...] = jnp.sum(value_low[...].astype(F32), axis=0, keepdims=True)
    share = across_lanes(query_low[...], query_weight[0])
    share += across_lanes(key_low[...], key_weight[0])
    share += across_lanes(value_low[...], value_weight[0])

    @pl.when(pl.program_id(0) == 0)
    def _():
        share_ref[...] = share

    @pl.when(pl.program_id(0) != 0)
    def _():
        share_ref[...] += share


def attend_back(layer, length, saved, attended_low, query_weight, key_weight, value_weight, output_weight, *earlier):
    queries, keys, values, _, logsum = saved
    count, width = attended_low.shape
    heads = queries.shape[1]
    pair = 2 * HEAD_DIM
    steps = heads // pair
    whole = pl.BlockSpec((count, width), lambda i: (0, 0))
    weight = pl.BlockSpec((1, width, pair), lambda i: (layer, 0, i))
    part = pl.BlockSpec((count, pair), lambda i: (0, i))
    part_shape = jax.ShapeDtypeStruct((count, heads), BF16)
    sums = pl.BlockSpec((1, pair), lambda i: (0, i))
    sums_shape = jax.ShapeDtypeStruct((1, heads), F32)
    return pl.pallas_call(
        lambda *refs: attend_back_kernel(*refs[:10], *refs[10 + len(earlier) :]),
        grid=(steps,),
        in_specs=[SCALAR, part, part, part, pl.BlockSpec((1, 2, count), lambda i: (i, 0, 0)), whole]
        + [weight] * 3
        + [pl.BlockSpec((1, pair, width), lambda i: (layer, i, 0))]
        + [pl.BlockSpec(memory_space=pl.ANY)] * len(earlier),
        out_specs=[part] * 3 + [whole, sums, sums],
        out_shape=[part_shape] * 3 + [jax.ShapeDtypeStruct((count, width), F32), sums_shape, sums_shape],
        compiler_params=LIMIT,
        cost_estimate=pl.CostEstimate(
            flops=8 * count * width * heads + 10 * count * count * heads,
            bytes_accessed=8 * width * heads + 8 * count * width,
            transcendentals=count * count * heads // HEAD_DIM,
        ),
        name="attend_back",
    )(length.reshape(1), queries, keys, values, logsum, attended_low, query_weight, key_weight, value_weight, output_weight, *earlier)


def pieces_kernel(place_ref, down_in, up_in, piece_ref):
    width = piece_ref.shape[2]

    @pl.when(place_ref[1] == 0)
    def _():
        piece_ref[0] = down_in[0].astype(F32)

    @pl.when(place_ref[1] != 0)
    def _():
        half = up_in.shape[1]
        piece_ref[0, :half, :] = up_in[0, :, :width].astype(F32)
        piece_ref[0, half:, :] = up_in[0, :, width:].astype(F32)


def weight_pieces(chip, core, down_weight, up_weight):
    layers, units, width = down_weight.shape
    rows = units // 16
    return pl.pallas_call(
        pieces_kernel,
        grid_spec=pltpu.PrefetchScalarGridSpec(
            num_scalar_prefetch=1,
            grid=(layers,),
            in_specs=[
                pl.BlockSpec((1, rows, width), lambda l, place: (l, place[0], 0)),
                pl.BlockSpec((1, rows // 2, units), lambda l, place: (l, place[0], 0)),
            ],
            out_specs=pl.BlockSpec((1, rows, width), lambda l, place: (l, 0, 0)),
        ),
        out_shape=jax.ShapeDtypeStruct((layers, rows, width), F32),
        compiler_params=LIMIT,
        name="weight_pieces",
    )(jnp.stack([chip, core]), down_weight, up_weight)


def feed_sums_kernel(received, part_ref, active, pre_low, ffn_low, hidden_low, *refs):
    out_ref = refs[-1]

    def write(left, right):
        total = t_dot_in_kernel(left[...], right[...])
        out_ref[...] = total + refs[0][...] if received else total

    @pl.when(part_ref[0] == 0)
    def _():
        write(active, ffn_low)

    @pl.when(part_ref[0] != 0)
    def _():
        write(pre_low, hidden_low)


def feed_sums(part, active, pre_low, ffn_low, hidden_low, received=None, columns=None, into=None):
    slots, units = active.shape
    width = ffn_low.shape[1]
    block = units // 4
    left = pl.BlockSpec((slots, block), lambda i: (0, i))
    right = pl.BlockSpec((slots, width), lambda i: (0, 0))
    rows = pl.BlockSpec((block, width), lambda i: (i, 0))
    more = [item for item in (received, into) if item is not None]
    place = 0 if into is None else 1
    return pl.pallas_call(
        lambda *refs: feed_sums_kernel(received is not None, *refs),
        grid=(4,),
        in_specs=[SCALAR] + [left] * 2 + [right] * 2 + [rows, pl.BlockSpec(memory_space=pl.ANY)][: len(more)],
        out_specs=pl.BlockSpec((block, width), lambda i: (i, place)),
        out_shape=jax.ShapeDtypeStruct((units, width if columns is None else columns), F32),
        input_output_aliases={6: 0} if place else {},
        compiler_params=LIMIT,
        cost_estimate=pl.CostEstimate(
            flops=2 * slots * units * width, bytes_accessed=(8 if more else 4) * units * width, transcendentals=0
        ),
        name="feed_sums",
    )(part.reshape(1), active, pre_low, ffn_low, hidden_low, *more)


def attention_sums_kernel(received, part_ref, query_ref, key_ref, value_ref, mixture_ref, slot_ref, grad_ref, *refs):
    out_ref = refs[-1]
    second = lax.rem(pl.program_id(0), 2)

    def write(which, left, right):
        @pl.when(2 * part_ref[0] + second == which)
        def _():
            total = t_dot_in_kernel(left[...], right[...])
            out_ref[...] = total + refs[0][...] if received else total

    write(0, query_ref, slot_ref)
    write(1, key_ref, slot_ref)
    write(2, value_ref, slot_ref)
    write(3, mixture_ref, grad_ref)


def attention_sums(part, lows, mixture, rounded, attended_low, received=None, into=None, place=0):
    slots, heads = mixture.shape
    half = rounded.shape[1] // 2
    left = pl.BlockSpec((slots, heads), lambda i: (0, 0))
    right = pl.BlockSpec((slots, half), lambda i: (0, i // 2))
    rows = pl.BlockSpec((heads, half), lambda i: (i, 0))
    more = [item for item in (received, into) if item is not None]
    shape = (4 * heads, half) if into is None else into.shape
    return pl.pallas_call(
        lambda *refs: attention_sums_kernel(received is not None, *refs),
        grid=(4,),
        in_specs=[SCALAR] + [left] * 4 + [right] * 2 + [rows, pl.BlockSpec(memory_space=pl.ANY)][: len(more)],
        out_specs=pl.BlockSpec((heads, half), lambda i: (i, place)),
        out_shape=jax.ShapeDtypeStruct(shape, F32),
        input_output_aliases={} if into is None else {8: 0},
        compiler_params=LIMIT,
        cost_estimate=pl.CostEstimate(flops=8 * slots * heads * half, bytes_accessed=16 * heads * half, transcendentals=0),
        name="attention_sums",
    )(part.reshape(1), *lows, mixture, rounded, attended_low, *more)


def sort_kernel(piece_ref, down_ref, up_ref):
    chips, _, rows, width = piece_ref.shape
    for i in range(chips):
        down_ref[i * rows : (i + 1) * rows, :] = piece_ref[i, 0].astype(BF16)
        up = piece_ref[i, 1].astype(BF16)
        half = rows // 2
        up_ref[i * half : (i + 1) * half, :width] = up[:half]
        up_ref[i * half : (i + 1) * half, width:] = up[half:]


def sort_weights(gathered):
    chips, _, rows, width = gathered.shape
    step = 4
    units = chips * rows
    return pl.pallas_call(
        sort_kernel,
        grid=(chips // step,),
        in_specs=[pl.BlockSpec((step, 2, rows, width), lambda i: (i, 0, 0, 0))],
        out_specs=[
            pl.BlockSpec((step * rows, width), lambda i: (i, 0)),
            pl.BlockSpec((step * rows // 2, units), lambda i: (i, 0)),
        ],
        out_shape=[
            jax.ShapeDtypeStruct((units, width), BF16),
            jax.ShapeDtypeStruct((width, units), BF16),
        ],
        compiler_params=LIMIT,
        cost_estimate=pl.CostEstimate(flops=0, bytes_accessed=12 * units * width, transcendentals=0),
        name="sort_weights",
    )(gathered)


def rows_of(ref):
    chips, _, rows, columns = ref.shape
    return ref[...].reshape(chips * rows, columns)


def place_kernel(down_in, up_in, query_in, key_in, value_in, output_in, *refs):
    down_ref, up_ref, query_ref, key_ref, value_ref, output_ref = refs[-6:]
    down_ref[0] = rows_of(down_in)
    up_ref[0] = rows_of(up_in).T
    query_ref[0] = rows_of(query_in).T
    key_ref[0] = rows_of(key_in).T
    value_ref[0] = rows_of(value_in).T
    output_ref[0] = rows_of(output_in)


def place_gradients(gathered, width, layer_feed, layer_attention, into=()):
    chips, _, rows, _ = gathered.shape
    step = 4
    units, block = chips * rows, step * rows
    half = width // 2

    def feed_in(core):
        return pl.BlockSpec((step, 1, rows, width), lambda i: (i, core, 0, 0))

    def attention_in(core, which):
        return pl.BlockSpec((step, 1, rows, half), lambda i: (2 * (i // 2) + which, core, 0, 2))

    tall = pl.BlockSpec((1, half, block), lambda i: (layer_attention, i // 2, 0))
    tall_shape = jax.ShapeDtypeStruct((2, width, block), F32)
    return pl.pallas_call(
        place_kernel,
        grid=(chips // step,),
        in_specs=[feed_in(0), feed_in(1)]
        + [attention_in(0, 0), attention_in(0, 1), attention_in(1, 0), attention_in(1, 1)]
        + [pl.BlockSpec(memory_space=pl.ANY)] * len(into),
        out_specs=[
            pl.BlockSpec((1, block, width), lambda i: (layer_feed, i, 0)),
            pl.BlockSpec((1, width, block), lambda i: (layer_feed, 0, i)),
        ]
        + [tall] * 3
        + [pl.BlockSpec((1, block, half), lambda i: (layer_attention, 0, i // 2))],
        out_shape=[
            jax.ShapeDtypeStruct((2, units, width), F32),
            jax.ShapeDtypeStruct((2, width, units), F32),
        ]
        + [tall_shape] * 3
        + [jax.ShapeDtypeStruct((2, block, width), F32)],
        input_output_aliases={6 + k: k for k in range(len(into))},
        compiler_params=LIMIT,
        cost_estimate=pl.CostEstimate(flops=0, bytes_accessed=24 * units * width, transcendentals=0),
        name="place_gradients",
    )(*[gathered] * 6, *into)


def local(
    tokens,
    cotangent,
    lengths,
    repeats,
    query_weight,
    query_bias,
    key_weight,
    value_weight,
    value_bias,
    output_weight,
    output_bias,
    attn_gain,
    attn_shift,
    up_weight,
    up_bias,
    down_weight,
    down_bias,
    ffn_gain,
    ffn_shift,
):
    length = lengths[0]
    side = lax.axis_index("h")
    core = lax.axis_index("c")
    chip = lax.axis_index("y") * 4 + lax.axis_index("x")
    first_core = core == 0
    slots, width = tokens.shape
    half_slots = slots // 2
    units = up_weight.shape[2]
    columns = query_weight.shape[2]

    rows_down = units // 16
    pieces = weight_pieces(chip, core, down_weight, up_weight)
    gathered1, pieces2 = lax.all_gather(swap(pieces[0], "h"), PLANE + ("c",)), pieces[1]
    peer_up_bias = swap(up_bias.astype(F32), "h")

    def own_slots(values):
        return piece(values, side, half_slots)

    def feed_weights_back(saved, pre_lows, ffn_low, columns):
        actives, hidden_low = saved[3], saved[4]
        received = [
            swap(feed_sums(1 - core, active, pre_low, ffn_low, hidden_low), "c")
            for active, pre_low in zip(actives, pre_lows, strict=True)
        ]
        total = feed_sums(core, actives[0], pre_lows[0], ffn_low, hidden_low, received[0], columns)
        return feed_sums(core, actives[1], pre_lows[1], ffn_low, hidden_low, received[1], columns, total)

    def attention_forward(layer, rounded):
        *attention, share, sent = attend(
            layer,
            length,
            side,
            rounded,
            query_weight,
            query_bias[layer].astype(F32)[None],
            key_weight,
            value_weight,
            value_bias[layer].astype(F32)[None],
            output_weight,
        )
        return attention, share, sent

    def attention_back(layer, saved, grad_one_sent, received, *earlier):
        grad_one = 2.0 * in_order(side, grad_one_sent, received)
        attended_low = grad_one.astype(BF16)
        *lows, share, query_sum, value_sum = attend_back(
            layer, length, saved, attended_low, query_weight, key_weight, value_weight, output_weight, *earlier
        )
        small = [jnp.concatenate([query_sum[0], value_sum[0]]), column_sum(attended_low)]
        return grad_one, lows, attended_low, share, small

    def feed_back(layer, gradient, saved):
        scaled_two, inverse_two, pres, actives, hidden_low, scaled_one, inverse_one = saved
        grad_two = normalize_back(gradient, ffn_gain[layer], scaled_two, inverse_two)
        ffn_low = grad_two.astype(BF16)
        downs, ups = (down_weight[layer], peer_down[layer]), (up_weight[layer], peer_up[layer])
        pre_lows = [
            (dot_t(ffn_low, down) * gelu_slope(pre)).astype(BF16) for down, pre in zip(downs, pres, strict=True)
        ]
        grad_hidden = grad_two + dot_t(pre_lows[0], ups[0]) + dot_t(pre_lows[1], ups[1])
        grad_one = normalize_back(grad_hidden, attn_gain[layer], scaled_one, inverse_one)
        shared = [
            jnp.sum(grad_hidden * scaled_one, axis=0),
            jnp.sum(grad_hidden, axis=0),
            column_sum(ffn_low),
            jnp.sum(gradient * scaled_two, axis=0),
            jnp.sum(gradient, axis=0),
        ]
        biases = [column_sum(item).reshape(-1, width) for item in pre_lows]
        return grad_one, ffn_low, pre_lows, shared, biases

    def layer_forward(layer, x_own, share, received, peers):
        attended = share + received + output_bias[layer]
        hidden, scaled, inverse = normalize(x_own + attended, attn_gain[layer], attn_shift[layer])
        hidden_low = hidden.astype(BF16)
        pre = dot(hidden_low, up_weight[layer]) + up_bias[layer]
        active = gelu(pre).astype(BF16)
        ffn_out = dot(active, down_weight[layer])
        peer_down, peer_up = peers
        pre_peer = dot(hidden_low, peer_up) + peer_up_bias[layer]
        active_peer = gelu(pre_peer).astype(BF16)
        ffn_out = ffn_out + dot(active_peer, peer_down) + down_bias[layer]
        out, scaled_two, inverse_two = normalize(hidden + ffn_out, ffn_gain[layer], ffn_shift[layer])
        saved = (scaled_two, inverse_two, (pre, pre_peer), (active, active_peer), hidden_low, scaled, inverse)
        return out, saved

    att1, share, sent = attention_forward(0, tokens)
    pieces2, sent = together(pieces2, sent)
    pieces2 = swap(pieces2, "h")
    peers1 = sort_weights(gathered1.reshape(16, 2, rows_down, width))
    x2_own, saved1 = layer_forward(0, own_slots(tokens).astype(F32), share, swap(sent, "h"), peers1)
    sent = 0.5 * x2_own
    pieces2, sent = together(pieces2, sent)
    gathered2 = lax.all_gather(pieces2, PLANE + ("c",))
    x2_low = (2.0 * in_order(side, sent, swap(sent, "h"))).astype(BF16)
    att2, share, sent = attention_forward(1, x2_low)
    peers2 = sort_weights(gathered2.reshape(16, 2, rows_down, width))
    sent, peer_down, peer_up = together(swap(sent, "h"), *peers2)
    _, saved2 = layer_forward(1, x2_own, share, sent, (peer_down, peer_up))
    scaled_last = saved2[0]
    mixture = att2[3]
    peer_down, peer_up = (peers1[0], peers2[0]), (peers1[1], peers2[1])

    places = side * half_slots + jnp.arange(half_slots)
    weighting = jnp.where(places < length, repeats[0], 0).astype(F32)[:, None]
    gradient2 = own_slots(cotangent).astype(F32) * weighting
    grad_one_own, ffn_low, pre_lows, shared2, biases2 = feed_back(1, gradient2, saved2)
    sent = 0.5 * grad_one_own
    received = swap(sent, "h")
    feed2 = feed_weights_back(saved2, pre_lows, ffn_low, 2 * width)
    earlier = feed2
    feed2 = lax.psum_scatter(feed2, PLANE, tiled=True)
    _, lows2, attended_low2, share, small_att2 = attention_back(1, att2, sent, received, earlier)
    received = swap(piece(share, 1 - side, half_slots), "h")
    attn2_received = swap(attention_sums(1 - core, lows2, mixture, x2_low, attended_low2), "c")
    gradient1 = grad_one_own + own_slots(share) + received

    grad_one_own1, ffn_low, pre_lows, shared1, biases1 = feed_back(0, gradient1, saved1)
    sent = 0.5 * grad_one_own1
    received = swap(sent, "h")
    rest = feed_weights_back(saved1, pre_lows, ffn_low, 2 * width + columns)
    rest = attention_sums(core, lows2, mixture, x2_low, attended_low2, attn2_received, rest, 2 * width // columns)
    rest, received, feed2 = together(rest, received, feed2)
    rest = lax.psum_scatter(rest, PLANE, tiled=True)
    grad_one1, lows1, attended_low1, share, small_att1 = attention_back(0, att1, sent, received)
    attn1_received = swap(attention_sums(1 - core, lows1, att1[3], tokens, attended_low1), "c")
    attn1 = plane_sum(attention_sums(core, lows1, att1[3], tokens, attended_low1, attn1_received))

    def across(own, peer):
        diagonal = lax.ppermute(peer, ("zl", "h"), ((0, 3), (3, 0), (1, 2), (2, 1)))
        own = own + swap(own, "zl")
        peer = swap(peer, "h") + diagonal
        return jnp.concatenate([own[:, :width] + peer, own[:, width:]], axis=1)

    def gather(*parts):
        own = jnp.concatenate(parts, axis=1)
        return lax.all_gather(own, PLANE + ("c",)).reshape(16, 2, *own.shape)

    feed2 = across(feed2[:, :width], feed2[:, width:])
    attn1 = attn1 + swap(attn1, "zl")
    feed2, attn1, rest = together(feed2, attn1, rest)
    gathered = gather(feed2, attn1)
    rest = across(jnp.concatenate([rest[:, :width], rest[:, 2 * width :]], axis=1), rest[:, width : 2 * width])
    placed = place_gradients(gathered, width, 1, 0)
    placed = place_gradients(gather(rest), width, 0, 1, placed)
    grad_down, grad_up, grad_query, grad_key, grad_value, grad_output = placed

    token_grad = grad_one1 + pair_sum(share)
    scaled_last, token_grad = together(scaled_last, token_grad)
    scaled_all = in_order(side, scaled_last, swap(scaled_last, "h"))
    block_output = (scaled_all * ffn_gain[1] + ffn_shift[1]).astype(BF16)
    shared = jnp.stack(shared1 + shared2)
    mine = jnp.concatenate([shared, biases1[0], biases2[0]])
    mine = mine + swap(jnp.concatenate([shared, biases1[1], biases2[1]]), "h")
    small = jnp.concatenate([mine, jnp.stack(small_att1 + small_att2)])
    small, block_output = together(small, block_output)
    small = small + swap(small, "c")
    for axis, pairs in LINKS:
        small = small + lax.ppermute(small, axis, pairs)
    small = small + swap(small, "zl")
    bias_rows = units // width
    shared = small[:10].reshape(2, 5, width)
    grad_up_bias = small[10 : 10 + 2 * bias_rows].reshape(2, units)
    attention = small[10 + 2 * bias_rows :].reshape(2, 2, width)

    return (
        block_output,
        token_grad,
        grad_query,
        attention[:, 0, :columns],
        grad_key,
        grad_value,
        attention[:, 0, columns:],
        grad_output,
        attention[:, 1],
        shared[:, 0],
        shared[:, 1],
        grad_up,
        grad_up_bias,
        grad_down,
        shared[:, 2],
        shared[:, 3],
        shared[:, 4],
    )


def solution(mesh):
    fine = Mesh(mesh.devices.reshape(4, 2, 4, 2, 2), ("y", "zl", "x", "c", "h"))
    rows = ("y", "zl", "x", "c")
    in_specs = (
        P(rows, None),
        P(rows, None),
        P(rows),
        P(rows),
        P(None, None, "h"),
        P(None, "h"),
        P(None, None, "h"),
        P(None, None, "h"),
        P(None, "h"),
        P(None, "h", None),
        P(),
        P(),
        P(),
        P(None, None, "h"),
        P(None, "h"),
        P(None, "h", None),
        P(),
        P(),
        P(),
    )
    out_specs = (
        P(rows, None),
        P(rows, None),
        P(None, None, "h"),
        P(None, "h"),
        P(None, None, "h"),
        P(None, None, "h"),
        P(None, "h"),
        P(None, "h", None),
        P(),
        P(),
        P(),
        P(None, None, "h"),
        P(None, "h"),
        P(None, "h", None),
        P(),
        P(),
        P(),
    )
    return jax.shard_map(local, mesh=fine, in_specs=in_specs, out_specs=out_specs, check_vma=False)
```

```python
import jax
import jax.numpy as jnp
from jax import lax
from jax.experimental import pallas as pl
from jax.experimental.pallas import tpu as pltpu
from jax.sharding import Mesh, PartitionSpec as P

HEAD_DIM = 64
EPS = 1e-12
F32 = jnp.float32
BF16 = jnp.bfloat16
SWAP = ((0, 1), (1, 0))
EDGE0 = ((0, 1), (1, 0), (2, 3), (3, 2))
EDGE1 = ((1, 2), (2, 1), (3, 0), (0, 3))
LINKS = (("x", EDGE0), ("x", EDGE1), ("y", EDGE0), ("y", EDGE1))
PLANE = ("y", "x")


def normalize(summed, gain, shift):
    center = summed - jnp.mean(summed, axis=-1, keepdims=True)
    inverse = lax.rsqrt(jnp.mean(center * center, axis=-1, keepdims=True) + EPS)
    scaled = center * inverse
    return (scaled * gain + shift, scaled, inverse)


def normalize_back(gradient, gain, scaled, inverse):
    gained = gradient * gain
    return inverse * (
        gained
        - jnp.mean(gained, axis=-1, keepdims=True)
        - scaled * jnp.mean(gained * scaled, axis=-1, keepdims=True)
    )


def normal_cdf(values):
    return 0.5 * (1.0 + lax.erf(values * (0.5**0.5)))


def gelu(values):
    return values * normal_cdf(values)


def gelu_slope(values):
    density = jnp.exp(-0.5 * values * values) * 0.3989422804014327
    return normal_cdf(values) + values * density


def dot(left, right):
    return jnp.dot(left, right, preferred_element_type=F32)


def dot_t(left, right):
    return jnp.einsum("sd,fd->sf", left, right, preferred_element_type=F32)


def t_dot(left, right):
    return jnp.einsum("sf,sd->fd", left, right, preferred_element_type=F32)


def column_sum(values):
    return jnp.sum(values.astype(F32), axis=0)


def swap(values, axis):
    return lax.ppermute(values, axis, SWAP)


def pair_sum(values):
    return values + swap(values, "h")


def piece(values, index, size):
    return lax.dynamic_slice_in_dim(values, index * size, size, 0)


def ring_parts(values, axis, dim):
    place = lax.axis_index(axis)
    kept = lax.dynamic_index_in_dim(values, place, dim, keepdims=False)
    received = []
    for distance in (1, 3, 2):
        sent = lax.dynamic_index_in_dim(values, lax.rem(place + distance, 4), dim, keepdims=False)
        pairs = [(start, (start + distance) % 4) for start in range(4)]
        received.append(lax.ppermute(sent, axis, pairs))
    return [kept, *received]


def plane_sum(values):
    rows, columns = values.shape
    values = values.reshape(4, 4, 2, rows // 32, columns)
    x_first = ring_parts(values[:, :, 0], "x", 1)
    y_first = ring_parts(values[:, :, 1], "y", 0)
    parts = together(*x_first, *y_first)
    x_first = ring_parts(sum(parts[1:4], parts[0]), "y", 0)
    y_first = ring_parts(sum(parts[5:], parts[4]), "x", 0)
    parts = together(*x_first, *y_first)
    return jnp.concatenate([sum(parts[1:4], parts[0]), sum(parts[5:], parts[4])])


def in_order(side, mine, other):
    return jnp.concatenate([jnp.where(side == 0, mine, other), jnp.where(side == 0, other, mine)])


def together(*values):
    return lax.optimization_barrier(values)


def t_dot_in_kernel(left, right):
    return lax.dot_general(left, right, (((0,), (0,)), ((), ())), preferred_element_type=F32)


LIMIT = pltpu.CompilerParams(vmem_limit_bytes=48 * 2**20)
SCALAR = pl.BlockSpec(memory_space=pltpu.SMEM)


def across_lanes(left, right):
    return lax.dot_general(left, right, (((1,), (1,)), ((), ())), preferred_element_type=F32)


def attend_kernel(
    place_ref,
    slot_ref,
    query_weight,
    query_bias,
    key_weight,
    value_weight,
    value_bias,
    output_weight,
    query_ref,
    key_ref,
    value_ref,
    mixture_ref,
    logsum_ref,
    own_ref,
    sent_ref,
):
    slots = slot_ref[...]
    query_ref[...] = (dot(slots, query_weight[0]) + query_bias[...]).astype(BF16)
    key_ref[...] = dot(slots, key_weight[0]).astype(BF16)
    value_ref[...] = (dot(slots, value_weight[0]) + value_bias[...]).astype(BF16)
    count = slots.shape[0]
    valid = lax.broadcasted_iota(jnp.int32, (count, count), 0) < place_ref[0]
    for head in range(2):
        cut = slice(head * HEAD_DIM, (head + 1) * HEAD_DIM)
        scores = across_lanes(key_ref[:, cut], query_ref[:, cut] * HEAD_DIM**-0.5)
        scores = jnp.where(valid, scores, -1e30)
        highest = jnp.max(scores, axis=0, keepdims=True)
        raised = jnp.exp(scores - highest)
        totals = jnp.sum(raised, axis=0, keepdims=True)
        probs = (raised * (1.0 / totals)).astype(BF16)
        mixture_ref[:, cut] = t_dot_in_kernel(probs, value_ref[:, cut]).astype(BF16)
        logsum_ref[0, head : head + 1, :] = highest + jnp.log(totals)
    half = count // 2
    for side, share_ref in ((place_ref[1], own_ref), (1 - place_ref[1], sent_ref)):
        rows = mixture_ref[pl.ds(pl.multiple_of(side * half, half), half), :]
        share = dot(rows, output_weight[0])

        @pl.when(pl.program_id(0) == 0)
        def _():
            share_ref[...] = share

        @pl.when(pl.program_id(0) != 0)
        def _():
            share_ref[...] += share


def attend(layer, length, side, slots, query_weight, query_bias, key_weight, value_weight, value_bias, output_weight):
    count, width = slots.shape
    heads = query_weight.shape[2]
    pair = 2 * HEAD_DIM
    steps = heads // pair
    whole = pl.BlockSpec((count, width), lambda i: (0, 0))
    weight = pl.BlockSpec((1, width, pair), lambda i: (layer, 0, i))
    bias = pl.BlockSpec((1, pair), lambda i: (0, i))
    part = pl.BlockSpec((count, pair), lambda i: (0, i))
    part_shape = jax.ShapeDtypeStruct((count, heads), BF16)
    return pl.pallas_call(
        attend_kernel,
        grid=(steps,),
        in_specs=[SCALAR, whole, weight, bias, weight, weight, bias]
        + [pl.BlockSpec((1, pair, width), lambda i: (layer, i, 0))],
        out_specs=[part] * 4
        + [pl.BlockSpec((1, 2, count), lambda i: (i, 0, 0))]
        + [pl.BlockSpec((count // 2, width), lambda i: (0, 0))] * 2,
        out_shape=[part_shape] * 4
        + [jax.ShapeDtypeStruct((steps, 2, count), F32)]
        + [jax.ShapeDtypeStruct((count // 2, width), F32)] * 2,
        compiler_params=LIMIT,
        cost_estimate=pl.CostEstimate(
            flops=8 * count * width * heads + 4 * count * count * heads,
            bytes_accessed=8 * width * heads + 8 * count * width,
            transcendentals=count * count * heads // HEAD_DIM,
        ),
        name="attend",
    )(jnp.stack([length, side]), slots, query_weight, query_bias, key_weight, value_weight, value_bias, output_weight)


def attend_back_kernel(
    length_ref,
    query_ref,
    key_ref,
    value_ref,
    logsum_ref,
    grad_ref,
    query_weight,
    key_weight,
    value_weight,
    output_weight,
    query_low,
    key_low,
    value_low,
    share_ref,
    query_sum,
    value_sum,
):
    grads = across_lanes(grad_ref[...], output_weight[0]).astype(BF16)
    count = grads.shape[0]
    valid = lax.broadcasted_iota(jnp.int32, (count, count), 0) < length_ref[0]
    scale = HEAD_DIM**-0.5
    for head in range(2):
        cut = slice(head * HEAD_DIM, (head + 1) * HEAD_DIM)
        queries, keys, grad = query_ref[:, cut], key_ref[:, cut], grads[:, cut]
        scores = jnp.where(valid, across_lanes(keys, queries * scale), -1e30)
        probs = jnp.exp(scores - logsum_ref[0, head : head + 1, :])
        grad_probs = across_lanes(value_ref[:, cut], grad)
        inner = jnp.sum(probs * grad_probs, axis=0, keepdims=True)
        grad_scores = (probs * (grad_probs - inner)).astype(BF16)
        query_low[:, cut] = (t_dot_in_kernel(grad_scores, keys) * scale).astype(BF16)
        key_low[:, cut] = (dot(grad_scores, queries) * scale).astype(BF16)
        value_low[:, cut] = dot(probs.astype(BF16), grad).astype(BF16)
    query_sum[...] = jnp.sum(query_low[...].astype(F32), axis=0, keepdims=True)
    value_sum[...] = jnp.sum(value_low[...].astype(F32), axis=0, keepdims=True)
    share = across_lanes(query_low[...], query_weight[0])
    share += across_lanes(key_low[...], key_weight[0])
    share += across_lanes(value_low[...], value_weight[0])

    @pl.when(pl.program_id(0) == 0)
    def _():
        share_ref[...] = share

    @pl.when(pl.program_id(0) != 0)
    def _():
        share_ref[...] += share


def attend_back(layer, length, saved, attended_low, query_weight, key_weight, value_weight, output_weight):
    queries, keys, values, _, logsum = saved
    count, width = attended_low.shape
    heads = queries.shape[1]
    pair = 2 * HEAD_DIM
    steps = heads // pair
    whole = pl.BlockSpec((count, width), lambda i: (0, 0))
    weight = pl.BlockSpec((1, width, pair), lambda i: (layer, 0, i))
    part = pl.BlockSpec((count, pair), lambda i: (0, i))
    part_shape = jax.ShapeDtypeStruct((count, heads), BF16)
    sums = pl.BlockSpec((1, pair), lambda i: (0, i))
    sums_shape = jax.ShapeDtypeStruct((1, heads), F32)
    return pl.pallas_call(
        attend_back_kernel,
        grid=(steps,),
        in_specs=[SCALAR, part, part, part, pl.BlockSpec((1, 2, count), lambda i: (i, 0, 0)), whole]
        + [weight] * 3
        + [pl.BlockSpec((1, pair, width), lambda i: (layer, i, 0))],
        out_specs=[part] * 3 + [whole, sums, sums],
        out_shape=[part_shape] * 3 + [jax.ShapeDtypeStruct((count, width), F32), sums_shape, sums_shape],
        compiler_params=LIMIT,
        cost_estimate=pl.CostEstimate(
            flops=8 * count * width * heads + 10 * count * count * heads,
            bytes_accessed=8 * width * heads + 8 * count * width,
            transcendentals=count * count * heads // HEAD_DIM,
        ),
        name="attend_back",
    )(length.reshape(1), queries, keys, values, logsum, attended_low, query_weight, key_weight, value_weight, output_weight)


def pieces_kernel(place_ref, down_in, up_in, piece_ref):
    width = piece_ref.shape[2]

    @pl.when(place_ref[1] == 0)
    def _():
        piece_ref[0] = down_in[0].astype(F32)

    @pl.when(place_ref[1] != 0)
    def _():
        half = up_in.shape[1]
        piece_ref[0, :half, :] = up_in[0, :, :width].astype(F32)
        piece_ref[0, half:, :] = up_in[0, :, width:].astype(F32)


def weight_pieces(chip, core, down_weight, up_weight):
    layers, units, width = down_weight.shape
    rows = units // 16
    return pl.pallas_call(
        pieces_kernel,
        grid_spec=pltpu.PrefetchScalarGridSpec(
            num_scalar_prefetch=1,
            grid=(layers,),
            in_specs=[
                pl.BlockSpec((1, rows, width), lambda l, place: (l, place[0], 0)),
                pl.BlockSpec((1, rows // 2, units), lambda l, place: (l, place[0], 0)),
            ],
            out_specs=pl.BlockSpec((1, rows, width), lambda l, place: (l, 0, 0)),
        ),
        out_shape=jax.ShapeDtypeStruct((layers, rows, width), F32),
        compiler_params=LIMIT,
        name="weight_pieces",
    )(jnp.stack([chip, core]), down_weight, up_weight)


def feed_sums_kernel(received, part_ref, act_own, act_peer, pre_own, pre_peer, ffn_low, hidden_low, *refs):
    out_ref = refs[-1]
    width = ffn_low.shape[1]

    def write(own, peer, right):
        for k, left in enumerate((own, peer)):
            total = t_dot_in_kernel(left[...], right[...])
            cut = slice(k * width, (k + 1) * width)
            out_ref[:, cut] = total + refs[0][:, cut] if received else total

    @pl.when(part_ref[0] == 0)
    def _():
        write(act_own, act_peer, ffn_low)

    @pl.when(part_ref[0] != 0)
    def _():
        write(pre_own, pre_peer, hidden_low)


def feed_sums(part, actives, pre_lows, ffn_low, hidden_low, columns, received=None):
    slots, units = actives[0].shape
    width = ffn_low.shape[1]
    block = units // 4
    left = pl.BlockSpec((slots, block), lambda i: (0, i))
    right = pl.BlockSpec((slots, width), lambda i: (0, 0))
    rows = pl.BlockSpec((block, 2 * width), lambda i: (i, 0))
    more = [] if received is None else [received]
    return pl.pallas_call(
        lambda *refs: feed_sums_kernel(bool(more), *refs),
        grid=(4,),
        in_specs=[SCALAR] + [left] * 4 + [right] * 2 + [rows] * len(more),
        out_specs=rows,
        out_shape=jax.ShapeDtypeStruct((units, columns), F32),
        compiler_params=LIMIT,
        cost_estimate=pl.CostEstimate(
            flops=4 * slots * units * width, bytes_accessed=(8 + 8 * len(more)) * units * width, transcendentals=0
        ),
        name="feed_sums",
    )(part.reshape(1), *actives, *pre_lows, ffn_low, hidden_low, *more)


def attention_sums_kernel(received, part_ref, query_ref, key_ref, value_ref, mixture_ref, slot_ref, grad_ref, *refs):
    out_ref = refs[-1]
    second = lax.rem(pl.program_id(0), 2)

    def write(which, left, right):
        @pl.when(2 * part_ref[0] + second == which)
        def _():
            total = t_dot_in_kernel(left[...], right[...])
            out_ref[...] = total + refs[0][...] if received else total

    write(0, query_ref, slot_ref)
    write(1, key_ref, slot_ref)
    write(2, value_ref, slot_ref)
    write(3, mixture_ref, grad_ref)


def attention_sums(part, lows, mixture, rounded, attended_low, received=None, into=None, place=0):
    slots, heads = mixture.shape
    half = rounded.shape[1] // 2
    left = pl.BlockSpec((slots, heads), lambda i: (0, 0))
    right = pl.BlockSpec((slots, half), lambda i: (0, i // 2))
    rows = pl.BlockSpec((heads, half), lambda i: (i, 0))
    more = [item for item in (received, into) if item is not None]
    shape = (4 * heads, half) if into is None else into.shape
    return pl.pallas_call(
        lambda *refs: attention_sums_kernel(received is not None, *refs),
        grid=(4,),
        in_specs=[SCALAR] + [left] * 4 + [right] * 2 + [rows, pl.BlockSpec(memory_space=pl.ANY)][: len(more)],
        out_specs=pl.BlockSpec((heads, half), lambda i: (i, place)),
        out_shape=jax.ShapeDtypeStruct(shape, F32),
        input_output_aliases={} if into is None else {8: 0},
        compiler_params=LIMIT,
        cost_estimate=pl.CostEstimate(flops=8 * slots * heads * half, bytes_accessed=16 * heads * half, transcendentals=0),
        name="attention_sums",
    )(part.reshape(1), *lows, mixture, rounded, attended_low, *more)


def sort_kernel(units_rows, piece_ref, down_ref, up_ref, *output_refs):
    chips, _, _, width = piece_ref.shape
    rows = units_rows
    for i in range(chips):
        down_ref[i * rows : (i + 1) * rows, :] = piece_ref[i, 0, :rows].astype(BF16)
        up = piece_ref[i, 1, :rows].astype(BF16)
        half = rows // 2
        up_ref[i * half : (i + 1) * half, :width] = up[:half]
        up_ref[i * half : (i + 1) * half, width:] = up[half:]
    for output_ref in output_refs:
        output_ref[...] = piece_ref[:, 0, rows:].reshape(output_ref.shape).astype(BF16)


def sort_weights(gathered, units):
    chips, _, rows, width = gathered.shape
    step = 4
    heads = chips * rows - units
    more = 1 if heads else 0
    return pl.pallas_call(
        lambda *refs: sort_kernel(units // chips, *refs),
        grid=(chips // step,),
        in_specs=[pl.BlockSpec((step, 2, rows, width), lambda i: (i, 0, 0, 0))],
        out_specs=[
            pl.BlockSpec((units * step // chips, width), lambda i: (i, 0)),
            pl.BlockSpec((width * step // chips, units), lambda i: (i, 0)),
        ]
        + [pl.BlockSpec((heads * step // chips, width), lambda i: (i, 0))] * more,
        out_shape=[
            jax.ShapeDtypeStruct((units, width), BF16),
            jax.ShapeDtypeStruct((width, units), BF16),
        ]
        + [jax.ShapeDtypeStruct((heads, width), BF16)] * more,
        compiler_params=LIMIT,
        cost_estimate=pl.CostEstimate(flops=0, bytes_accessed=12 * units * width, transcendentals=0),
        name="sort_weights",
    )(gathered)


def rows_of(ref):
    chips, _, rows, columns = ref.shape
    return ref[...].reshape(chips * rows, columns)


def place_feed_kernel(down_in, up_in, down_ref, up_ref):
    down_ref[0] = rows_of(down_in)
    up_ref[0] = rows_of(up_in).T


def place_attention_kernel(query_in, key_in, value_in, output_in, query_ref, key_ref, value_ref, output_ref):
    query_ref[0] = rows_of(query_in).T
    key_ref[0] = rows_of(key_in).T
    value_ref[0] = rows_of(value_in).T
    output_ref[0] = rows_of(output_in)


def place_gradients(gathered, width):
    chips, _, rows, _ = gathered.shape
    step = 4
    units, block = chips * rows, step * rows
    half = width // 2

    def feed_in(core):
        return pl.BlockSpec((step, 1, rows, width), lambda l, i: (i, core, 0, 1 - l))

    def attention_in(core, which):
        return pl.BlockSpec((step, 1, rows, half), lambda l, i: (2 * i + which, core, 0, 5 - l))

    limit = pltpu.CompilerParams(vmem_limit_bytes=40 * 2**20)
    down, up = pl.pallas_call(
        place_feed_kernel,
        grid=(2, chips // step),
        in_specs=[feed_in(0), feed_in(1)],
        out_specs=[
            pl.BlockSpec((1, block, width), lambda l, i: (l, i, 0)),
            pl.BlockSpec((1, width, block), lambda l, i: (l, 0, i)),
        ],
        out_shape=[
            jax.ShapeDtypeStruct((2, units, width), F32),
            jax.ShapeDtypeStruct((2, width, units), F32),
        ],
        compiler_params=limit,
        name="place_feed",
    )(gathered, gathered)
    tall = pl.BlockSpec((1, half, block), lambda l, i: (l, i, 0))
    tall_shape = jax.ShapeDtypeStruct((2, width, block), F32)
    query, key, value, output = pl.pallas_call(
        place_attention_kernel,
        grid=(2, 2),
        in_specs=[attention_in(0, 0), attention_in(0, 1), attention_in(1, 0), attention_in(1, 1)],
        out_specs=[tall, tall, tall, pl.BlockSpec((1, block, half), lambda l, i: (l, 0, i))],
        out_shape=[tall_shape, tall_shape, tall_shape, jax.ShapeDtypeStruct((2, block, width), F32)],
        compiler_params=limit,
        name="place_attention",
    )(gathered, gathered, gathered, gathered)
    return query, key, value, output, up, down


def local(
    tokens,
    cotangent,
    lengths,
    repeats,
    query_weight,
    query_bias,
    key_weight,
    value_weight,
    value_bias,
    output_weight,
    output_bias,
    attn_gain,
    attn_shift,
    up_weight,
    up_bias,
    down_weight,
    down_bias,
    ffn_gain,
    ffn_shift,
):
    length = lengths[0]
    side = lax.axis_index("h")
    core = lax.axis_index("c")
    chip = lax.axis_index("y") * 4 + lax.axis_index("x")
    first_core = core == 0
    slots, width = tokens.shape
    half_slots = slots // 2
    units = up_weight.shape[2]
    columns = query_weight.shape[2]

    rows_down = units // 16
    pieces = weight_pieces(chip, core, down_weight, up_weight)
    pieces2 = jnp.concatenate([pieces[1], piece(output_weight[1], chip, columns // 16).astype(F32)])
    pieces1, pieces2 = together(swap(pieces[0], "h"), pieces2)
    gathered1 = lax.all_gather(pieces1, PLANE + ("c",))
    pieces2 = swap(pieces2, "h")
    peer_up_bias = swap(up_bias.astype(F32), "h")

    def own_slots(values):
        return piece(values, side, half_slots)

    def feed_weights_back(saved, pre_lows, ffn_low, columns):
        actives, hidden_low = saved[3], saved[4]
        received = swap(feed_sums(1 - core, actives, pre_lows, ffn_low, hidden_low, 2 * width), "c")
        return feed_sums(core, actives, pre_lows, ffn_low, hidden_low, columns, received)

    def attention_forward(layer, rounded):
        *attention, share, sent = attend(
            layer,
            length,
            side,
            rounded,
            query_weight,
            query_bias[layer].astype(F32)[None],
            key_weight,
            value_weight,
            value_bias[layer].astype(F32)[None],
            output_weight,
        )
        return attention, share, sent

    def attention_back(layer, saved, grad_one_sent, received):
        grad_one = 2.0 * in_order(side, grad_one_sent, received)
        attended_low = grad_one.astype(BF16)
        *lows, share, query_sum, value_sum = attend_back(
            layer, length, saved, attended_low, query_weight, key_weight, value_weight, output_weight
        )
        small = [jnp.concatenate([query_sum[0], value_sum[0]]), column_sum(attended_low)]
        return grad_one, lows, attended_low, share, small

    def feed_back(layer, gradient, saved):
        scaled_two, inverse_two, pres, actives, hidden_low, scaled_one, inverse_one = saved
        grad_two = normalize_back(gradient, ffn_gain[layer], scaled_two, inverse_two)
        ffn_low = grad_two.astype(BF16)
        downs, ups = (down_weight[layer], peer_down[layer]), (up_weight[layer], peer_up[layer])
        pre_lows = [
            (dot_t(ffn_low, down) * gelu_slope(pre)).astype(BF16) for down, pre in zip(downs, pres, strict=True)
        ]
        grad_hidden = grad_two + dot_t(pre_lows[0], ups[0]) + dot_t(pre_lows[1], ups[1])
        grad_one = normalize_back(grad_hidden, attn_gain[layer], scaled_one, inverse_one)
        shared = [
            jnp.sum(grad_hidden * scaled_one, axis=0),
            jnp.sum(grad_hidden, axis=0),
            column_sum(ffn_low),
            jnp.sum(gradient * scaled_two, axis=0),
            jnp.sum(gradient, axis=0),
        ]
        biases = [column_sum(item).reshape(-1, width) for item in pre_lows]
        return grad_one, ffn_low, pre_lows, shared, biases

    def layer_forward(layer, x_own, attended, peers):
        attended = attended + output_bias[layer]
        hidden, scaled, inverse = normalize(x_own + attended, attn_gain[layer], attn_shift[layer])
        hidden_low = hidden.astype(BF16)
        pre = dot(hidden_low, up_weight[layer]) + up_bias[layer]
        active = gelu(pre).astype(BF16)
        ffn_out = dot(active, down_weight[layer])
        peer_down, peer_up = peers
        pre_peer = dot(hidden_low, peer_up) + peer_up_bias[layer]
        active_peer = gelu(pre_peer).astype(BF16)
        ffn_out = ffn_out + dot(active_peer, peer_down) + down_bias[layer]
        out, scaled_two, inverse_two = normalize(hidden + ffn_out, ffn_gain[layer], ffn_shift[layer])
        saved = (scaled_two, inverse_two, (pre, pre_peer), (active, active_peer), hidden_low, scaled, inverse)
        return out, saved

    att1, share, sent = attention_forward(0, tokens)
    pieces2, sent = together(pieces2, sent)
    peers1 = sort_weights(gathered1.reshape(16, 2, rows_down, width), units)
    gathered2 = lax.all_gather(pieces2, PLANE + ("c",))
    x2_own, saved1 = layer_forward(0, own_slots(tokens).astype(F32), share + swap(sent, "h"), peers1)
    sent = 0.5 * x2_own
    x2_low = (2.0 * in_order(side, sent, swap(sent, "h"))).astype(BF16)
    att2, share, _ = attention_forward(1, x2_low)
    received = swap(0.5 * piece(att2[3], 1 - side, half_slots).astype(F32), "h")
    received, *peers2 = together(
        received, *sort_weights(gathered2.reshape(16, 2, rows_down + columns // 16, width), units)
    )
    attended = share + dot((2.0 * received).astype(BF16), peers2[2])
    _, saved2 = layer_forward(1, x2_own, attended, peers2[:2])
    scaled_last = saved2[0]
    mixture = att2[3]
    peer_down, peer_up = (peers1[0], peers2[0]), (peers1[1], peers2[1])

    places = side * half_slots + jnp.arange(half_slots)
    weighting = jnp.where(places < length, repeats[0], 0).astype(F32)[:, None]
    gradient2 = own_slots(cotangent).astype(F32) * weighting
    grad_one_own, ffn_low, pre_lows, shared2, biases2 = feed_back(1, gradient2, saved2)
    sent = 0.5 * grad_one_own
    received = swap(sent, "h")
    feed2 = feed_weights_back(saved2, pre_lows, ffn_low, 2 * width)
    feed2, received = together(feed2, received)
    feed2 = lax.psum_scatter(feed2, PLANE, tiled=True)
    _, lows2, attended_low2, share, small_att2 = attention_back(1, att2, sent, received)
    received = swap(piece(share, 1 - side, half_slots), "h")
    attn2_received = swap(attention_sums(1 - core, lows2, mixture, x2_low, attended_low2), "c")
    gradient1 = grad_one_own + own_slots(share) + received

    grad_one_own1, ffn_low, pre_lows, shared1, biases1 = feed_back(0, gradient1, saved1)
    sent = 0.5 * grad_one_own1
    received = swap(sent, "h")
    rest = feed_weights_back(saved1, pre_lows, ffn_low, 2 * width + columns)
    rest = attention_sums(core, lows2, mixture, x2_low, attended_low2, attn2_received, rest, 2 * width // columns)
    rest, received, feed2 = together(rest, received, feed2)
    rest = lax.psum_scatter(rest, PLANE, tiled=True)
    grad_one1, lows1, attended_low1, share, small_att1 = attention_back(0, att1, sent, received)
    attn1_received = swap(attention_sums(1 - core, lows1, att1[3], tokens, attended_low1), "c")
    attn1 = plane_sum(attention_sums(core, lows1, att1[3], tokens, attended_low1, attn1_received))

    def across(own, peer):
        diagonal = lax.ppermute(peer, ("zl", "h"), ((0, 3), (3, 0), (1, 2), (2, 1)))
        own = own + swap(own, "zl")
        peer = swap(peer, "h") + diagonal
        return jnp.concatenate([own[:, :width] + peer, own[:, width:]], axis=1)

    feed2 = across(feed2[:, :width], feed2[:, width:])
    attn1 = attn1 + swap(attn1, "zl")
    feed2, attn1, rest = together(feed2, attn1, rest)
    rest = across(jnp.concatenate([rest[:, :width], rest[:, 2 * width :]], axis=1), rest[:, width : 2 * width])
    own = jnp.concatenate([feed2, rest, attn1], axis=1)
    gathered = lax.all_gather(own, PLANE + ("c",)).reshape(16, 2, *own.shape)
    grad_query, grad_key, grad_value, grad_output, grad_up, grad_down = place_gradients(gathered, width)

    token_grad = grad_one1 + pair_sum(share)
    scaled_last, token_grad = together(scaled_last, token_grad)
    scaled_all = in_order(side, scaled_last, swap(scaled_last, "h"))
    block_output = (scaled_all * ffn_gain[1] + ffn_shift[1]).astype(BF16)
    shared = jnp.stack(shared1 + shared2)
    mine = jnp.concatenate([shared, biases1[0], biases2[0]])
    mine = mine + swap(jnp.concatenate([shared, biases1[1], biases2[1]]), "h")
    small = jnp.concatenate([mine, jnp.stack(small_att1 + small_att2)])
    small, block_output = together(small, block_output)
    small = small + swap(small, "c")
    for axis, pairs in LINKS:
        small = small + lax.ppermute(small, axis, pairs)
    small = small + swap(small, "zl")
    bias_rows = units // width
    shared = small[:10].reshape(2, 5, width)
    grad_up_bias = small[10 : 10 + 2 * bias_rows].reshape(2, units)
    attention = small[10 + 2 * bias_rows :].reshape(2, 2, width)

    return (
        block_output,
        token_grad,
        grad_query,
        attention[:, 0, :columns],
        grad_key,
        grad_value,
        attention[:, 0, columns:],
        grad_output,
        attention[:, 1],
        shared[:, 0],
        shared[:, 1],
        grad_up,
        grad_up_bias,
        grad_down,
        shared[:, 2],
        shared[:, 3],
        shared[:, 4],
    )


def solution(mesh):
    fine = Mesh(mesh.devices.reshape(4, 2, 4, 2, 2), ("y", "zl", "x", "c", "h"))
    rows = ("y", "zl", "x", "c")
    in_specs = (
        P(rows, None),
        P(rows, None),
        P(rows),
        P(rows),
        P(None, None, "h"),
        P(None, "h"),
        P(None, None, "h"),
        P(None, None, "h"),
        P(None, "h"),
        P(None, "h", None),
        P(),
        P(),
        P(),
        P(None, None, "h"),
        P(None, "h"),
        P(None, "h", None),
        P(),
        P(),
        P(),
    )
    out_specs = (
        P(rows, None),
        P(rows, None),
        P(None, None, "h"),
        P(None, "h"),
        P(None, None, "h"),
        P(None, None, "h"),
        P(None, "h"),
        P(None, "h", None),
        P(),
        P(),
        P(),
        P(None, None, "h"),
        P(None, "h"),
        P(None, "h", None),
        P(),
        P(),
        P(),
    )
    return jax.shard_map(local, mesh=fine, in_specs=in_specs, out_specs=out_specs, check_vma=False)
```

```python
import jax
import jax.numpy as jnp
from jax import lax
from jax.experimental import pallas as pl
from jax.experimental.pallas import tpu as pltpu
from jax.sharding import Mesh, PartitionSpec as P

HEAD_DIM = 64
EPS = 1e-12
F32 = jnp.float32
BF16 = jnp.bfloat16
SWAP = ((0, 1), (1, 0))
EDGE0 = ((0, 1), (1, 0), (2, 3), (3, 2))
EDGE1 = ((1, 2), (2, 1), (3, 0), (0, 3))
LINKS = (("x", EDGE0), ("x", EDGE1), ("y", EDGE0), ("y", EDGE1))
PLANE = ("y", "x")


def normalize(summed, gain, shift):
    center = summed - jnp.mean(summed, axis=-1, keepdims=True)
    inverse = lax.rsqrt(jnp.mean(center * center, axis=-1, keepdims=True) + EPS)
    scaled = center * inverse
    return (scaled * gain + shift, scaled, inverse)


def normalize_back(gradient, gain, scaled, inverse):
    gained = gradient * gain
    return inverse * (
        gained
        - jnp.mean(gained, axis=-1, keepdims=True)
        - scaled * jnp.mean(gained * scaled, axis=-1, keepdims=True)
    )


def normal_cdf(values):
    return 0.5 * (1.0 + lax.erf(values * (0.5**0.5)))


def gelu(values):
    return values * normal_cdf(values)


def gelu_slope(values):
    density = jnp.exp(-0.5 * values * values) * 0.3989422804014327
    return normal_cdf(values) + values * density


def dot(left, right):
    return jnp.dot(left, right, preferred_element_type=F32)


def dot_t(left, right):
    return jnp.einsum("sd,fd->sf", left, right, preferred_element_type=F32)


def t_dot(left, right):
    return jnp.einsum("sf,sd->fd", left, right, preferred_element_type=F32)


def column_sum(values):
    return jnp.sum(values.astype(F32), axis=0)


def swap(values, axis):
    return lax.ppermute(values, axis, SWAP)


def pair_sum(values):
    return values + swap(values, "h")


def piece(values, index, size):
    return lax.dynamic_slice_in_dim(values, index * size, size, 0)


def ring_parts(values, axis, dim):
    place = lax.axis_index(axis)
    kept = lax.dynamic_index_in_dim(values, place, dim, keepdims=False)
    received = []
    for distance in (1, 3, 2):
        sent = lax.dynamic_index_in_dim(values, lax.rem(place + distance, 4), dim, keepdims=False)
        pairs = [(start, (start + distance) % 4) for start in range(4)]
        received.append(lax.ppermute(sent, axis, pairs))
    return [kept, *received]


def plane_sum(values):
    rows, columns = values.shape
    values = values.reshape(4, 4, 2, rows // 32, columns)
    x_first = ring_parts(values[:, :, 0], "x", 1)
    y_first = ring_parts(values[:, :, 1], "y", 0)
    parts = together(*x_first, *y_first)
    x_first = ring_parts(sum(parts[1:4], parts[0]), "y", 0)
    y_first = ring_parts(sum(parts[5:], parts[4]), "x", 0)
    parts = together(*x_first, *y_first)
    return jnp.concatenate([sum(parts[1:4], parts[0]), sum(parts[5:], parts[4])])


def in_order(side, mine, other):
    return jnp.concatenate([jnp.where(side == 0, mine, other), jnp.where(side == 0, other, mine)])


def together(*values):
    return lax.optimization_barrier(values)


def t_dot_in_kernel(left, right):
    return lax.dot_general(left, right, (((0,), (0,)), ((), ())), preferred_element_type=F32)


LIMIT = pltpu.CompilerParams(vmem_limit_bytes=48 * 2**20)
SCALAR = pl.BlockSpec(memory_space=pltpu.SMEM)


def across_lanes(left, right):
    return lax.dot_general(left, right, (((1,), (1,)), ((), ())), preferred_element_type=F32)


def attend_kernel(
    sends_mixture,
    place_ref,
    slot_ref,
    query_weight,
    query_bias,
    key_weight,
    value_weight,
    value_bias,
    output_weight,
    query_ref,
    key_ref,
    value_ref,
    mixture_ref,
    logsum_ref,
    own_ref,
    sent_ref,
):
    slots = slot_ref[...]
    query_ref[...] = (dot(slots, query_weight[0]) + query_bias[...]).astype(BF16)
    key_ref[...] = dot(slots, key_weight[0]).astype(BF16)
    value_ref[...] = (dot(slots, value_weight[0]) + value_bias[...]).astype(BF16)
    count = slots.shape[0]
    valid = lax.broadcasted_iota(jnp.int32, (count, count), 0) < place_ref[0]
    for head in range(2):
        cut = slice(head * HEAD_DIM, (head + 1) * HEAD_DIM)
        scores = across_lanes(key_ref[:, cut], query_ref[:, cut] * HEAD_DIM**-0.5)
        scores = jnp.where(valid, scores, -1e30)
        highest = jnp.max(scores, axis=0, keepdims=True)
        raised = jnp.exp(scores - highest)
        totals = jnp.sum(raised, axis=0, keepdims=True)
        probs = (raised * (1.0 / totals)).astype(BF16)
        mixture_ref[:, cut] = t_dot_in_kernel(probs, value_ref[:, cut]).astype(BF16)
        logsum_ref[0, head : head + 1, :] = highest + jnp.log(totals)
    half = count // 2

    def rows_at(side):
        return mixture_ref[pl.ds(pl.multiple_of(side * half, half), half), :]

    parts = [(place_ref[1], own_ref)]
    if sends_mixture:
        sent_ref[...] = 0.5 * rows_at(1 - place_ref[1]).astype(F32)
    else:
        parts.append((1 - place_ref[1], sent_ref))
    for side, share_ref in parts:
        share = dot(rows_at(side), output_weight[0])

        @pl.when(pl.program_id(0) == 0)
        def _():
            share_ref[...] = share

        @pl.when(pl.program_id(0) != 0)
        def _():
            share_ref[...] += share


def attend(
    layer, length, side, slots, query_weight, query_bias, key_weight, value_weight, value_bias, output_weight, sends_mixture
):
    count, width = slots.shape
    heads = query_weight.shape[2]
    pair = 2 * HEAD_DIM
    steps = heads // pair
    whole = pl.BlockSpec((count, width), lambda i: (0, 0))
    weight = pl.BlockSpec((1, width, pair), lambda i: (layer, 0, i))
    bias = pl.BlockSpec((1, pair), lambda i: (0, i))
    part = pl.BlockSpec((count, pair), lambda i: (0, i))
    part_shape = jax.ShapeDtypeStruct((count, heads), BF16)
    shared = pl.BlockSpec((count // 2, width), lambda i: (0, 0))
    sent, sent_width = shared, width
    if sends_mixture:
        sent, sent_width = pl.BlockSpec((count // 2, pair), lambda i: (0, i)), heads
    return pl.pallas_call(
        lambda *refs: attend_kernel(sends_mixture, *refs),
        grid=(steps,),
        in_specs=[SCALAR, whole, weight, bias, weight, weight, bias]
        + [pl.BlockSpec((1, pair, width), lambda i: (layer, i, 0))],
        out_specs=[part] * 4
        + [pl.BlockSpec((1, 2, count), lambda i: (i, 0, 0))]
        + [shared, sent],
        out_shape=[part_shape] * 4
        + [jax.ShapeDtypeStruct((steps, 2, count), F32)]
        + [jax.ShapeDtypeStruct((count // 2, width), F32), jax.ShapeDtypeStruct((count // 2, sent_width), F32)],
        compiler_params=LIMIT,
        cost_estimate=pl.CostEstimate(
            flops=8 * count * width * heads + 4 * count * count * heads,
            bytes_accessed=8 * width * heads + 8 * count * width,
            transcendentals=count * count * heads // HEAD_DIM,
        ),
        name="attend",
    )(jnp.stack([length, side]), slots, query_weight, query_bias, key_weight, value_weight, value_bias, output_weight)


def attend_back_kernel(
    length_ref,
    query_ref,
    key_ref,
    value_ref,
    logsum_ref,
    grad_ref,
    query_weight,
    key_weight,
    value_weight,
    output_weight,
    query_low,
    key_low,
    value_low,
    share_ref,
    query_sum,
    value_sum,
):
    grads = across_lanes(grad_ref[...], output_weight[0]).astype(BF16)
    count = grads.shape[0]
    valid = lax.broadcasted_iota(jnp.int32, (count, count), 0) < length_ref[0]
    scale = HEAD_DIM**-0.5
    for head in range(2):
        cut = slice(head * HEAD_DIM, (head + 1) * HEAD_DIM)
        queries, keys, grad = query_ref[:, cut], key_ref[:, cut], grads[:, cut]
        scores = jnp.where(valid, across_lanes(keys, queries * scale), -1e30)
        probs = jnp.exp(scores - logsum_ref[0, head : head + 1, :])
        grad_probs = across_lanes(value_ref[:, cut], grad)
        inner = jnp.sum(probs * grad_probs, axis=0, keepdims=True)
        grad_scores = (probs * (grad_probs - inner)).astype(BF16)
        query_low[:, cut] = (t_dot_in_kernel(grad_scores, keys) * scale).astype(BF16)
        key_low[:, cut] = (dot(grad_scores, queries) * scale).astype(BF16)
        value_low[:, cut] = dot(probs.astype(BF16), grad).astype(BF16)
    query_sum[...] = jnp.sum(query_low[...].astype(F32), axis=0, keepdims=True)
    value_sum[...] = jnp.sum(value_low[...].astype(F32), axis=0, keepdims=True)
    share = across_lanes(query_low[...], query_weight[0])
    share += across_lanes(key_low[...], key_weight[0])
    share += across_lanes(value_low[...], value_weight[0])

    @pl.when(pl.program_id(0) == 0)
    def _():
        share_ref[...] = share

    @pl.when(pl.program_id(0) != 0)
    def _():
        share_ref[...] += share


def attend_back(layer, length, saved, attended_low, query_weight, key_weight, value_weight, output_weight):
    queries, keys, values, _, logsum = saved
    count, width = attended_low.shape
    heads = queries.shape[1]
    pair = 2 * HEAD_DIM
    steps = heads // pair
    whole = pl.BlockSpec((count, width), lambda i: (0, 0))
    weight = pl.BlockSpec((1, width, pair), lambda i: (layer, 0, i))
    part = pl.BlockSpec((count, pair), lambda i: (0, i))
    part_shape = jax.ShapeDtypeStruct((count, heads), BF16)
    sums = pl.BlockSpec((1, pair), lambda i: (0, i))
    sums_shape = jax.ShapeDtypeStruct((1, heads), F32)
    return pl.pallas_call(
        attend_back_kernel,
        grid=(steps,),
        in_specs=[SCALAR, part, part, part, pl.BlockSpec((1, 2, count), lambda i: (i, 0, 0)), whole]
        + [weight] * 3
        + [pl.BlockSpec((1, pair, width), lambda i: (layer, i, 0))],
        out_specs=[part] * 3 + [whole, sums, sums],
        out_shape=[part_shape] * 3 + [jax.ShapeDtypeStruct((count, width), F32), sums_shape, sums_shape],
        compiler_params=LIMIT,
        cost_estimate=pl.CostEstimate(
            flops=8 * count * width * heads + 10 * count * count * heads,
            bytes_accessed=8 * width * heads + 8 * count * width,
            transcendentals=count * count * heads // HEAD_DIM,
        ),
        name="attend_back",
    )(length.reshape(1), queries, keys, values, logsum, attended_low, query_weight, key_weight, value_weight, output_weight)


def pieces_kernel(place_ref, down_in, up_in, piece_ref):
    width = piece_ref.shape[2]

    @pl.when(place_ref[1] == 0)
    def _():
        piece_ref[0] = down_in[0].astype(F32)

    @pl.when(place_ref[1] != 0)
    def _():
        half = up_in.shape[1]
        piece_ref[0, :half, :] = up_in[0, :, :width].astype(F32)
        piece_ref[0, half:, :] = up_in[0, :, width:].astype(F32)


def weight_pieces(chip, core, down_weight, up_weight):
    layers, units, width = down_weight.shape
    rows = units // 16
    return pl.pallas_call(
        pieces_kernel,
        grid_spec=pltpu.PrefetchScalarGridSpec(
            num_scalar_prefetch=1,
            grid=(layers,),
            in_specs=[
                pl.BlockSpec((1, rows, width), lambda l, place: (l, place[0], 0)),
                pl.BlockSpec((1, rows // 2, units), lambda l, place: (l, place[0], 0)),
            ],
            out_specs=pl.BlockSpec((1, rows, width), lambda l, place: (l, 0, 0)),
        ),
        out_shape=jax.ShapeDtypeStruct((layers, rows, width), F32),
        compiler_params=LIMIT,
        name="weight_pieces",
    )(jnp.stack([chip, core]), down_weight, up_weight)


def feed_sums_kernel(received, part_ref, act_own, act_peer, pre_own, pre_peer, ffn_low, hidden_low, *refs):
    out_ref = refs[-1]
    width = ffn_low.shape[1]

    def write(own, peer, right):
        for k, left in enumerate((own, peer)):
            total = t_dot_in_kernel(left[...], right[...])
            cut = slice(k * width, (k + 1) * width)
            out_ref[:, cut] = total + refs[0][:, cut] if received else total

    @pl.when(part_ref[0] == 0)
    def _():
        write(act_own, act_peer, ffn_low)

    @pl.when(part_ref[0] != 0)
    def _():
        write(pre_own, pre_peer, hidden_low)


def feed_sums(part, actives, pre_lows, ffn_low, hidden_low, columns, received=None):
    slots, units = actives[0].shape
    width = ffn_low.shape[1]
    block = units // 4
    left = pl.BlockSpec((slots, block), lambda i: (0, i))
    right = pl.BlockSpec((slots, width), lambda i: (0, 0))
    rows = pl.BlockSpec((block, 2 * width), lambda i: (i, 0))
    more = [] if received is None else [received]
    return pl.pallas_call(
        lambda *refs: feed_sums_kernel(bool(more), *refs),
        grid=(4,),
        in_specs=[SCALAR] + [left] * 4 + [right] * 2 + [rows] * len(more),
        out_specs=rows,
        out_shape=jax.ShapeDtypeStruct((units, columns), F32),
        compiler_params=LIMIT,
        cost_estimate=pl.CostEstimate(
            flops=4 * slots * units * width, bytes_accessed=(8 + 8 * len(more)) * units * width, transcendentals=0
        ),
        name="feed_sums",
    )(part.reshape(1), *actives, *pre_lows, ffn_low, hidden_low, *more)


def attention_sums_kernel(received, part_ref, query_ref, key_ref, value_ref, mixture_ref, slot_ref, grad_ref, *refs):
    out_ref = refs[-1]
    second = lax.rem(pl.program_id(0), 2)

    def write(which, left, right):
        @pl.when(2 * part_ref[0] + second == which)
        def _():
            total = t_dot_in_kernel(left[...], right[...])
            out_ref[...] = total + refs[0][...] if received else total

    write(0, query_ref, slot_ref)
    write(1, key_ref, slot_ref)
    write(2, value_ref, slot_ref)
    write(3, mixture_ref, grad_ref)


def attention_sums(part, lows, mixture, rounded, attended_low, received=None, into=None, place=0):
    slots, heads = mixture.shape
    half = rounded.shape[1] // 2
    left = pl.BlockSpec((slots, heads), lambda i: (0, 0))
    right = pl.BlockSpec((slots, half), lambda i: (0, i // 2))
    rows = pl.BlockSpec((heads, half), lambda i: (i, 0))
    more = [item for item in (received, into) if item is not None]
    shape = (4 * heads, half) if into is None else into.shape
    return pl.pallas_call(
        lambda *refs: attention_sums_kernel(received is not None, *refs),
        grid=(4,),
        in_specs=[SCALAR] + [left] * 4 + [right] * 2 + [rows, pl.BlockSpec(memory_space=pl.ANY)][: len(more)],
        out_specs=pl.BlockSpec((heads, half), lambda i: (i, place)),
        out_shape=jax.ShapeDtypeStruct(shape, F32),
        input_output_aliases={} if into is None else {8: 0},
        compiler_params=LIMIT,
        cost_estimate=pl.CostEstimate(flops=8 * slots * heads * half, bytes_accessed=16 * heads * half, transcendentals=0),
        name="attention_sums",
    )(part.reshape(1), *lows, mixture, rounded, attended_low, *more)


def sort_kernel(piece_ref, down_ref, up_ref):
    chips, _, rows, width = piece_ref.shape
    for i in range(chips):
        down_ref[i * rows : (i + 1) * rows, :] = piece_ref[i, 0].astype(BF16)
        up = piece_ref[i, 1].astype(BF16)
        half = rows // 2
        up_ref[i * half : (i + 1) * half, :width] = up[:half]
        up_ref[i * half : (i + 1) * half, width:] = up[half:]


def sort_weights(gathered):
    chips, _, rows, width = gathered.shape
    step = 2
    units = chips * rows
    return pl.pallas_call(
        sort_kernel,
        grid=(chips // step,),
        in_specs=[pl.BlockSpec((step, 2, rows, width), lambda i: (i, 0, 0, 0))],
        out_specs=[
            pl.BlockSpec((step * rows, width), lambda i: (i, 0)),
            pl.BlockSpec((step * rows // 2, units), lambda i: (i, 0)),
        ],
        out_shape=[
            jax.ShapeDtypeStruct((units, width), BF16),
            jax.ShapeDtypeStruct((width, units), BF16),
        ],
        compiler_params=LIMIT,
        cost_estimate=pl.CostEstimate(flops=0, bytes_accessed=12 * units * width, transcendentals=0),
        name="sort_weights",
    )(gathered)


def rows_of(ref):
    chips, _, rows, columns = ref.shape
    return ref[...].reshape(chips * rows, columns)


def place_feed_kernel(down_in, up_in, down_ref, up_ref):
    down_ref[0] = rows_of(down_in)
    up_ref[0] = rows_of(up_in).T


def place_attention_kernel(query_in, key_in, value_in, output_in, query_ref, key_ref, value_ref, output_ref):
    query_ref[0] = rows_of(query_in).T
    key_ref[0] = rows_of(key_in).T
    value_ref[0] = rows_of(value_in).T
    output_ref[0] = rows_of(output_in)


def place_gradients(gathered, width):
    chips, _, rows, _ = gathered.shape
    step = 4
    units, block = chips * rows, step * rows
    half = width // 2

    def feed_in(core):
        return pl.BlockSpec((step, 1, rows, width), lambda l, i: (i, core, 0, 1 - l))

    def attention_in(core, which):
        return pl.BlockSpec((step, 1, rows, half), lambda l, i: (2 * i + which, core, 0, 5 - l))

    limit = pltpu.CompilerParams(vmem_limit_bytes=40 * 2**20)
    down, up = pl.pallas_call(
        place_feed_kernel,
        grid=(2, chips // step),
        in_specs=[feed_in(0), feed_in(1)],
        out_specs=[
            pl.BlockSpec((1, block, width), lambda l, i: (l, i, 0)),
            pl.BlockSpec((1, width, block), lambda l, i: (l, 0, i)),
        ],
        out_shape=[
            jax.ShapeDtypeStruct((2, units, width), F32),
            jax.ShapeDtypeStruct((2, width, units), F32),
        ],
        compiler_params=limit,
        name="place_feed",
    )(gathered, gathered)
    tall = pl.BlockSpec((1, half, block), lambda l, i: (l, i, 0))
    tall_shape = jax.ShapeDtypeStruct((2, width, block), F32)
    query, key, value, output = pl.pallas_call(
        place_attention_kernel,
        grid=(2, 2),
        in_specs=[attention_in(0, 0), attention_in(0, 1), attention_in(1, 0), attention_in(1, 1)],
        out_specs=[tall, tall, tall, pl.BlockSpec((1, block, half), lambda l, i: (l, 0, i))],
        out_shape=[tall_shape, tall_shape, tall_shape, jax.ShapeDtypeStruct((2, block, width), F32)],
        compiler_params=limit,
        name="place_attention",
    )(gathered, gathered, gathered, gathered)
    return query, key, value, output, up, down


def local(
    tokens,
    cotangent,
    lengths,
    repeats,
    query_weight,
    query_bias,
    key_weight,
    value_weight,
    value_bias,
    output_weight,
    output_bias,
    attn_gain,
    attn_shift,
    up_weight,
    up_bias,
    down_weight,
    down_bias,
    ffn_gain,
    ffn_shift,
):
    length = lengths[0]
    side = lax.axis_index("h")
    core = lax.axis_index("c")
    chip = lax.axis_index("y") * 4 + lax.axis_index("x")
    first_core = core == 0
    slots, width = tokens.shape
    half_slots = slots // 2
    units = up_weight.shape[2]
    columns = query_weight.shape[2]

    rows_down = units // 16
    pieces = weight_pieces(chip, core, down_weight, up_weight)
    pieces1, pieces2 = together(swap(pieces[0], "h"), pieces[1])
    gathered1 = lax.all_gather(pieces1, PLANE + ("c",))
    pieces2 = swap(pieces2, "h")
    peer_up_bias = swap(up_bias.astype(F32), "h")

    def own_slots(values):
        return piece(values, side, half_slots)

    def feed_weights_back(saved, pre_lows, ffn_low, columns):
        actives, hidden_low = saved[3], saved[4]
        received = swap(feed_sums(1 - core, actives, pre_lows, ffn_low, hidden_low, 2 * width), "c")
        return feed_sums(core, actives, pre_lows, ffn_low, hidden_low, columns, received)

    def attention_forward(layer, rounded):
        *attention, share, sent = attend(
            layer,
            length,
            side,
            rounded,
            query_weight,
            query_bias[layer].astype(F32)[None],
            key_weight,
            value_weight,
            value_bias[layer].astype(F32)[None],
            output_weight,
            layer == 1,
        )
        return attention, share, sent

    def attention_back(layer, saved, grad_one_sent, received):
        grad_one = 2.0 * in_order(side, grad_one_sent, received)
        attended_low = grad_one.astype(BF16)
        *lows, share, query_sum, value_sum = attend_back(
            layer, length, saved, attended_low, query_weight, key_weight, value_weight, output_weight
        )
        small = [jnp.concatenate([query_sum[0], value_sum[0]]), column_sum(attended_low)]
        return grad_one, lows, attended_low, share, small

    def feed_back(layer, gradient, saved):
        scaled_two, inverse_two, pres, actives, hidden_low, scaled_one, inverse_one = saved
        grad_two = normalize_back(gradient, ffn_gain[layer], scaled_two, inverse_two)
        ffn_low = grad_two.astype(BF16)
        downs, ups = (down_weight[layer], peer_down[layer]), (up_weight[layer], peer_up[layer])
        pre_lows = [
            (dot_t(ffn_low, down) * gelu_slope(pre)).astype(BF16) for down, pre in zip(downs, pres, strict=True)
        ]
        grad_hidden = grad_two + dot_t(pre_lows[0], ups[0]) + dot_t(pre_lows[1], ups[1])
        grad_one = normalize_back(grad_hidden, attn_gain[layer], scaled_one, inverse_one)
        shared = [
            jnp.sum(grad_hidden * scaled_one, axis=0),
            jnp.sum(grad_hidden, axis=0),
            column_sum(ffn_low),
            jnp.sum(gradient * scaled_two, axis=0),
            jnp.sum(gradient, axis=0),
        ]
        biases = [column_sum(item).reshape(-1, width) for item in pre_lows]
        return grad_one, ffn_low, pre_lows, shared, biases

    def layer_forward(layer, x_own, attended, peers):
        attended = attended + output_bias[layer]
        hidden, scaled, inverse = normalize(x_own + attended, attn_gain[layer], attn_shift[layer])
        hidden_low = hidden.astype(BF16)
        pre = dot(hidden_low, up_weight[layer]) + up_bias[layer]
        active = gelu(pre).astype(BF16)
        ffn_out = dot(active, down_weight[layer])
        peer_down, peer_up = peers
        pre_peer = dot(hidden_low, peer_up) + peer_up_bias[layer]
        active_peer = gelu(pre_peer).astype(BF16)
        ffn_out = ffn_out + dot(active_peer, peer_down) + down_bias[layer]
        out, scaled_two, inverse_two = normalize(hidden + ffn_out, ffn_gain[layer], ffn_shift[layer])
        saved = (scaled_two, inverse_two, (pre, pre_peer), (active, active_peer), hidden_low, scaled, inverse)
        return out, saved

    att1, share, sent = attention_forward(0, tokens)
    pieces2, sent = together(pieces2, sent)
    peers1 = sort_weights(gathered1.reshape(16, 2, rows_down, width))
    gathered2 = lax.all_gather(pieces2, PLANE + ("c",))
    received, peer_output = together(swap(sent, "h"), 0.5 * output_weight[1].astype(F32))
    peer_output = swap(peer_output, "h")
    x2_own, saved1 = layer_forward(0, own_slots(tokens).astype(F32), share + received, peers1)
    sent, peer_output = together(0.5 * x2_own, peer_output)
    peer_output = (2.0 * peer_output).astype(BF16)
    x2_low = (2.0 * in_order(side, sent, swap(sent, "h"))).astype(BF16)
    att2, share, sent = attention_forward(1, x2_low)
    received, *peers2 = together(swap(sent, "h"), *sort_weights(gathered2.reshape(16, 2, rows_down, width)))
    attended = share + dot((2.0 * received).astype(BF16), peer_output)
    _, saved2 = layer_forward(1, x2_own, attended, peers2)
    scaled_last = saved2[0]
    mixture = att2[3]
    peer_down, peer_up = (peers1[0], peers2[0]), (peers1[1], peers2[1])

    places = side * half_slots + jnp.arange(half_slots)
    weighting = jnp.where(places < length, repeats[0], 0).astype(F32)[:, None]
    gradient2 = own_slots(cotangent).astype(F32) * weighting
    grad_one_own, ffn_low, pre_lows, shared2, biases2 = feed_back(1, gradient2, saved2)
    sent = 0.5 * grad_one_own
    received = swap(sent, "h")
    feed2 = feed_weights_back(saved2, pre_lows, ffn_low, 2 * width)
    feed2, received = together(feed2, received)
    feed2 = lax.psum_scatter(feed2, PLANE, tiled=True)
    _, lows2, attended_low2, share, small_att2 = attention_back(1, att2, sent, received)
    received = swap(piece(share, 1 - side, half_slots), "h")
    attn2_received = swap(attention_sums(1 - core, lows2, mixture, x2_low, attended_low2), "c")
    gradient1 = grad_one_own + own_slots(share) + received

    grad_one_own1, ffn_low, pre_lows, shared1, biases1 = feed_back(0, gradient1, saved1)
    sent = 0.5 * grad_one_own1
    received = swap(sent, "h")
    rest = feed_weights_back(saved1, pre_lows, ffn_low, 2 * width + columns)
    rest = attention_sums(core, lows2, mixture, x2_low, attended_low2, attn2_received, rest, 2 * width // columns)
    rest, received, feed2 = together(rest, received, feed2)
    rest = lax.psum_scatter(rest, PLANE, tiled=True)
    grad_one1, lows1, attended_low1, share, small_att1 = attention_back(0, att1, sent, received)
    attn1_received = swap(attention_sums(1 - core, lows1, att1[3], tokens, attended_low1), "c")
    attn1 = plane_sum(attention_sums(core, lows1, att1[3], tokens, attended_low1, attn1_received))

    def across(own, peer):
        diagonal = lax.ppermute(peer, ("zl", "h"), ((0, 3), (3, 0), (1, 2), (2, 1)))
        own = own + swap(own, "zl")
        peer = swap(peer, "h") + diagonal
        return jnp.concatenate([own[:, :width] + peer, own[:, width:]], axis=1)

    feed2 = across(feed2[:, :width], feed2[:, width:])
    attn1 = attn1 + swap(attn1, "zl")
    feed2, attn1, rest = together(feed2, attn1, rest)
    rest = across(jnp.concatenate([rest[:, :width], rest[:, 2 * width :]], axis=1), rest[:, width : 2 * width])
    own = jnp.concatenate([feed2, rest, attn1], axis=1)
    gathered = lax.all_gather(own, PLANE + ("c",)).reshape(16, 2, *own.shape)
    grad_query, grad_key, grad_value, grad_output, grad_up, grad_down = place_gradients(gathered, width)

    token_grad = grad_one1 + pair_sum(share)
    scaled_last, token_grad = together(scaled_last, token_grad)
    scaled_all = in_order(side, scaled_last, swap(scaled_last, "h"))
    block_output = (scaled_all * ffn_gain[1] + ffn_shift[1]).astype(BF16)
    shared = jnp.stack(shared1 + shared2)
    mine = jnp.concatenate([shared, biases1[0], biases2[0]])
    mine = mine + swap(jnp.concatenate([shared, biases1[1], biases2[1]]), "h")
    small = jnp.concatenate([mine, jnp.stack(small_att1 + small_att2)])
    small, block_output = together(small, block_output)
    small = small + swap(small, "c")
    for axis, pairs in LINKS:
        small = small + lax.ppermute(small, axis, pairs)
    small = small + swap(small, "zl")
    bias_rows = units // width
    shared = small[:10].reshape(2, 5, width)
    grad_up_bias = small[10 : 10 + 2 * bias_rows].reshape(2, units)
    attention = small[10 + 2 * bias_rows :].reshape(2, 2, width)

    return (
        block_output,
        token_grad,
        grad_query,
        attention[:, 0, :columns],
        grad_key,
        grad_value,
        attention[:, 0, columns:],
        grad_output,
        attention[:, 1],
        shared[:, 0],
        shared[:, 1],
        grad_up,
        grad_up_bias,
        grad_down,
        shared[:, 2],
        shared[:, 3],
        shared[:, 4],
    )


def solution(mesh):
    fine = Mesh(mesh.devices.reshape(4, 2, 4, 2, 2), ("y", "zl", "x", "c", "h"))
    rows = ("y", "zl", "x", "c")
    in_specs = (
        P(rows, None),
        P(rows, None),
        P(rows),
        P(rows),
        P(None, None, "h"),
        P(None, "h"),
        P(None, None, "h"),
        P(None, None, "h"),
        P(None, "h"),
        P(None, "h", None),
        P(),
        P(),
        P(),
        P(None, None, "h"),
        P(None, "h"),
        P(None, "h", None),
        P(),
        P(),
        P(),
    )
    out_specs = (
        P(rows, None),
        P(rows, None),
        P(None, None, "h"),
        P(None, "h"),
        P(None, None, "h"),
        P(None, None, "h"),
        P(None, "h"),
        P(None, "h", None),
        P(),
        P(),
        P(),
        P(None, None, "h"),
        P(None, "h"),
        P(None, "h", None),
        P(),
        P(),
        P(),
    )
    return jax.shard_map(local, mesh=fine, in_specs=in_specs, out_specs=out_specs, check_vma=False)
```

```python
import jax
import jax.numpy as jnp
from jax import lax
from jax.experimental import pallas as pl
from jax.experimental.pallas import tpu as pltpu
from jax.sharding import Mesh, PartitionSpec as P

HEAD_DIM = 64
EPS = 1e-12
F32 = jnp.float32
BF16 = jnp.bfloat16
SWAP = ((0, 1), (1, 0))
EDGE0 = ((0, 1), (1, 0), (2, 3), (3, 2))
EDGE1 = ((1, 2), (2, 1), (3, 0), (0, 3))
LINKS = (("x", EDGE0), ("x", EDGE1), ("y", EDGE0), ("y", EDGE1))
PLANE = ("y", "x")


def normalize(summed, gain, shift):
    center = summed - jnp.mean(summed, axis=-1, keepdims=True)
    inverse = lax.rsqrt(jnp.mean(center * center, axis=-1, keepdims=True) + EPS)
    scaled = center * inverse
    return (scaled * gain + shift, scaled, inverse)


def normalize_back(gradient, gain, scaled, inverse):
    gained = gradient * gain
    return inverse * (
        gained
        - jnp.mean(gained, axis=-1, keepdims=True)
        - scaled * jnp.mean(gained * scaled, axis=-1, keepdims=True)
    )


def normal_cdf(values):
    return 0.5 * (1.0 + lax.erf(values * (0.5**0.5)))


def gelu(values):
    return values * normal_cdf(values)


def gelu_slope(values):
    density = jnp.exp(-0.5 * values * values) * 0.3989422804014327
    return normal_cdf(values) + values * density


def dot(left, right):
    return jnp.dot(left, right, preferred_element_type=F32)


def dot_t(left, right):
    return jnp.einsum("sd,fd->sf", left, right, preferred_element_type=F32)


def t_dot(left, right):
    return jnp.einsum("sf,sd->fd", left, right, preferred_element_type=F32)


def column_sum(values):
    return jnp.sum(values.astype(F32), axis=0)


def swap(values, axis):
    return lax.ppermute(values, axis, SWAP)


def pair_sum(values):
    return values + swap(values, "h")


def piece(values, index, size):
    return lax.dynamic_slice_in_dim(values, index * size, size, 0)


def ring_parts(values, axis, dim):
    place = lax.axis_index(axis)
    kept = lax.dynamic_index_in_dim(values, place, dim, keepdims=False)
    received = []
    for distance in (1, 3, 2):
        sent = lax.dynamic_index_in_dim(values, lax.rem(place + distance, 4), dim, keepdims=False)
        pairs = [(start, (start + distance) % 4) for start in range(4)]
        received.append(lax.ppermute(sent, axis, pairs))
    return [kept, *received]


def plane_sum(values):
    rows, columns = values.shape
    values = values.reshape(4, 4, 2, rows // 32, columns)
    x_first = ring_parts(values[:, :, 0], "x", 1)
    y_first = ring_parts(values[:, :, 1], "y", 0)
    parts = together(*x_first, *y_first)
    x_first = ring_parts(sum(parts[1:4], parts[0]), "y", 0)
    y_first = ring_parts(sum(parts[5:], parts[4]), "x", 0)
    parts = together(*x_first, *y_first)
    return jnp.concatenate([sum(parts[1:4], parts[0]), sum(parts[5:], parts[4])])


def in_order(side, mine, other):
    return jnp.concatenate([jnp.where(side == 0, mine, other), jnp.where(side == 0, other, mine)])


def together(*values):
    return lax.optimization_barrier(values)


def t_dot_in_kernel(left, right):
    return lax.dot_general(left, right, (((0,), (0,)), ((), ())), preferred_element_type=F32)


LIMIT = pltpu.CompilerParams(vmem_limit_bytes=24 * 2**20)
SCALAR = pl.BlockSpec(memory_space=pltpu.SMEM)


def across_lanes(left, right):
    return lax.dot_general(left, right, (((1,), (1,)), ((), ())), preferred_element_type=F32)


def attend_kernel(
    sends_mixture,
    place_ref,
    slot_ref,
    query_weight,
    query_bias,
    key_weight,
    value_weight,
    value_bias,
    output_weight,
    query_ref,
    key_ref,
    value_ref,
    mixture_ref,
    logsum_ref,
    own_ref,
    sent_ref,
):
    slots = slot_ref[...]
    query_ref[...] = (dot(slots, query_weight[0]) + query_bias[...]).astype(BF16)
    key_ref[...] = dot(slots, key_weight[0]).astype(BF16)
    value_ref[...] = (dot(slots, value_weight[0]) + value_bias[...]).astype(BF16)
    count = slots.shape[0]
    valid = lax.broadcasted_iota(jnp.int32, (count, count), 0) < place_ref[0]
    for head in range(2):
        cut = slice(head * HEAD_DIM, (head + 1) * HEAD_DIM)
        scores = across_lanes(key_ref[:, cut], query_ref[:, cut] * HEAD_DIM**-0.5)
        scores = jnp.where(valid, scores, -1e30)
        highest = jnp.max(scores, axis=0, keepdims=True)
        raised = jnp.exp(scores - highest)
        totals = jnp.sum(raised, axis=0, keepdims=True)
        probs = (raised * (1.0 / totals)).astype(BF16)
        mixture_ref[:, cut] = t_dot_in_kernel(probs, value_ref[:, cut]).astype(BF16)
        logsum_ref[0, head : head + 1, :] = highest + jnp.log(totals)
    half = count // 2

    def rows_at(side):
        return mixture_ref[pl.ds(pl.multiple_of(side * half, half), half), :]

    parts = [(place_ref[1], own_ref)]
    if sends_mixture:
        sent_ref[...] = 0.5 * rows_at(1 - place_ref[1]).astype(F32)
    else:
        parts.append((1 - place_ref[1], sent_ref))
    for side, share_ref in parts:
        share = dot(rows_at(side), output_weight[0])

        @pl.when(pl.program_id(0) == 0)
        def _():
            share_ref[...] = share

        @pl.when(pl.program_id(0) != 0)
        def _():
            share_ref[...] += share


def attend(
    layer, length, side, slots, query_weight, query_bias, key_weight, value_weight, value_bias, output_weight, sends_mixture
):
    count, width = slots.shape
    heads = query_weight.shape[2]
    pair = 2 * HEAD_DIM
    steps = heads // pair
    whole = pl.BlockSpec((count, width), lambda i: (0, 0))
    weight = pl.BlockSpec((1, width, pair), lambda i: (layer, 0, i))
    bias = pl.BlockSpec((1, pair), lambda i: (0, i))
    part = pl.BlockSpec((count, pair), lambda i: (0, i))
    part_shape = jax.ShapeDtypeStruct((count, heads), BF16)
    shared = pl.BlockSpec((count // 2, width), lambda i: (0, 0))
    sent, sent_width = shared, width
    if sends_mixture:
        sent, sent_width = pl.BlockSpec((count // 2, pair), lambda i: (0, i)), heads
    return pl.pallas_call(
        lambda *refs: attend_kernel(sends_mixture, *refs),
        grid=(steps,),
        in_specs=[SCALAR, whole, weight, bias, weight, weight, bias]
        + [pl.BlockSpec((1, pair, width), lambda i: (layer, i, 0))],
        out_specs=[part] * 4
        + [pl.BlockSpec((1, 2, count), lambda i: (i, 0, 0))]
        + [shared, sent],
        out_shape=[part_shape] * 4
        + [jax.ShapeDtypeStruct((steps, 2, count), F32)]
        + [jax.ShapeDtypeStruct((count // 2, width), F32), jax.ShapeDtypeStruct((count // 2, sent_width), F32)],
        compiler_params=LIMIT,
        cost_estimate=pl.CostEstimate(
            flops=8 * count * width * heads + 4 * count * count * heads,
            bytes_accessed=8 * width * heads + 8 * count * width,
            transcendentals=count * count * heads // HEAD_DIM,
        ),
        name="attend",
    )(jnp.stack([length, side]), slots, query_weight, query_bias, key_weight, value_weight, value_bias, output_weight)


def attend_back_kernel(
    length_ref,
    query_ref,
    key_ref,
    value_ref,
    logsum_ref,
    grad_ref,
    query_weight,
    key_weight,
    value_weight,
    output_weight,
    query_low,
    key_low,
    value_low,
    share_ref,
    query_sum,
    value_sum,
):
    grads = across_lanes(grad_ref[...], output_weight[0]).astype(BF16)
    count = grads.shape[0]
    valid = lax.broadcasted_iota(jnp.int32, (count, count), 0) < length_ref[0]
    scale = HEAD_DIM**-0.5
    for head in range(2):
        cut = slice(head * HEAD_DIM, (head + 1) * HEAD_DIM)
        queries, keys, grad = query_ref[:, cut], key_ref[:, cut], grads[:, cut]
        scores = jnp.where(valid, across_lanes(keys, queries * scale), -1e30)
        probs = jnp.exp(scores - logsum_ref[0, head : head + 1, :])
        grad_probs = across_lanes(value_ref[:, cut], grad)
        inner = jnp.sum(probs * grad_probs, axis=0, keepdims=True)
        grad_scores = (probs * (grad_probs - inner)).astype(BF16)
        query_low[:, cut] = (t_dot_in_kernel(grad_scores, keys) * scale).astype(BF16)
        key_low[:, cut] = (dot(grad_scores, queries) * scale).astype(BF16)
        value_low[:, cut] = dot(probs.astype(BF16), grad).astype(BF16)
    query_sum[...] = jnp.sum(query_low[...].astype(F32), axis=0, keepdims=True)
    value_sum[...] = jnp.sum(value_low[...].astype(F32), axis=0, keepdims=True)
    share = across_lanes(query_low[...], query_weight[0])
    share += across_lanes(key_low[...], key_weight[0])
    share += across_lanes(value_low[...], value_weight[0])

    @pl.when(pl.program_id(0) == 0)
    def _():
        share_ref[...] = share

    @pl.when(pl.program_id(0) != 0)
    def _():
        share_ref[...] += share


def attend_back(layer, length, saved, attended_low, query_weight, key_weight, value_weight, output_weight):
    queries, keys, values, _, logsum = saved
    count, width = attended_low.shape
    heads = queries.shape[1]
    pair = 2 * HEAD_DIM
    steps = heads // pair
    whole = pl.BlockSpec((count, width), lambda i: (0, 0))
    weight = pl.BlockSpec((1, width, pair), lambda i: (layer, 0, i))
    part = pl.BlockSpec((count, pair), lambda i: (0, i))
    part_shape = jax.ShapeDtypeStruct((count, heads), BF16)
    sums = pl.BlockSpec((1, pair), lambda i: (0, i))
    sums_shape = jax.ShapeDtypeStruct((1, heads), F32)
    return pl.pallas_call(
        attend_back_kernel,
        grid=(steps,),
        in_specs=[SCALAR, part, part, part, pl.BlockSpec((1, 2, count), lambda i: (i, 0, 0)), whole]
        + [weight] * 3
        + [pl.BlockSpec((1, pair, width), lambda i: (layer, i, 0))],
        out_specs=[part] * 3 + [whole, sums, sums],
        out_shape=[part_shape] * 3 + [jax.ShapeDtypeStruct((count, width), F32), sums_shape, sums_shape],
        compiler_params=LIMIT,
        cost_estimate=pl.CostEstimate(
            flops=8 * count * width * heads + 10 * count * count * heads,
            bytes_accessed=8 * width * heads + 8 * count * width,
            transcendentals=count * count * heads // HEAD_DIM,
        ),
        name="attend_back",
    )(length.reshape(1), queries, keys, values, logsum, attended_low, query_weight, key_weight, value_weight, output_weight)


def pieces_kernel(place_ref, down_in, up_in, piece_ref):
    width = piece_ref.shape[2]

    @pl.when(place_ref[1] == 0)
    def _():
        piece_ref[0] = down_in[0].astype(F32)

    @pl.when(place_ref[1] != 0)
    def _():
        half = up_in.shape[1]
        piece_ref[0, :half, :] = up_in[0, :, :width].astype(F32)
        piece_ref[0, half:, :] = up_in[0, :, width:].astype(F32)


def weight_pieces(chip, core, down_weight, up_weight):
    layers, units, width = down_weight.shape
    rows = units // 16
    return pl.pallas_call(
        pieces_kernel,
        grid_spec=pltpu.PrefetchScalarGridSpec(
            num_scalar_prefetch=1,
            grid=(layers,),
            in_specs=[
                pl.BlockSpec((1, rows, width), lambda l, place: (l, place[0], 0)),
                pl.BlockSpec((1, rows // 2, units), lambda l, place: (l, place[0], 0)),
            ],
            out_specs=pl.BlockSpec((1, rows, width), lambda l, place: (l, 0, 0)),
        ),
        out_shape=jax.ShapeDtypeStruct((layers, rows, width), F32),
        compiler_params=LIMIT,
        name="weight_pieces",
    )(jnp.stack([chip, core]), down_weight, up_weight)


def feed_sums_kernel(received, part_ref, act_own, act_peer, pre_own, pre_peer, ffn_low, hidden_low, *refs):
    out_ref = refs[-1]
    width = ffn_low.shape[1]

    def write(own, peer, right):
        for k, left in enumerate((own, peer)):
            total = t_dot_in_kernel(left[...], right[...])
            cut = slice(k * width, (k + 1) * width)
            out_ref[:, cut] = total + refs[0][:, cut] if received else total

    @pl.when(part_ref[0] == 0)
    def _():
        write(act_own, act_peer, ffn_low)

    @pl.when(part_ref[0] != 0)
    def _():
        write(pre_own, pre_peer, hidden_low)


def feed_sums(part, actives, pre_lows, ffn_low, hidden_low, columns, received=None):
    slots, units = actives[0].shape
    width = ffn_low.shape[1]
    block = units // 4
    left = pl.BlockSpec((slots, block), lambda i: (0, i))
    right = pl.BlockSpec((slots, width), lambda i: (0, 0))
    rows = pl.BlockSpec((block, 2 * width), lambda i: (i, 0))
    more = [] if received is None else [received]
    return pl.pallas_call(
        lambda *refs: feed_sums_kernel(bool(more), *refs),
        grid=(4,),
        in_specs=[SCALAR] + [left] * 4 + [right] * 2 + [rows] * len(more),
        out_specs=rows,
        out_shape=jax.ShapeDtypeStruct((units, columns), F32),
        compiler_params=LIMIT,
        cost_estimate=pl.CostEstimate(
            flops=4 * slots * units * width, bytes_accessed=(8 + 8 * len(more)) * units * width, transcendentals=0
        ),
        name="feed_sums",
    )(part.reshape(1), *actives, *pre_lows, ffn_low, hidden_low, *more)


def attention_sums_kernel(received, part_ref, query_ref, key_ref, value_ref, mixture_ref, slot_ref, grad_ref, *refs):
    out_ref = refs[-1]
    second = lax.rem(pl.program_id(0), 2)

    def write(which, left, right):
        @pl.when(2 * part_ref[0] + second == which)
        def _():
            total = t_dot_in_kernel(left[...], right[...])
            out_ref[...] = total + refs[0][...] if received else total

    write(0, query_ref, slot_ref)
    write(1, key_ref, slot_ref)
    write(2, value_ref, slot_ref)
    write(3, mixture_ref, grad_ref)


def attention_sums(part, lows, mixture, rounded, attended_low, received=None, into=None, place=0):
    slots, heads = mixture.shape
    half = rounded.shape[1] // 2
    left = pl.BlockSpec((slots, heads), lambda i: (0, 0))
    right = pl.BlockSpec((slots, half), lambda i: (0, i // 2))
    rows = pl.BlockSpec((heads, half), lambda i: (i, 0))
    more = [item for item in (received, into) if item is not None]
    shape = (4 * heads, half) if into is None else into.shape
    return pl.pallas_call(
        lambda *refs: attention_sums_kernel(received is not None, *refs),
        grid=(4,),
        in_specs=[SCALAR] + [left] * 4 + [right] * 2 + [rows, pl.BlockSpec(memory_space=pl.ANY)][: len(more)],
        out_specs=pl.BlockSpec((heads, half), lambda i: (i, place)),
        out_shape=jax.ShapeDtypeStruct(shape, F32),
        input_output_aliases={} if into is None else {8: 0},
        compiler_params=LIMIT,
        cost_estimate=pl.CostEstimate(flops=8 * slots * heads * half, bytes_accessed=16 * heads * half, transcendentals=0),
        name="attention_sums",
    )(part.reshape(1), *lows, mixture, rounded, attended_low, *more)


def sort_kernel(piece_ref, down_ref, up_ref):
    chips, _, rows, width = piece_ref.shape
    for i in range(chips):
        down_ref[i * rows : (i + 1) * rows, :] = piece_ref[i, 0].astype(BF16)
        up = piece_ref[i, 1].astype(BF16)
        half = rows // 2
        up_ref[i * half : (i + 1) * half, :width] = up[:half]
        up_ref[i * half : (i + 1) * half, width:] = up[half:]


def sort_weights(gathered):
    chips, _, rows, width = gathered.shape
    step = 4
    units = chips * rows
    return pl.pallas_call(
        sort_kernel,
        grid=(chips // step,),
        in_specs=[pl.BlockSpec((step, 2, rows, width), lambda i: (i, 0, 0, 0))],
        out_specs=[
            pl.BlockSpec((step * rows, width), lambda i: (i, 0)),
            pl.BlockSpec((step * rows // 2, units), lambda i: (i, 0)),
        ],
        out_shape=[
            jax.ShapeDtypeStruct((units, width), BF16),
            jax.ShapeDtypeStruct((width, units), BF16),
        ],
        compiler_params=LIMIT,
        cost_estimate=pl.CostEstimate(flops=0, bytes_accessed=12 * units * width, transcendentals=0),
        name="sort_weights",
    )(gathered)


def rows_of(ref):
    chips, _, rows, columns = ref.shape
    return ref[...].reshape(chips * rows, columns)


def place_feed_kernel(down_in, up_in, down_ref, up_ref):
    down_ref[0] = rows_of(down_in)
    up_ref[0] = rows_of(up_in).T


def place_attention_kernel(query_in, key_in, value_in, output_in, query_ref, key_ref, value_ref, output_ref):
    query_ref[0] = rows_of(query_in).T
    key_ref[0] = rows_of(key_in).T
    value_ref[0] = rows_of(value_in).T
    output_ref[0] = rows_of(output_in)


def place_gradients(gathered, width):
    chips, _, rows, _ = gathered.shape
    step = 4
    units, block = chips * rows, step * rows
    half = width // 2

    def feed_in(core):
        return pl.BlockSpec((step, 1, rows, width), lambda l, i: (i, core, 0, 1 - l))

    def attention_in(core, which):
        return pl.BlockSpec((step, 1, rows, half), lambda l, i: (2 * i + which, core, 0, 5 - l))

    limit = pltpu.CompilerParams(vmem_limit_bytes=40 * 2**20)
    down, up = pl.pallas_call(
        place_feed_kernel,
        grid=(2, chips // step),
        in_specs=[feed_in(0), feed_in(1)],
        out_specs=[
            pl.BlockSpec((1, block, width), lambda l, i: (l, i, 0)),
            pl.BlockSpec((1, width, block), lambda l, i: (l, 0, i)),
        ],
        out_shape=[
            jax.ShapeDtypeStruct((2, units, width), F32),
            jax.ShapeDtypeStruct((2, width, units), F32),
        ],
        compiler_params=limit,
        name="place_feed",
    )(gathered, gathered)
    tall = pl.BlockSpec((1, half, block), lambda l, i: (l, i, 0))
    tall_shape = jax.ShapeDtypeStruct((2, width, block), F32)
    query, key, value, output = pl.pallas_call(
        place_attention_kernel,
        grid=(2, 2),
        in_specs=[attention_in(0, 0), attention_in(0, 1), attention_in(1, 0), attention_in(1, 1)],
        out_specs=[tall, tall, tall, pl.BlockSpec((1, block, half), lambda l, i: (l, 0, i))],
        out_shape=[tall_shape, tall_shape, tall_shape, jax.ShapeDtypeStruct((2, block, width), F32)],
        compiler_params=limit,
        name="place_attention",
    )(gathered, gathered, gathered, gathered)
    return query, key, value, output, up, down


def local(
    tokens,
    cotangent,
    lengths,
    repeats,
    query_weight,
    query_bias,
    key_weight,
    value_weight,
    value_bias,
    output_weight,
    output_bias,
    attn_gain,
    attn_shift,
    up_weight,
    up_bias,
    down_weight,
    down_bias,
    ffn_gain,
    ffn_shift,
):
    length = lengths[0]
    side = lax.axis_index("h")
    core = lax.axis_index("c")
    chip = lax.axis_index("y") * 4 + lax.axis_index("x")
    first_core = core == 0
    slots, width = tokens.shape
    half_slots = slots // 2
    units = up_weight.shape[2]
    columns = query_weight.shape[2]

    rows_down = units // 16
    pieces = weight_pieces(chip, core, down_weight, up_weight)
    pieces1, pieces2 = together(swap(pieces[0], "h"), pieces[1])
    gathered1 = lax.all_gather(pieces1, PLANE + ("c",))
    pieces2 = swap(pieces2, "h")
    peer_up_bias = swap(up_bias.astype(F32), "h")

    def own_slots(values):
        return piece(values, side, half_slots)

    def feed_weights_back(saved, pre_lows, ffn_low, columns):
        actives, hidden_low = saved[3], saved[4]
        received = swap(feed_sums(1 - core, actives, pre_lows, ffn_low, hidden_low, 2 * width), "c")
        return feed_sums(core, actives, pre_lows, ffn_low, hidden_low, columns, received)

    def attention_forward(layer, rounded):
        *attention, share, sent = attend(
            layer,
            length,
            side,
            rounded,
            query_weight,
            query_bias[layer].astype(F32)[None],
            key_weight,
            value_weight,
            value_bias[layer].astype(F32)[None],
            output_weight,
            layer == 1,
        )
        return attention, share, sent

    def attention_back(layer, saved, grad_one_sent, received):
        grad_one = 2.0 * in_order(side, grad_one_sent, received)
        attended_low = grad_one.astype(BF16)
        *lows, share, query_sum, value_sum = attend_back(
            layer, length, saved, attended_low, query_weight, key_weight, value_weight, output_weight
        )
        small = [jnp.concatenate([query_sum[0], value_sum[0]]), column_sum(attended_low)]
        return grad_one, lows, attended_low, share, small

    def feed_back(layer, gradient, saved):
        scaled_two, inverse_two, pres, actives, hidden_low, scaled_one, inverse_one = saved
        grad_two = normalize_back(gradient, ffn_gain[layer], scaled_two, inverse_two)
        ffn_low = grad_two.astype(BF16)
        downs, ups = (down_weight[layer], peer_down[layer]), (up_weight[layer], peer_up[layer])
        pre_lows = [
            (dot_t(ffn_low, down) * gelu_slope(pre)).astype(BF16) for down, pre in zip(downs, pres, strict=True)
        ]
        grad_hidden = grad_two + dot_t(pre_lows[0], ups[0]) + dot_t(pre_lows[1], ups[1])
        grad_one = normalize_back(grad_hidden, attn_gain[layer], scaled_one, inverse_one)
        shared = [
            jnp.sum(grad_hidden * scaled_one, axis=0),
            jnp.sum(grad_hidden, axis=0),
            column_sum(ffn_low),
            jnp.sum(gradient * scaled_two, axis=0),
            jnp.sum(gradient, axis=0),
        ]
        biases = [column_sum(item).reshape(-1, width) for item in pre_lows]
        return grad_one, ffn_low, pre_lows, shared, biases

    def layer_forward(layer, x_own, attended, peers):
        attended = attended + output_bias[layer]
        hidden, scaled, inverse = normalize(x_own + attended, attn_gain[layer], attn_shift[layer])
        hidden_low = hidden.astype(BF16)
        pre = dot(hidden_low, up_weight[layer]) + up_bias[layer]
        active = gelu(pre).astype(BF16)
        ffn_out = dot(active, down_weight[layer])
        peer_down, peer_up = peers
        pre_peer = dot(hidden_low, peer_up) + peer_up_bias[layer]
        active_peer = gelu(pre_peer).astype(BF16)
        ffn_out = ffn_out + dot(active_peer, peer_down) + down_bias[layer]
        out, scaled_two, inverse_two = normalize(hidden + ffn_out, ffn_gain[layer], ffn_shift[layer])
        saved = (scaled_two, inverse_two, (pre, pre_peer), (active, active_peer), hidden_low, scaled, inverse)
        return out, saved

    att1, share, sent = attention_forward(0, tokens)
    pieces2, sent = together(pieces2, sent)
    peers1 = sort_weights(gathered1.reshape(16, 2, rows_down, width))
    gathered2 = lax.all_gather(pieces2, PLANE + ("c",))
    received, peer_output = together(swap(sent, "h"), 0.5 * output_weight[1].astype(F32))
    peer_output = swap(peer_output, "h")
    x2_own, saved1 = layer_forward(0, own_slots(tokens).astype(F32), share + received, peers1)
    sent, peer_output = together(0.5 * x2_own, peer_output)
    peer_output = (2.0 * peer_output).astype(BF16)
    x2_low = (2.0 * in_order(side, sent, swap(sent, "h"))).astype(BF16)
    att2, share, sent = attention_forward(1, x2_low)
    received, *peers2 = together(swap(sent, "h"), *sort_weights(gathered2.reshape(16, 2, rows_down, width)))
    attended = share + dot((2.0 * received).astype(BF16), peer_output)
    _, saved2 = layer_forward(1, x2_own, attended, peers2)
    scaled_last = saved2[0]
    mixture = att2[3]
    peer_down, peer_up = (peers1[0], peers2[0]), (peers1[1], peers2[1])

    places = side * half_slots + jnp.arange(half_slots)
    weighting = jnp.where(places < length, repeats[0], 0).astype(F32)[:, None]
    gradient2 = own_slots(cotangent).astype(F32) * weighting
    grad_one_own, ffn_low, pre_lows, shared2, biases2 = feed_back(1, gradient2, saved2)
    sent = 0.5 * grad_one_own
    received = swap(sent, "h")
    feed2 = feed_weights_back(saved2, pre_lows, ffn_low, 2 * width)
    feed2, received = together(feed2, received)
    feed2 = lax.psum_scatter(feed2, PLANE, tiled=True)
    _, lows2, attended_low2, share, small_att2 = attention_back(1, att2, sent, received)
    received = swap(piece(share, 1 - side, half_slots), "h")
    attn2_received = swap(attention_sums(1 - core, lows2, mixture, x2_low, attended_low2), "c")
    gradient1 = grad_one_own + own_slots(share) + received

    grad_one_own1, ffn_low, pre_lows, shared1, biases1 = feed_back(0, gradient1, saved1)
    sent = 0.5 * grad_one_own1
    received = swap(sent, "h")
    rest = feed_weights_back(saved1, pre_lows, ffn_low, 2 * width + columns)
    rest = attention_sums(core, lows2, mixture, x2_low, attended_low2, attn2_received, rest, 2 * width // columns)
    rest, received, feed2 = together(rest, received, feed2)
    rest = lax.psum_scatter(rest, PLANE, tiled=True)
    grad_one1, lows1, attended_low1, share, small_att1 = attention_back(0, att1, sent, received)
    attn1_received = swap(attention_sums(1 - core, lows1, att1[3], tokens, attended_low1), "c")
    attn1 = plane_sum(attention_sums(core, lows1, att1[3], tokens, attended_low1, attn1_received))

    def across(own, peer):
        diagonal = lax.ppermute(peer, ("zl", "h"), ((0, 3), (3, 0), (1, 2), (2, 1)))
        own = own + swap(own, "zl")
        peer = swap(peer, "h") + diagonal
        return jnp.concatenate([own[:, :width] + peer, own[:, width:]], axis=1)

    feed2 = across(feed2[:, :width], feed2[:, width:])
    attn1 = attn1 + swap(attn1, "zl")
    feed2, attn1, rest = together(feed2, attn1, rest)
    rest = across(jnp.concatenate([rest[:, :width], rest[:, 2 * width :]], axis=1), rest[:, width : 2 * width])
    own = jnp.concatenate([feed2, rest, attn1], axis=1)
    gathered = lax.all_gather(own, PLANE + ("c",)).reshape(16, 2, *own.shape)
    grad_query, grad_key, grad_value, grad_output, grad_up, grad_down = place_gradients(gathered, width)

    token_grad = grad_one1 + pair_sum(share)
    scaled_last, token_grad = together(scaled_last, token_grad)
    scaled_all = in_order(side, scaled_last, swap(scaled_last, "h"))
    block_output = (scaled_all * ffn_gain[1] + ffn_shift[1]).astype(BF16)
    shared = jnp.stack(shared1 + shared2)
    mine = jnp.concatenate([shared, biases1[0], biases2[0]])
    mine = mine + swap(jnp.concatenate([shared, biases1[1], biases2[1]]), "h")
    small = jnp.concatenate([mine, jnp.stack(small_att1 + small_att2)])
    small, block_output = together(small, block_output)
    small = small + swap(small, "c")
    for axis, pairs in LINKS:
        small = small + lax.ppermute(small, axis, pairs)
    small = small + swap(small, "zl")
    bias_rows = units // width
    shared = small[:10].reshape(2, 5, width)
    grad_up_bias = small[10 : 10 + 2 * bias_rows].reshape(2, units)
    attention = small[10 + 2 * bias_rows :].reshape(2, 2, width)

    return (
        block_output,
        token_grad,
        grad_query,
        attention[:, 0, :columns],
        grad_key,
        grad_value,
        attention[:, 0, columns:],
        grad_output,
        attention[:, 1],
        shared[:, 0],
        shared[:, 1],
        grad_up,
        grad_up_bias,
        grad_down,
        shared[:, 2],
        shared[:, 3],
        shared[:, 4],
    )


def solution(mesh):
    fine = Mesh(mesh.devices.reshape(4, 2, 4, 2, 2), ("y", "zl", "x", "c", "h"))
    rows = ("y", "zl", "x", "c")
    in_specs = (
        P(rows, None),
        P(rows, None),
        P(rows),
        P(rows),
        P(None, None, "h"),
        P(None, "h"),
        P(None, None, "h"),
        P(None, None, "h"),
        P(None, "h"),
        P(None, "h", None),
        P(),
        P(),
        P(),
        P(None, None, "h"),
        P(None, "h"),
        P(None, "h", None),
        P(),
        P(),
        P(),
    )
    out_specs = (
        P(rows, None),
        P(rows, None),
        P(None, None, "h"),
        P(None, "h"),
        P(None, None, "h"),
        P(None, None, "h"),
        P(None, "h"),
        P(None, "h", None),
        P(),
        P(),
        P(),
        P(None, None, "h"),
        P(None, "h"),
        P(None, "h", None),
        P(),
        P(),
        P(),
    )
    return jax.shard_map(local, mesh=fine, in_specs=in_specs, out_specs=out_specs, check_vma=False)
```

```python
import jax
import jax.numpy as jnp
from jax import lax
from jax.experimental import pallas as pl
from jax.experimental.pallas import tpu as pltpu
from jax.sharding import Mesh, PartitionSpec as P

HEAD_DIM = 64
EPS = 1e-12
F32 = jnp.float32
BF16 = jnp.bfloat16
SWAP = ((0, 1), (1, 0))
EDGE0 = ((0, 1), (1, 0), (2, 3), (3, 2))
EDGE1 = ((1, 2), (2, 1), (3, 0), (0, 3))
LINKS = (("x", EDGE0), ("x", EDGE1), ("y", EDGE0), ("y", EDGE1))
PLANE = ("y", "x")


def normalize(summed, gain, shift):
    center = summed - jnp.mean(summed, axis=-1, keepdims=True)
    inverse = lax.rsqrt(jnp.mean(center * center, axis=-1, keepdims=True) + EPS)
    scaled = center * inverse
    return (scaled * gain + shift, scaled, inverse)


def normalize_back(gradient, gain, scaled, inverse):
    gained = gradient * gain
    return inverse * (
        gained
        - jnp.mean(gained, axis=-1, keepdims=True)
        - scaled * jnp.mean(gained * scaled, axis=-1, keepdims=True)
    )


def normal_cdf(values):
    return 0.5 * (1.0 + lax.erf(values * (0.5**0.5)))


def gelu(values):
    return values * normal_cdf(values)


def gelu_slope(values):
    density = jnp.exp(-0.5 * values * values) * 0.3989422804014327
    return normal_cdf(values) + values * density


def dot(left, right):
    return jnp.dot(left, right, preferred_element_type=F32)


def dot_t(left, right):
    return jnp.einsum("sd,fd->sf", left, right, preferred_element_type=F32)


def t_dot(left, right):
    return jnp.einsum("sf,sd->fd", left, right, preferred_element_type=F32)


def column_sum(values):
    return jnp.sum(values.astype(F32), axis=0)


def swap(values, axis):
    return lax.ppermute(values, axis, SWAP)


def pair_sum(values):
    return values + swap(values, "h")


def piece(values, index, size):
    return lax.dynamic_slice_in_dim(values, index * size, size, 0)


def ring_parts(values, axis, dim):
    place = lax.axis_index(axis)
    kept = lax.dynamic_index_in_dim(values, place, dim, keepdims=False)
    received = []
    for distance in (1, 3, 2):
        sent = lax.dynamic_index_in_dim(values, lax.rem(place + distance, 4), dim, keepdims=False)
        pairs = [(start, (start + distance) % 4) for start in range(4)]
        received.append(lax.ppermute(sent, axis, pairs))
    return [kept, *received]


def plane_sum(values):
    rows, columns = values.shape
    values = values.reshape(4, 4, 2, rows // 32, columns)
    x_first = ring_parts(values[:, :, 0], "x", 1)
    y_first = ring_parts(values[:, :, 1], "y", 0)
    parts = together(*x_first, *y_first)
    x_first = ring_parts(sum(parts[1:4], parts[0]), "y", 0)
    y_first = ring_parts(sum(parts[5:], parts[4]), "x", 0)
    parts = together(*x_first, *y_first)
    return jnp.concatenate([sum(parts[1:4], parts[0]), sum(parts[5:], parts[4])])


def in_order(side, mine, other):
    return jnp.concatenate([jnp.where(side == 0, mine, other), jnp.where(side == 0, other, mine)])


def together(*values):
    return lax.optimization_barrier(values)


def t_dot_in_kernel(left, right):
    return lax.dot_general(left, right, (((0,), (0,)), ((), ())), preferred_element_type=F32)


LIMIT = pltpu.CompilerParams(vmem_limit_bytes=24 * 2**20)
SCALAR = pl.BlockSpec(memory_space=pltpu.SMEM)


def across_lanes(left, right):
    return lax.dot_general(left, right, (((1,), (1,)), ((), ())), preferred_element_type=F32)


def attend_kernel(
    sends_mixture,
    place_ref,
    slot_ref,
    query_weight,
    query_bias,
    key_weight,
    value_weight,
    value_bias,
    output_weight,
    query_ref,
    key_ref,
    value_ref,
    mixture_ref,
    logsum_ref,
    own_ref,
    sent_ref,
):
    slots = slot_ref[...]
    query_ref[...] = (dot(slots, query_weight[0]) + query_bias[...]).astype(BF16)
    key_ref[...] = dot(slots, key_weight[0]).astype(BF16)
    value_ref[...] = (dot(slots, value_weight[0]) + value_bias[...]).astype(BF16)
    count = slots.shape[0]
    valid = lax.broadcasted_iota(jnp.int32, (count, count), 0) < place_ref[0]
    for head in range(2):
        cut = slice(head * HEAD_DIM, (head + 1) * HEAD_DIM)
        scores = across_lanes(key_ref[:, cut], query_ref[:, cut] * HEAD_DIM**-0.5)
        scores = jnp.where(valid, scores, -1e30)
        highest = jnp.max(scores, axis=0, keepdims=True)
        raised = jnp.exp(scores - highest)
        totals = jnp.sum(raised, axis=0, keepdims=True)
        probs = (raised * (1.0 / totals)).astype(BF16)
        mixture_ref[:, cut] = t_dot_in_kernel(probs, value_ref[:, cut]).astype(BF16)
        logsum_ref[0, head : head + 1, :] = highest + jnp.log(totals)
    half = count // 2

    def rows_at(side):
        return mixture_ref[pl.ds(pl.multiple_of(side * half, half), half), :]

    parts = [(place_ref[1], own_ref)]
    if sends_mixture:
        sent_ref[...] = 0.5 * rows_at(1 - place_ref[1]).astype(F32)
    else:
        parts.append((1 - place_ref[1], sent_ref))
    for side, share_ref in parts:
        share = dot(rows_at(side), output_weight[0])

        @pl.when(pl.program_id(0) == 0)
        def _():
            share_ref[...] = share

        @pl.when(pl.program_id(0) != 0)
        def _():
            share_ref[...] += share


def attend(
    layer, length, side, slots, query_weight, query_bias, key_weight, value_weight, value_bias, output_weight, sends_mixture
):
    count, width = slots.shape
    heads = query_weight.shape[2]
    pair = 2 * HEAD_DIM
    steps = heads // pair
    whole = pl.BlockSpec((count, width), lambda i: (0, 0))
    weight = pl.BlockSpec((1, width, pair), lambda i: (layer, 0, i))
    bias = pl.BlockSpec((1, pair), lambda i: (0, i))
    part = pl.BlockSpec((count, pair), lambda i: (0, i))
    part_shape = jax.ShapeDtypeStruct((count, heads), BF16)
    shared = pl.BlockSpec((count // 2, width), lambda i: (0, 0))
    sent, sent_width = shared, width
    if sends_mixture:
        sent, sent_width = pl.BlockSpec((count // 2, pair), lambda i: (0, i)), heads
    return pl.pallas_call(
        lambda *refs: attend_kernel(sends_mixture, *refs),
        grid=(steps,),
        in_specs=[SCALAR, whole, weight, bias, weight, weight, bias]
        + [pl.BlockSpec((1, pair, width), lambda i: (layer, i, 0))],
        out_specs=[part] * 4
        + [pl.BlockSpec((1, 2, count), lambda i: (i, 0, 0))]
        + [shared, sent],
        out_shape=[part_shape] * 4
        + [jax.ShapeDtypeStruct((steps, 2, count), F32)]
        + [jax.ShapeDtypeStruct((count // 2, width), F32), jax.ShapeDtypeStruct((count // 2, sent_width), F32)],
        compiler_params=LIMIT,
        cost_estimate=pl.CostEstimate(
            flops=8 * count * width * heads + 4 * count * count * heads,
            bytes_accessed=8 * width * heads + 8 * count * width,
            transcendentals=count * count * heads // HEAD_DIM,
        ),
        name="attend",
    )(jnp.stack([length, side]), slots, query_weight, query_bias, key_weight, value_weight, value_bias, output_weight)


def attend_back_kernel(
    length_ref,
    query_ref,
    key_ref,
    value_ref,
    logsum_ref,
    grad_ref,
    query_weight,
    key_weight,
    value_weight,
    output_weight,
    query_low,
    key_low,
    value_low,
    share_ref,
    query_sum,
    value_sum,
):
    grads = across_lanes(grad_ref[...], output_weight[0]).astype(BF16)
    count = grads.shape[0]
    valid = lax.broadcasted_iota(jnp.int32, (count, count), 0) < length_ref[0]
    scale = HEAD_DIM**-0.5
    for head in range(2):
        cut = slice(head * HEAD_DIM, (head + 1) * HEAD_DIM)
        queries, keys, grad = query_ref[:, cut], key_ref[:, cut], grads[:, cut]
        scores = jnp.where(valid, across_lanes(keys, queries * scale), -1e30)
        probs = jnp.exp(scores - logsum_ref[0, head : head + 1, :])
        grad_probs = across_lanes(value_ref[:, cut], grad)
        inner = jnp.sum(probs * grad_probs, axis=0, keepdims=True)
        grad_scores = (probs * (grad_probs - inner)).astype(BF16)
        query_low[:, cut] = (t_dot_in_kernel(grad_scores, keys) * scale).astype(BF16)
        key_low[:, cut] = (dot(grad_scores, queries) * scale).astype(BF16)
        value_low[:, cut] = dot(probs.astype(BF16), grad).astype(BF16)
    query_sum[...] = jnp.sum(query_low[...].astype(F32), axis=0, keepdims=True)
    value_sum[...] = jnp.sum(value_low[...].astype(F32), axis=0, keepdims=True)
    share = across_lanes(query_low[...], query_weight[0])
    share += across_lanes(key_low[...], key_weight[0])
    share += across_lanes(value_low[...], value_weight[0])

    @pl.when(pl.program_id(0) == 0)
    def _():
        share_ref[...] = share

    @pl.when(pl.program_id(0) != 0)
    def _():
        share_ref[...] += share


def attend_back(layer, length, saved, attended_low, query_weight, key_weight, value_weight, output_weight):
    queries, keys, values, _, logsum = saved
    count, width = attended_low.shape
    heads = queries.shape[1]
    pair = 2 * HEAD_DIM
    steps = heads // pair
    whole = pl.BlockSpec((count, width), lambda i: (0, 0))
    weight = pl.BlockSpec((1, width, pair), lambda i: (layer, 0, i))
    part = pl.BlockSpec((count, pair), lambda i: (0, i))
    part_shape = jax.ShapeDtypeStruct((count, heads), BF16)
    sums = pl.BlockSpec((1, pair), lambda i: (0, i))
    sums_shape = jax.ShapeDtypeStruct((1, heads), F32)
    return pl.pallas_call(
        attend_back_kernel,
        grid=(steps,),
        in_specs=[SCALAR, part, part, part, pl.BlockSpec((1, 2, count), lambda i: (i, 0, 0)), whole]
        + [weight] * 3
        + [pl.BlockSpec((1, pair, width), lambda i: (layer, i, 0))],
        out_specs=[part] * 3 + [whole, sums, sums],
        out_shape=[part_shape] * 3 + [jax.ShapeDtypeStruct((count, width), F32), sums_shape, sums_shape],
        compiler_params=LIMIT,
        cost_estimate=pl.CostEstimate(
            flops=8 * count * width * heads + 10 * count * count * heads,
            bytes_accessed=8 * width * heads + 8 * count * width,
            transcendentals=count * count * heads // HEAD_DIM,
        ),
        name="attend_back",
    )(length.reshape(1), queries, keys, values, logsum, attended_low, query_weight, key_weight, value_weight, output_weight)


def pieces_kernel(place_ref, down_ref, up_ref, piece_ref, down_rows, up_rows, done):
    layers, rows, width = piece_ref.shape
    chip = place_ref[0]
    half = rows // 2

    @pl.when(place_ref[1] == 0)
    def _():
        source = down_ref.at[:, pl.ds(pl.multiple_of(chip * rows, rows), rows), :]
        copy = pltpu.make_async_copy(source, down_rows, done)
        copy.start()
        copy.wait()
        piece_ref[...] = down_rows[...].astype(F32)

    @pl.when(place_ref[1] != 0)
    def _():
        source = up_ref.at[:, pl.ds(pl.multiple_of(chip * half, half), half), :]
        copy = pltpu.make_async_copy(source, up_rows, done)
        copy.start()
        copy.wait()
        for layer in range(layers):
            piece_ref[layer, :half, :] = up_rows[layer, :, :width].astype(F32)
            piece_ref[layer, half:, :] = up_rows[layer, :, width:].astype(F32)


def weight_pieces(chip, core, down_weight, up_weight):
    layers, units, width = down_weight.shape
    rows = units // 16
    return pl.pallas_call(
        pieces_kernel,
        in_specs=[SCALAR] + [pl.BlockSpec(memory_space=pltpu.HBM)] * 2,
        out_specs=pl.BlockSpec(memory_space=pltpu.VMEM),
        out_shape=jax.ShapeDtypeStruct((layers, rows, width), F32),
        scratch_shapes=[
            pltpu.VMEM((layers, rows, width), BF16),
            pltpu.VMEM((layers, rows // 2, units), BF16),
            pltpu.SemaphoreType.DMA,
        ],
        compiler_params=LIMIT,
        name="weight_pieces",
    )(jnp.stack([chip, core]), down_weight, up_weight)


def feed_sums_kernel(received, part_ref, act_own, act_peer, pre_own, pre_peer, ffn_low, hidden_low, *refs):
    out_ref = refs[-1]
    width = ffn_low.shape[1]

    def write(own, peer, right):
        for k, left in enumerate((own, peer)):
            total = t_dot_in_kernel(left[...], right[...])
            cut = slice(k * width, (k + 1) * width)
            out_ref[:, cut] = total + refs[0][:, cut] if received else total

    @pl.when(part_ref[0] == 0)
    def _():
        write(act_own, act_peer, ffn_low)

    @pl.when(part_ref[0] != 0)
    def _():
        write(pre_own, pre_peer, hidden_low)


def feed_sums(part, actives, pre_lows, ffn_low, hidden_low, columns, received=None):
    slots, units = actives[0].shape
    width = ffn_low.shape[1]
    block = units // 4
    left = pl.BlockSpec((slots, block), lambda i: (0, i))
    right = pl.BlockSpec((slots, width), lambda i: (0, 0))
    rows = pl.BlockSpec((block, 2 * width), lambda i: (i, 0))
    more = [] if received is None else [received]
    return pl.pallas_call(
        lambda *refs: feed_sums_kernel(bool(more), *refs),
        grid=(4,),
        in_specs=[SCALAR] + [left] * 4 + [right] * 2 + [rows] * len(more),
        out_specs=rows,
        out_shape=jax.ShapeDtypeStruct((units, columns), F32),
        compiler_params=LIMIT,
        cost_estimate=pl.CostEstimate(
            flops=4 * slots * units * width, bytes_accessed=(8 + 8 * len(more)) * units * width, transcendentals=0
        ),
        name="feed_sums",
    )(part.reshape(1), *actives, *pre_lows, ffn_low, hidden_low, *more)


def attention_sums_kernel(received, part_ref, query_ref, key_ref, value_ref, mixture_ref, slot_ref, grad_ref, *refs):
    out_ref = refs[-1]
    second = lax.rem(pl.program_id(0), 2)

    def write(which, left, right):
        @pl.when(2 * part_ref[0] + second == which)
        def _():
            total = t_dot_in_kernel(left[...], right[...])
            out_ref[...] = total + refs[0][...] if received else total

    write(0, query_ref, slot_ref)
    write(1, key_ref, slot_ref)
    write(2, value_ref, slot_ref)
    write(3, mixture_ref, grad_ref)


def attention_sums(part, lows, mixture, rounded, attended_low, received=None, into=None, place=0):
    slots, heads = mixture.shape
    half = rounded.shape[1] // 2
    left = pl.BlockSpec((slots, heads), lambda i: (0, 0))
    right = pl.BlockSpec((slots, half), lambda i: (0, i // 2))
    rows = pl.BlockSpec((heads, half), lambda i: (i, 0))
    more = [item for item in (received, into) if item is not None]
    shape = (4 * heads, half) if into is None else into.shape
    return pl.pallas_call(
        lambda *refs: attention_sums_kernel(received is not None, *refs),
        grid=(4,),
        in_specs=[SCALAR] + [left] * 4 + [right] * 2 + [rows, pl.BlockSpec(memory_space=pl.ANY)][: len(more)],
        out_specs=pl.BlockSpec((heads, half), lambda i: (i, place)),
        out_shape=jax.ShapeDtypeStruct(shape, F32),
        input_output_aliases={} if into is None else {8: 0},
        compiler_params=LIMIT,
        cost_estimate=pl.CostEstimate(flops=8 * slots * heads * half, bytes_accessed=16 * heads * half, transcendentals=0),
        name="attention_sums",
    )(part.reshape(1), *lows, mixture, rounded, attended_low, *more)


def sort_kernel(piece_ref, down_ref, up_ref):
    chips, _, rows, width = piece_ref.shape
    for i in range(chips):
        down_ref[i * rows : (i + 1) * rows, :] = piece_ref[i, 0].astype(BF16)
        up = piece_ref[i, 1].astype(BF16)
        half = rows // 2
        up_ref[i * half : (i + 1) * half, :width] = up[:half]
        up_ref[i * half : (i + 1) * half, width:] = up[half:]


def sort_weights(gathered):
    chips, _, rows, width = gathered.shape
    step = 4
    units = chips * rows
    return pl.pallas_call(
        sort_kernel,
        grid=(chips // step,),
        in_specs=[pl.BlockSpec((step, 2, rows, width), lambda i: (i, 0, 0, 0))],
        out_specs=[
            pl.BlockSpec((step * rows, width), lambda i: (i, 0)),
            pl.BlockSpec((step * rows // 2, units), lambda i: (i, 0)),
        ],
        out_shape=[
            jax.ShapeDtypeStruct((units, width), BF16),
            jax.ShapeDtypeStruct((width, units), BF16),
        ],
        compiler_params=LIMIT,
        cost_estimate=pl.CostEstimate(flops=0, bytes_accessed=12 * units * width, transcendentals=0),
        name="sort_weights",
    )(gathered)


def rows_of(ref):
    chips, _, rows, columns = ref.shape
    return ref[...].reshape(chips * rows, columns)


def place_feed_kernel(down_in, up_in, down_ref, up_ref):
    down_ref[0] = rows_of(down_in)
    up_ref[0] = rows_of(up_in).T


def place_attention_kernel(query_in, key_in, value_in, output_in, query_ref, key_ref, value_ref, output_ref):
    query_ref[0] = rows_of(query_in).T
    key_ref[0] = rows_of(key_in).T
    value_ref[0] = rows_of(value_in).T
    output_ref[0] = rows_of(output_in)


def place_gradients(gathered, width):
    chips, _, rows, _ = gathered.shape
    step = 4
    units, block = chips * rows, step * rows
    half = width // 2

    def feed_in(core):
        return pl.BlockSpec((step, 1, rows, width), lambda l, i: (i, core, 0, 1 - l))

    def attention_in(core, which):
        return pl.BlockSpec((step, 1, rows, half), lambda l, i: (2 * i + which, core, 0, 5 - l))

    limit = pltpu.CompilerParams(vmem_limit_bytes=40 * 2**20)
    down, up = pl.pallas_call(
        place_feed_kernel,
        grid=(2, chips // step),
        in_specs=[feed_in(0), feed_in(1)],
        out_specs=[
            pl.BlockSpec((1, block, width), lambda l, i: (l, i, 0)),
            pl.BlockSpec((1, width, block), lambda l, i: (l, 0, i)),
        ],
        out_shape=[
            jax.ShapeDtypeStruct((2, units, width), F32),
            jax.ShapeDtypeStruct((2, width, units), F32),
        ],
        compiler_params=limit,
        name="place_feed",
    )(gathered, gathered)
    tall = pl.BlockSpec((1, half, block), lambda l, i: (l, i, 0))
    tall_shape = jax.ShapeDtypeStruct((2, width, block), F32)
    query, key, value, output = pl.pallas_call(
        place_attention_kernel,
        grid=(2, 2),
        in_specs=[attention_in(0, 0), attention_in(0, 1), attention_in(1, 0), attention_in(1, 1)],
        out_specs=[tall, tall, tall, pl.BlockSpec((1, block, half), lambda l, i: (l, 0, i))],
        out_shape=[tall_shape, tall_shape, tall_shape, jax.ShapeDtypeStruct((2, block, width), F32)],
        compiler_params=limit,
        name="place_attention",
    )(gathered, gathered, gathered, gathered)
    return query, key, value, output, up, down


def local(
    tokens,
    cotangent,
    lengths,
    repeats,
    query_weight,
    query_bias,
    key_weight,
    value_weight,
    value_bias,
    output_weight,
    output_bias,
    attn_gain,
    attn_shift,
    up_weight,
    up_bias,
    down_weight,
    down_bias,
    ffn_gain,
    ffn_shift,
):
    length = lengths[0]
    side = lax.axis_index("h")
    core = lax.axis_index("c")
    chip = lax.axis_index("y") * 4 + lax.axis_index("x")
    first_core = core == 0
    slots, width = tokens.shape
    half_slots = slots // 2
    units = up_weight.shape[2]
    columns = query_weight.shape[2]

    rows_down = units // 16
    pieces = weight_pieces(chip, core, down_weight, up_weight)
    pieces1, pieces2 = together(swap(pieces[0], "h"), pieces[1])
    gathered1 = lax.all_gather(pieces1, PLANE + ("c",))
    pieces2 = swap(pieces2, "h")
    peer_up_bias = swap(up_bias.astype(F32), "h")

    def own_slots(values):
        return piece(values, side, half_slots)

    def feed_weights_back(saved, pre_lows, ffn_low, columns, *first):
        actives, hidden_low = saved[3], saved[4]
        received = swap(feed_sums(1 - core, actives, pre_lows, ffn_low, hidden_low, 2 * width), "c")
        if first:
            received, *first = together(received, *first)
        total = feed_sums(core, actives, pre_lows, ffn_low, hidden_low, columns, received)
        return total, *first

    def attention_forward(layer, rounded):
        *attention, share, sent = attend(
            layer,
            length,
            side,
            rounded,
            query_weight,
            query_bias[layer].astype(F32)[None],
            key_weight,
            value_weight,
            value_bias[layer].astype(F32)[None],
            output_weight,
            layer == 1,
        )
        return attention, share, sent

    def attention_back(layer, saved, grad_one_sent, received):
        grad_one = 2.0 * in_order(side, grad_one_sent, received)
        attended_low = grad_one.astype(BF16)
        *lows, share, query_sum, value_sum = attend_back(
            layer, length, saved, attended_low, query_weight, key_weight, value_weight, output_weight
        )
        small = [jnp.concatenate([query_sum[0], value_sum[0]]), column_sum(attended_low)]
        return grad_one, lows, attended_low, share, small

    def feed_back(layer, gradient, saved):
        scaled_two, inverse_two, pres, actives, hidden_low, scaled_one, inverse_one = saved
        grad_two = normalize_back(gradient, ffn_gain[layer], scaled_two, inverse_two)
        ffn_low = grad_two.astype(BF16)
        downs, ups = (down_weight[layer], peer_down[layer]), (up_weight[layer], peer_up[layer])
        pre_lows = [
            (dot_t(ffn_low, down) * gelu_slope(pre)).astype(BF16) for down, pre in zip(downs, pres, strict=True)
        ]
        grad_hidden = grad_two + dot_t(pre_lows[0], ups[0]) + dot_t(pre_lows[1], ups[1])
        grad_one = normalize_back(grad_hidden, attn_gain[layer], scaled_one, inverse_one)
        shared = [
            jnp.sum(grad_hidden * scaled_one, axis=0),
            jnp.sum(grad_hidden, axis=0),
            column_sum(ffn_low),
            jnp.sum(gradient * scaled_two, axis=0),
            jnp.sum(gradient, axis=0),
        ]
        biases = [column_sum(item).reshape(-1, width) for item in pre_lows]
        return grad_one, ffn_low, pre_lows, shared, biases

    def layer_forward(layer, x_own, attended, peers):
        attended = attended + output_bias[layer]
        hidden, scaled, inverse = normalize(x_own + attended, attn_gain[layer], attn_shift[layer])
        hidden_low = hidden.astype(BF16)
        pre = dot(hidden_low, up_weight[layer]) + up_bias[layer]
        active = gelu(pre).astype(BF16)
        ffn_out = dot(active, down_weight[layer])
        peer_down, peer_up = peers
        pre_peer = dot(hidden_low, peer_up) + peer_up_bias[layer]
        active_peer = gelu(pre_peer).astype(BF16)
        ffn_out = ffn_out + dot(active_peer, peer_down) + down_bias[layer]
        out, scaled_two, inverse_two = normalize(hidden + ffn_out, ffn_gain[layer], ffn_shift[layer])
        saved = (scaled_two, inverse_two, (pre, pre_peer), (active, active_peer), hidden_low, scaled, inverse)
        return out, saved

    att1, share, sent = attention_forward(0, tokens)
    pieces2, sent = together(pieces2, sent)
    peers1 = sort_weights(gathered1.reshape(16, 2, rows_down, width))
    gathered2 = lax.all_gather(pieces2, PLANE + ("c",))
    received, peer_output = together(swap(sent, "h"), 0.5 * output_weight[1].astype(F32))
    peer_output = swap(peer_output, "h")
    x2_own, saved1 = layer_forward(0, own_slots(tokens).astype(F32), share + received, peers1)
    sent, peer_output = together(0.5 * x2_own, peer_output)
    peer_output = (2.0 * peer_output).astype(BF16)
    x2_low = (2.0 * in_order(side, sent, swap(sent, "h"))).astype(BF16)
    att2, share, sent = attention_forward(1, x2_low)
    received, *peers2 = together(swap(sent, "h"), *sort_weights(gathered2.reshape(16, 2, rows_down, width)))
    attended = share + dot((2.0 * received).astype(BF16), peer_output)
    _, saved2 = layer_forward(1, x2_own, attended, peers2)
    scaled_last = saved2[0]
    mixture = att2[3]
    peer_down, peer_up = (peers1[0], peers2[0]), (peers1[1], peers2[1])

    places = side * half_slots + jnp.arange(half_slots)
    weighting = jnp.where(places < length, repeats[0], 0).astype(F32)[:, None]
    gradient2 = own_slots(cotangent).astype(F32) * weighting
    grad_one_own, ffn_low, pre_lows, shared2, biases2 = feed_back(1, gradient2, saved2)
    sent = 0.5 * grad_one_own
    cut = half_slots * 5 // 8
    received, late = swap(sent[:cut], "h"), swap(sent[cut:], "h")
    feed2, received = feed_weights_back(saved2, pre_lows, ffn_low, 2 * width, received)
    received = jnp.concatenate([received, late])
    feed2 = lax.psum_scatter(feed2, PLANE, tiled=True)
    _, lows2, attended_low2, share, small_att2 = attention_back(1, att2, sent, received)
    received = swap(piece(share, 1 - side, half_slots), "h")
    attn2_received = swap(attention_sums(1 - core, lows2, mixture, x2_low, attended_low2), "c")
    gradient1 = grad_one_own + own_slots(share) + received

    grad_one_own1, ffn_low, pre_lows, shared1, biases1 = feed_back(0, gradient1, saved1)
    sent = 0.5 * grad_one_own1
    received = swap(sent, "h")
    (rest,) = feed_weights_back(saved1, pre_lows, ffn_low, 2 * width + columns)
    rest = attention_sums(core, lows2, mixture, x2_low, attended_low2, attn2_received, rest, 2 * width // columns)
    rest, received, feed2 = together(rest, received, feed2)
    rest = lax.psum_scatter(rest, PLANE, tiled=True)
    grad_one1, lows1, attended_low1, share, small_att1 = attention_back(0, att1, sent, received)
    attn1_received = swap(attention_sums(1 - core, lows1, att1[3], tokens, attended_low1), "c")
    attn1 = plane_sum(attention_sums(core, lows1, att1[3], tokens, attended_low1, attn1_received))

    def across(own, peer):
        diagonal = lax.ppermute(peer, ("zl", "h"), ((0, 3), (3, 0), (1, 2), (2, 1)))
        own = own + swap(own, "zl")
        peer = swap(peer, "h") + diagonal
        return jnp.concatenate([own[:, :width] + peer, own[:, width:]], axis=1)

    feed2 = across(feed2[:, :width], feed2[:, width:])
    attn1 = attn1 + swap(attn1, "zl")
    feed2, attn1, rest = together(feed2, attn1, rest)
    rest = across(jnp.concatenate([rest[:, :width], rest[:, 2 * width :]], axis=1), rest[:, width : 2 * width])
    own = jnp.concatenate([feed2, rest, attn1], axis=1)
    gathered = lax.all_gather(own, PLANE + ("c",)).reshape(16, 2, *own.shape)
    grad_query, grad_key, grad_value, grad_output, grad_up, grad_down = place_gradients(gathered, width)

    token_grad = grad_one1 + pair_sum(share)
    scaled_last, token_grad = together(scaled_last, token_grad)
    scaled_all = in_order(side, scaled_last, swap(scaled_last, "h"))
    block_output = (scaled_all * ffn_gain[1] + ffn_shift[1]).astype(BF16)
    shared = jnp.stack(shared1 + shared2)
    mine = jnp.concatenate([shared, biases1[0], biases2[0]])
    mine = mine + swap(jnp.concatenate([shared, biases1[1], biases2[1]]), "h")
    small = jnp.concatenate([mine, jnp.stack(small_att1 + small_att2)])
    small, block_output = together(small, block_output)
    small = small + swap(small, "c")
    for axis, pairs in LINKS:
        small = small + lax.ppermute(small, axis, pairs)
    small = small + swap(small, "zl")
    bias_rows = units // width
    shared = small[:10].reshape(2, 5, width)
    grad_up_bias = small[10 : 10 + 2 * bias_rows].reshape(2, units)
    attention = small[10 + 2 * bias_rows :].reshape(2, 2, width)

    return (
        block_output,
        token_grad,
        grad_query,
        attention[:, 0, :columns],
        grad_key,
        grad_value,
        attention[:, 0, columns:],
        grad_output,
        attention[:, 1],
        shared[:, 0],
        shared[:, 1],
        grad_up,
        grad_up_bias,
        grad_down,
        shared[:, 2],
        shared[:, 3],
        shared[:, 4],
    )


def solution(mesh):
    fine = Mesh(mesh.devices.reshape(4, 2, 4, 2, 2), ("y", "zl", "x", "c", "h"))
    rows = ("y", "zl", "x", "c")
    in_specs = (
        P(rows, None),
        P(rows, None),
        P(rows),
        P(rows),
        P(None, None, "h"),
        P(None, "h"),
        P(None, None, "h"),
        P(None, None, "h"),
        P(None, "h"),
        P(None, "h", None),
        P(),
        P(),
        P(),
        P(None, None, "h"),
        P(None, "h"),
        P(None, "h", None),
        P(),
        P(),
        P(),
    )
    out_specs = (
        P(rows, None),
        P(rows, None),
        P(None, None, "h"),
        P(None, "h"),
        P(None, None, "h"),
        P(None, None, "h"),
        P(None, "h"),
        P(None, "h", None),
        P(),
        P(),
        P(),
        P(None, None, "h"),
        P(None, "h"),
        P(None, "h", None),
        P(),
        P(),
        P(),
    )
    return jax.shard_map(local, mesh=fine, in_specs=in_specs, out_specs=out_specs, check_vma=False)
```
